128 devices in a mesh: node: 8 (over z, core), local: 16 (over x, y).
Axes of the slice: x: 4, y: 4, z: 4, core: 2. Of those that a mesh axis runs over, the one named last changes fastest.
Arguments:
- tokens: bfloat16 [1024, 7168], P(('node', 'local')), may hold values from -6 to 6
- routes: int32 [1024, 8], P(('node', 'local')), may hold values from 0 to 15, all different within a row; in each aligned block of 8 rows (0 to 7, 8 to 15, ...) at most 5 rows name the same one
- gate_scores: float32 [1024, 8], P(('node', 'local')), may hold values from 0.05 to 1
- gate_weight: bfloat16 [16, 7168, 2048], P('local', None, 'node'), may hold values from -0.0625 to 0.0625
- up_weight: bfloat16 [16, 7168, 2048], P('local', None, 'node'), may hold values from -0.0625 to 0.0625
- down_weight: bfloat16 [16, 2048, 7168], P('local', 'node'), may hold values from -0.125 to 0.125
- query_nope: bfloat16 [1024, 16384], P('node', 'local'), may hold values from -6 to 6
- query_rope: bfloat16 [1024, 8192], P('node', 'local'), may hold values from -8 to 8
- key_up: bfloat16 [128, 128, 512], P('local'), may hold values from -0.5 to 0.5
- value_up: bfloat16 [128, 512, 128], P('local'), may hold values from -2 to 2
- latent_cache: bfloat16 [16, 4096, 512], P('node'), may hold values from -6 to 6
- rope_cache: bfloat16 [16, 4096, 64], P('node'), may hold values from -8 to 8
- new_latent: bfloat16 [1024, 512], P('node'), may hold values from -6 to 6
- new_rope: bfloat16 [1024, 64], P('node'), may hold values from -6 to 6
- lengths: int32 [16], P('node'), may hold values from 1024 to 4096, as said below
Outputs:
- routed_out: bfloat16 [1024, 7168], P(('node', 'local'))
- attention_out: bfloat16 [1024, 16384], P('node', 'local')
The draws below stay inside these ranges and needn't reach their ends.
Inputs may be any that keep to these rules, and one draw needn't show every extreme that they name: `routes`: in each aligned block of 8 rows (the rows of one device) no expert is named by more than 5 rows, a bound that some block reaches. `lengths`: one sequence has all 4096 slots live.
All inputs are finite; a program needn't handle non-finite values.
Results may differ from the reference program's by a relative error of at most 0.019.
Values may be sent and summed in bfloat16 or wider, within the bound.
No kernel may reach another device: no remote copies, remote signals or barrier semaphores. Data moves between devices by JAX's collectives and lax.ppermute only.
A program may use at most 128 MiB of HBM per device.

```python
import math
import jax
import jax.numpy as jnp
import numpy as np
from jax import lax

D = 7168
FF = 2048
HEADS = 128
NOPE = 128
ROPE = 64
LATENT = 512
VHEAD = 128
TOK_DEV = 8
NEW = 64
CACHE = 4096
EXPERTS = 16
TOPK = 8
CAP = 5
TOKENS = 1024
SEQS = 16
N_NODE = 8
N_LOCAL = 16


def draw_query_rope(key, part):
    key = jax.random.fold_in(key, 11)
    key_base = jax.random.fold_in(key, 0)
    base = jnp.clip(jax.random.normal(key_base, (SEQS * NEW, HEADS * ROPE), jnp.float32), -6.0, 6.0)
    return base.astype(jnp.bfloat16)


def draw_rope_cache(key, part):
    key = jax.random.fold_in(key, 12)
    base = jnp.clip(jax.random.normal(key, (SEQS, CACHE, ROPE), jnp.float32), -6.0, 6.0)
    return base.astype(jnp.bfloat16)


def draw_lengths(key, part):
    key = jax.random.fold_in(key, 13)
    key_length, key_pick = jax.random.split(key)
    drawn = jax.random.randint(key_length, (SEQS,), CACHE // 4, CACHE + 1)
    longest = jax.random.randint(key_pick, (), 0, SEQS)
    return jnp.where(jnp.arange(SEQS, dtype=jnp.int32) == longest, CACHE, drawn).astype(jnp.int32)


def shard_levels(stream_key, extent, shards, least, high):
    level, own = 1.0, jax.random.fold_in(stream_key, 6)
    for position, shards_of in shards:
        draws = jnp.exp(jax.random.uniform(jax.random.fold_in(own, position), (shards_of,), jnp.float32, least / len(shards), high / len(shards)))
        level = level * jnp.repeat(draws, extent[position] // shards_of).reshape([-1 if axis == position else 1 for axis in range(len(extent))])
    return level


def deal_out(key, own, number, rows, count, top, reach, skew):
    sequence = jax.random.permutation(key, count)
    crowded, ordinary = shares(count, rows * top, reach, skew, True), shares(count, rows * top, reach, skew, False)
    places = jnp.arange(count)

    def named(sizes, rotation):
        used = int((sizes > 0).sum())
        fixed = max(1, used // 4)
        passed = fixed + (places - fixed + rotation * (used - fixed)) % max(1, count - fixed)
        return jnp.zeros((count,), jnp.int32).at[sequence[jnp.where(places < fixed, places, passed)]].set(jnp.asarray(sizes, jnp.int32))

    sizes = jnp.where(number % 4 == 0, named(crowded, number // 4), named(ordinary, number - number // 4 - 1))
    mixed = jax.random.permutation(jax.random.fold_in(own, 3), count)
    giver, taker = mixed[0:count // 2 * 2:2], mixed[1:count // 2 * 2:2]
    margin = jnp.minimum(sizes[giver] - 1, reach - sizes[taker]) // 2
    margin = jnp.where((giver == sequence[0]) | (taker == sequence[0]) | (sizes[taker] == 0), 0, jnp.maximum(margin, 0))
    passed = jax.random.randint(jax.random.fold_in(own, 4), (count // 2,), 0, 1 << 20) % (margin + 1)
    sizes = sizes.at[giver].add(-passed).at[taker].add(passed)
    members = jnp.searchsorted(jnp.cumsum(sizes), jnp.arange(rows * top), side="right").astype(jnp.int32)
    grid = members.reshape(top, rows).T
    grid = grid[jax.random.permutation(jax.random.fold_in(own, 1), rows)]
    rotation = jax.random.randint(jax.random.fold_in(own, 2), (rows, 1), 0, top)
    return jnp.take_along_axis(grid, (jnp.arange(top)[None, :] + rotation) % top, axis=1)


def shares(count, total, bound, lean, full):
    weights = [(1 << 20) // math.isqrt(grade ** lean) + 1 for grade in range(1, count + 1)]
    largest = bound if full else min(bound, max(-(-total // count), total * weights[0] // sum(weights)))
    least = 1 if total - largest >= count - 1 else 0
    counts, surplus = [largest] + [least] * (count - 1), total - largest - least * (count - 1)
    while surplus > 0:
        free = [i for i in range(1, count) if counts[i] < largest] or [i for i in range(1, count) if counts[i] < bound]
        whole, remaining = sum([weights[i] for i in free]), surplus
        for i in free:
            addition = min(bound - counts[i], max(1, remaining * weights[i] // whole), surplus)
            counts[i] = counts[i] + addition
            surplus = surplus - addition
    return np.array(counts)


def bell_draw(rng, shape, deviation, limit, cuts=(), kind=jnp.bfloat16):
    values = deviation * jax.random.normal(rng, shape, jnp.float32)
    if cuts:
        values = values * shard_levels(rng, shape, cuts, -0.22, 0.18)
    return jnp.clip(values, -limit, limit).astype(kind)


def setup_inputs(seed: int = 0) -> dict:
    arg_keys = jax.random.split(jax.random.key(seed), 16)
    tokens = bell_draw(arg_keys[0], (TOKENS, D), 1.0, 6.0, ((0, 128),))
    routes_keys = jax.random.split(jax.random.fold_in(arg_keys[1], 1), TOKENS // TOK_DEV)
    routes_turns = jax.random.permutation(jax.random.fold_in(arg_keys[1], 3), TOKENS // TOK_DEV)
    routes = jax.vmap(lambda own, number: deal_out(jax.random.fold_in(arg_keys[1], 2), own, number, TOK_DEV, EXPERTS, TOPK, CAP, 2))(routes_keys, routes_turns).reshape((TOKENS, TOPK))
    gate_scores = jnp.clip(jnp.exp(math.log(1.0) - 2.9957323 * jax.random.uniform(arg_keys[2], (TOKENS, TOPK), jnp.float32) ** shard_levels(arg_keys[2], (TOKENS, TOPK), ((0, 128),), -0.2, 0.2)), 0.05, 1.0)
    gate_weight = bell_draw(arg_keys[3], (EXPERTS, D, FF), D ** -0.5, 0.0625, ((0, 16), (2, 8)))
    up_weight = bell_draw(arg_keys[4], (EXPERTS, D, FF), D ** -0.5, 0.0625, ((0, 16), (2, 8)))
    down_weight = bell_draw(arg_keys[5], (EXPERTS, FF, D), FF ** -0.5, 0.125, ((0, 16), (1, 8)))
    query_nope = bell_draw(arg_keys[6], (SEQS * NEW, HEADS * NOPE), 1.0, 6.0, ((0, 8), (1, 16)))
    query_rope = draw_query_rope(jax.random.fold_in(arg_keys[15], 71), 0)
    key_up = bell_draw(arg_keys[8], (HEADS, NOPE, LATENT), NOPE ** -0.5, 0.5, ((0, 16),))
    value_up = bell_draw(arg_keys[9], (HEADS, LATENT, VHEAD), (max(1, LATENT // 64)) ** -0.5, 2.0, ((0, 16),))
    latent_cache = bell_draw(arg_keys[10], (SEQS, CACHE, LATENT), 1.0, 6.0, ((0, 8),))
    rope_cache = draw_rope_cache(jax.random.fold_in(arg_keys[15], 71), 0)
    new_latent = bell_draw(arg_keys[12], (SEQS * NEW, LATENT), 1.0, 6.0, ((0, 8),))
    new_rope = bell_draw(arg_keys[13], (SEQS * NEW, ROPE), 1.0, 6.0, ((0, 8),))
    lengths = draw_lengths(jax.random.fold_in(arg_keys[15], 71), 0)
    return dict(tokens=tokens, routes=routes, gate_scores=gate_scores, gate_weight=gate_weight, up_weight=up_weight, down_weight=down_weight, query_nope=query_nope, query_rope=query_rope, key_up=key_up, value_up=value_up, latent_cache=latent_cache, rope_cache=rope_cache, new_latent=new_latent, new_rope=new_rope, lengths=lengths)


ROUTE_SCALE = 2.5
NEG_BIG = -1.0e30


def expert_output(rows_in, gate_matrix, up_matrix, down_matrix):
    gate_values = jnp.dot(rows_in, gate_matrix, preferred_element_type=jnp.float32)
    up_values = jnp.dot(rows_in, up_matrix, preferred_element_type=jnp.float32)
    activated = (jax.nn.silu(gate_values) * up_values).astype(jnp.bfloat16)
    slice_width = FF // N_NODE
    pieces = jnp.einsum("rsw,swd->rsd", activated.reshape(-1, N_NODE, slice_width).astype(jnp.float32), down_matrix.reshape(N_NODE, slice_width, D).astype(jnp.float32))
    pieces = lax.optimization_barrier(pieces.astype(jnp.bfloat16))
    return jnp.sum(pieces.astype(jnp.float32), axis=1)


def routed_reference(tokens, routes, gate_scores, gate_weight, up_weight, down_weight):
    weights = gate_scores / jnp.sum(gate_scores, axis=1, keepdims=True) * ROUTE_SCALE
    busiest = N_NODE * N_LOCAL * CAP

    def per_expert(total, packed):
        expert_id, gate_matrix, up_matrix, down_matrix = packed
        matches = routes == expert_id
        coefficient = jnp.sum(jnp.where(matches, weights, jnp.zeros_like(weights)), axis=1)
        chosen = jnp.any(matches, axis=1)
        row_order = jnp.argsort(jnp.where(chosen, 0, 1).astype(jnp.int32), stable=True)[:busiest]
        result = expert_output(tokens[row_order], gate_matrix, up_matrix, down_matrix)
        return total.at[row_order].add(coefficient[row_order][:, None] * result), None

    total = jnp.zeros((TOKENS, D), jnp.float32)
    total, ignored = lax.scan(per_expert, total, (jnp.arange(EXPERTS, dtype=jnp.int32), gate_weight, up_weight, down_weight))
    return total.astype(jnp.bfloat16)


def attention_reference(query_nope, query_rope, key_up, value_up, latent_cache, rope_cache, new_latent, new_rope, lengths):
    score_scale = (NOPE + ROPE) ** -0.5
    key_float = key_up.astype(jnp.float32)
    value_float = value_up.astype(jnp.float32)

    def attend(packed):
        nope_block, rope_block, latent_rows, rope_rows, fresh_latent, fresh_rope, length_value = packed
        query = nope_block.reshape(NEW, HEADS, NOPE).astype(jnp.float32)
        absorbed = jnp.einsum("thn,hnl->thl", query, key_float).astype(jnp.bfloat16).astype(jnp.float32)
        rotated = rope_block.reshape(NEW, HEADS, ROPE).astype(jnp.float32)
        cache_scores = (jnp.einsum("thl,jl->thj", absorbed, latent_rows.astype(jnp.float32)) + jnp.einsum("thr,jr->thj", rotated, rope_rows.astype(jnp.float32))) * score_scale
        fresh_scores = (jnp.einsum("thl,il->thi", absorbed, fresh_latent.astype(jnp.float32)) + jnp.einsum("thr,ir->thi", rotated, fresh_rope.astype(jnp.float32))) * score_scale
        visible = jnp.arange(CACHE, dtype=jnp.int32) < length_value
        causal = jnp.arange(NEW, dtype=jnp.int32)[None, :] <= jnp.arange(NEW, dtype=jnp.int32)[:, None]
        cache_scores = jnp.where(visible[None, None, :], cache_scores, NEG_BIG)
        fresh_scores = jnp.where(causal[:, None, :], fresh_scores, NEG_BIG)
        row_max = jnp.maximum(jnp.max(cache_scores, axis=2), jnp.max(fresh_scores, axis=2))[:, :, None]
        cache_exp = jnp.exp(cache_scores - row_max)
        fresh_exp = jnp.exp(fresh_scores - row_max)
        denominator = jnp.sum(cache_exp, axis=2, keepdims=True) + jnp.sum(fresh_exp, axis=2, keepdims=True)
        cache_probs = (cache_exp / denominator).astype(jnp.bfloat16).astype(jnp.float32)
        fresh_probs = (fresh_exp / denominator).astype(jnp.bfloat16).astype(jnp.float32)
        latent_out = jnp.einsum("thj,jl->thl", cache_probs, latent_rows.astype(jnp.float32)) + jnp.einsum("thi,il->thl", fresh_probs, fresh_latent.astype(jnp.float32))
        latent_out = latent_out.astype(jnp.bfloat16).astype(jnp.float32)
        values = jnp.einsum("thl,hlv->thv", latent_out, value_float).astype(jnp.bfloat16)
        return values.reshape(NEW, HEADS * VHEAD)

    stacked = lax.map(attend, (query_nope.reshape(SEQS, NEW, HEADS * NOPE), query_rope.reshape(SEQS, NEW, HEADS * ROPE), latent_cache, rope_cache, new_latent.reshape(SEQS, NEW, LATENT), new_rope.reshape(SEQS, NEW, ROPE), lengths))
    return stacked.reshape(SEQS * NEW, HEADS * VHEAD)


def reference(tokens, routes, gate_scores, gate_weight, up_weight, down_weight, query_nope, query_rope, key_up, value_up, latent_cache, rope_cache, new_latent, new_rope, lengths):
    routed_out = routed_reference(tokens, routes, gate_scores, gate_weight, up_weight, down_weight)
    attention_out = attention_reference(query_nope, query_rope, key_up, value_up, latent_cache, rope_cache, new_latent, new_rope, lengths)
    return (routed_out, attention_out)
```

```python
import jax
import jax.numpy as jnp
from jax import lax
from jax.sharding import Mesh, PartitionSpec as P

NOPE = 128
ROPE = 64
NEW = 64
CACHE = 4096
EXPERTS = 16


ROUTE_SCALE = 2.5
NEG_BIG = -1e30


Z, X, Y = 0, 1, 2
AXES = ("z", "x", "y")
RING = 4
SCHEDULES = ((X, Y, Z, 0, 2432), (Y, Z, X, 2432, 4864), (Z, X, Y, 4864, 7168))


def shift(value, axis, distance):
    pairs = [(place, (place + distance) % RING) for place in range(RING)]
    return lax.ppermute(value, AXES[axis], pairs)


def widened(value):
    return value.astype(jnp.float32)


def ring_reduce(block_of, axis):
    far = block_of(2).astype(jnp.bfloat16)
    half = far.shape[0] // 2
    from_left = shift(far[:half], axis, 1)
    from_right = shift(far[half:], axis, -1)
    up, down = block_of(1), block_of(3)
    up = jnp.concatenate([up[:half] + widened(from_left), up[half:]], axis=0).astype(jnp.bfloat16)
    down = jnp.concatenate([down[:half], down[half:] + widened(from_right)], axis=0).astype(jnp.bfloat16)
    from_left, from_right = shift(up, axis, 1), shift(down, axis, -1)
    return block_of(0) + widened(from_left) + widened(from_right)


def direct_reduce(block_of, axis):
    arrived = [shift(block_of(d).astype(jnp.bfloat16), axis, d) for d in (1, 2, 3)]
    return block_of(0) + widened(arrived[0]) + widened(arrived[1]) + widened(arrived[2])


def scattered_sum(hidden, down_part):
    rows, units = hidden.shape[3], hidden.shape[4]
    outputs = []
    for first, second, third, low, high in SCHEDULES:
        ordered = jnp.transpose(hidden, (first, second, third, 3, 4)).reshape(RING, RING * RING * rows, units)
        columns = down_part[:, low:high]

        def term(distance):
            return jnp.dot(ordered[distance], columns, preferred_element_type=jnp.float32)

        total = ring_reduce(term, first).astype(jnp.bfloat16).reshape(RING, RING * rows, high - low)
        total = ring_reduce(lambda d: widened(total[d]), second).astype(jnp.bfloat16)
        total = total.reshape(RING, rows, high - low)
        outputs.append(direct_reduce(lambda d: widened(total[d]), third).astype(jnp.bfloat16))
    return jnp.concatenate(outputs, axis=1)


def with_other_core(value):
    return lax.ppermute(value, "core", [(0, 1), (1, 0)])


def routed_layer(tokens, routes, gate_scores, gate_weight, up_weight, down_weight, beside):
    width = tokens.shape[1]
    rows = tokens.shape[0]
    expert_count = EXPERTS
    expert = lax.axis_index("x") * RING + lax.axis_index("y")
    weights = gate_scores / jnp.sum(gate_scores, axis=1, keepdims=True) * ROUTE_SCALE
    expert_ids = jnp.arange(expert_count, dtype=jnp.int32)
    dense = jnp.sum(jnp.where(routes[:, :, None] == expert_ids, weights[:, :, None], 0.0), axis=1)
    high = dense.astype(jnp.bfloat16)
    low = (dense - high.astype(jnp.float32)).astype(jnp.bfloat16)
    pad = jnp.zeros((rows, 128 - 2 * expert_count), jnp.bfloat16)
    packed = jnp.concatenate([tokens, high, low, pad], axis=1)
    gathered = lax.all_gather(packed, AXES, axis=0, tiled=True)
    gate_part, up_part, down_part = gate_weight[0], up_weight[0], down_weight[0]
    gate_other, up_other, down_other = (with_other_core(part) for part in (gate_part, up_part, down_part))
    gathered, beside = lax.optimization_barrier((gathered, beside))
    rows_in = gathered[:, :width]
    extra = gathered[:, width:].astype(jnp.float32)
    pick = (jnp.arange(128) % expert_count == expert) & (jnp.arange(128) < 2 * expert_count)
    coefficient = jnp.sum(jnp.where(pick, extra, 0.0), axis=1, keepdims=True)

    def hidden_of(gate_matrix, up_matrix):
        gate_values = jnp.dot(rows_in, gate_matrix, preferred_element_type=jnp.float32)
        up_values = jnp.dot(rows_in, up_matrix, preferred_element_type=jnp.float32)
        hidden = jax.nn.silu(gate_values) * up_values
        return jnp.where(coefficient > 0, hidden * coefficient, 0.0).astype(jnp.bfloat16)

    hidden = jnp.concatenate([hidden_of(gate_part, up_part), hidden_of(gate_other, up_other)], axis=1)
    hidden = hidden.reshape(RING, RING, RING, rows, -1)
    for axis in (Z, X, Y):
        hidden = jnp.roll(hidden, -lax.axis_index(AXES[axis]), axis=axis)
    down_both = jnp.concatenate([down_part, down_other], axis=0)
    return scattered_sum(hidden, down_both), beside


def attention_layer(
    query_nope,
    query_rope,
    key_up,
    value_up,
    latent_cache,
    rope_cache,
    new_latent,
    new_rope,
    lengths,
):
    head_count = key_up.shape[0]
    score_scale = (NOPE + ROPE) ** (-0.5)
    visible_ids = jnp.arange(CACHE, dtype=jnp.int32)
    causal = jnp.arange(NEW, dtype=jnp.int32)[None, :] <= jnp.arange(NEW, dtype=jnp.int32)[:, None]
    outputs = []
    for sequence in range(latent_cache.shape[0]):
        row_span = slice(sequence * NEW, (sequence + 1) * NEW)
        nope_block = query_nope[row_span].reshape(NEW, head_count, NOPE)
        rope_block = query_rope[row_span].reshape(NEW, head_count, ROPE)
        latent_rows = latent_cache[sequence]
        fresh_latent = new_latent[row_span]
        absorbed = jnp.einsum(
            "thn,hnl->thl", nope_block, key_up, preferred_element_type=jnp.float32
        ).astype(jnp.bfloat16)
        cache_scores = (
            jnp.einsum("thl,jl->thj", absorbed, latent_rows, preferred_element_type=jnp.float32)
            + jnp.einsum(
                "thr,jr->thj", rope_block, rope_cache[sequence], preferred_element_type=jnp.float32
            )
        ) * score_scale
        fresh_scores = (
            jnp.einsum("thl,il->thi", absorbed, fresh_latent, preferred_element_type=jnp.float32)
            + jnp.einsum(
                "thr,ir->thi", rope_block, new_rope[row_span], preferred_element_type=jnp.float32
            )
        ) * score_scale
        visible = visible_ids < lengths[sequence]
        cache_scores = jnp.where(visible[None, None, :], cache_scores, NEG_BIG)
        fresh_scores = jnp.where(causal[:, None, :], fresh_scores, NEG_BIG)
        row_max = jnp.maximum(jnp.max(cache_scores, axis=2), jnp.max(fresh_scores, axis=2))[
            :, :, None
        ]
        cache_exp = jnp.exp(cache_scores - row_max)
        fresh_exp = jnp.exp(fresh_scores - row_max)
        denominator = jnp.sum(cache_exp, axis=2, keepdims=True) + jnp.sum(
            fresh_exp, axis=2, keepdims=True
        )
        cache_probs = (cache_exp / denominator).astype(jnp.bfloat16)
        fresh_probs = (fresh_exp / denominator).astype(jnp.bfloat16)
        latent_out = jnp.einsum(
            "thj,jl->thl", cache_probs, latent_rows, preferred_element_type=jnp.float32
        ) + jnp.einsum("thi,il->thl", fresh_probs, fresh_latent, preferred_element_type=jnp.float32)
        latent_out = latent_out.astype(jnp.bfloat16)
        values = jnp.einsum(
            "thl,hlv->thv", latent_out, value_up, preferred_element_type=jnp.float32
        ).astype(jnp.bfloat16)
        outputs.append(values.reshape(NEW, -1))
    return jnp.concatenate(outputs, axis=0)


def body(
    tokens,
    routes,
    gate_scores,
    gate_weight,
    up_weight,
    down_weight,
    query_nope,
    query_rope,
    key_up,
    value_up,
    latent_cache,
    rope_cache,
    new_latent,
    new_rope,
    lengths,
):
    attention_out = attention_layer(
        query_nope,
        query_rope,
        key_up,
        value_up,
        latent_cache,
        rope_cache,
        new_latent,
        new_rope,
        lengths,
    )
    return routed_layer(tokens, routes, gate_scores, gate_weight, up_weight, down_weight, attention_out)


def solution(mesh):
    cube = Mesh(mesh.devices.reshape(4, 2, 4, 4), ("z", "core", "x", "y"))
    node, local = ("z", "core"), ("x", "y")
    every = node + local
    in_specs = (
        P(every, None),
        P(every, None),
        P(every, None),
        P(local, None, node),
        P(local, None, node),
        P(local, node, None),
        P(node, local),
        P(node, local),
        P(local, None, None),
        P(local, None, None),
        P(node, None, None),
        P(node, None, None),
        P(node, None),
        P(node, None),
        P(node),
    )
    out_specs = (P(every, None), P(node, local))
    return jax.shard_map(body, mesh=cube, in_specs=in_specs, out_specs=out_specs, check_vma=False)
```

```python
import jax
import jax.numpy as jnp
import numpy as np
from jax import lax
from jax.sharding import Mesh, PartitionSpec as P

NOPE = 128
ROPE = 64
NEW = 64
CACHE = 4096
EXPERTS = 16


ROUTE_SCALE = 2.5
NEG_BIG = -1e30


AXES = ("z", "core", "x", "y")
SIZES = (4, 2, 4, 4)
RING = 4
ORDERS = ((0, 3, 2), (0, 2, 3))


def shift(value, phase, distance):
    pairs = []
    for place in np.ndindex(*SIZES):
        target = list(place)
        axis = ORDERS[place[1]][phase]
        target[axis] = (target[axis] + distance) % RING
        pairs.append((int(np.ravel_multi_index(place, SIZES)), int(np.ravel_multi_index(target, SIZES))))
    return lax.ppermute(value, AXES, pairs)


def widened(value):
    return value.astype(jnp.float32)


def narrowed(value):
    return value.astype(jnp.bfloat16)


def ring_gather(value, phase):
    half = value.shape[0] // 2
    below, above = shift(value, phase, 1), shift(value, phase, -1)
    far_low, far_high = shift(below[:half], phase, 1), shift(above[half:], phase, -1)
    return value, above, below, far_low, far_high


def direct_gather(value, phase):
    return jnp.concatenate([value] + [shift(value, phase, -d) for d in (1, 3, 2)], axis=0)


def ring_reduce(own, above, below, far_low, far_high, phase):
    half_up = shift(narrowed(far_low(None)), phase, 1)
    half_down = shift(narrowed(far_high(None)), phase, -1)
    from_below = shift(narrowed(above(half_up)), phase, 1)
    from_above = shift(narrowed(below(half_down)), phase, -1)
    return own(from_below, from_above)


def array_terms(total):
    size = total.shape[0] // RING
    half = size // 2
    own, above, below, far = (total[i * size : (i + 1) * size] for i in range(RING))

    def up(arrived):
        return jnp.concatenate([above[:half] + widened(arrived), above[half:]], axis=0)

    def down(arrived):
        return jnp.concatenate([below[:half], below[half:] + widened(arrived)], axis=0)

    return (
        lambda one, two: own + widened(one) + widened(two),
        up,
        down,
        lambda arrived: far[:half],
        lambda arrived: far[half:],
    )


def direct_reduce(total, phase):
    size = total.shape[0] // RING
    own = widened(total[:size])
    for place, distance in ((1, 1), (2, 3), (3, 2)):
        own = own + widened(shift(total[place * size : (place + 1) * size], phase, distance))
    return own


def with_other_core(value):
    return lax.ppermute(value, "core", [(0, 1), (1, 0)])


def routed_layer(tokens, routes, gate_scores, gate_weight, up_weight, down_weight):
    width = tokens.shape[1]
    rows = tokens.shape[0]
    expert_count = EXPERTS
    expert = lax.axis_index("x") * RING + lax.axis_index("y")
    weights = gate_scores / jnp.sum(gate_scores, axis=1, keepdims=True) * ROUTE_SCALE
    expert_ids = jnp.arange(expert_count, dtype=jnp.int32)
    dense = jnp.sum(jnp.where(routes[:, :, None] == expert_ids, weights[:, :, None], 0.0), axis=1)
    high = dense.astype(jnp.bfloat16)
    low = (dense - high.astype(jnp.float32)).astype(jnp.bfloat16)
    pad = jnp.zeros((rows, 128 - 2 * expert_count), jnp.bfloat16)
    packed = jnp.concatenate([tokens, high, low, pad], axis=1)
    gate_part, up_part, down_part = gate_weight[0], up_weight[0], down_weight[0]
    gate_other, up_other, down_other = (with_other_core(part) for part in (gate_part, up_part, down_part))
    down_both = jnp.concatenate([down_part, down_other], axis=0)
    pick = (jnp.arange(128) % expert_count == expert) & (jnp.arange(128) < 2 * expert_count)

    def hidden_of(piece):
        rows_in = piece[:, :width]
        extra = piece[:, width:].astype(jnp.float32)
        coefficient = jnp.sum(jnp.where(pick, extra, 0.0), axis=1, keepdims=True)
        units = []
        for gate_matrix, up_matrix in ((gate_part, up_part), (gate_other, up_other)):
            gate_values = jnp.dot(rows_in, gate_matrix, preferred_element_type=jnp.float32)
            up_values = jnp.dot(rows_in, up_matrix, preferred_element_type=jnp.float32)
            hidden = jax.nn.silu(gate_values) * up_values
            units.append(jnp.where(coefficient > 0, hidden * coefficient, 0.0).astype(jnp.bfloat16))
        return jnp.concatenate(units, axis=1)

    def product(hidden):
        return jnp.dot(hidden, down_both, preferred_element_type=jnp.float32)

    small = direct_gather(packed, 0)
    middle = jnp.concatenate(ring_gather(small, 1), axis=0)
    own, above, below, far_low, far_high = ring_gather(middle, 2)
    hidden_own = hidden_of(own)
    hidden_near = hidden_of(jnp.concatenate([above, below], axis=0))
    hidden_far = hidden_of(jnp.concatenate([far_low, far_high], axis=0))
    size = middle.shape[0]
    half = size // 2

    def above_term(arrived):
        value = product(hidden_near[:size])
        return jnp.concatenate([value[:half] + widened(arrived), value[half:]], axis=0)

    def below_term(arrived):
        value = product(hidden_near[size:])
        return jnp.concatenate([value[:half], value[half:] + widened(arrived)], axis=0)

    total = ring_reduce(
        lambda one, two: product(hidden_own) + widened(one) + widened(two),
        above_term,
        below_term,
        lambda arrived: product(hidden_far[:half]),
        lambda arrived: product(hidden_far[half:]),
        2,
    )
    total = ring_reduce(*array_terms(total), 1)
    return narrowed(direct_reduce(narrowed(total), 0))


def attention_layer(
    query_nope,
    query_rope,
    key_up,
    value_up,
    latent_cache,
    rope_cache,
    new_latent,
    new_rope,
    lengths,
):
    head_count = key_up.shape[0]
    score_scale = (NOPE + ROPE) ** (-0.5)
    visible_ids = jnp.arange(CACHE, dtype=jnp.int32)
    causal = jnp.arange(NEW, dtype=jnp.int32)[None, :] <= jnp.arange(NEW, dtype=jnp.int32)[:, None]
    outputs = []
    for sequence in range(latent_cache.shape[0]):
        row_span = slice(sequence * NEW, (sequence + 1) * NEW)
        nope_block = query_nope[row_span].reshape(NEW, head_count, NOPE)
        rope_block = query_rope[row_span].reshape(NEW, head_count, ROPE)
        latent_rows = latent_cache[sequence]
        fresh_latent = new_latent[row_span]
        absorbed = jnp.einsum(
            "thn,hnl->thl", nope_block, key_up, preferred_element_type=jnp.float32
        ).astype(jnp.bfloat16)
        cache_scores = (
            jnp.einsum("thl,jl->thj", absorbed, latent_rows, preferred_element_type=jnp.float32)
            + jnp.einsum(
                "thr,jr->thj", rope_block, rope_cache[sequence], preferred_element_type=jnp.float32
            )
        ) * score_scale
        fresh_scores = (
            jnp.einsum("thl,il->thi", absorbed, fresh_latent, preferred_element_type=jnp.float32)
            + jnp.einsum(
                "thr,ir->thi", rope_block, new_rope[row_span], preferred_element_type=jnp.float32
            )
        ) * score_scale
        visible = visible_ids < lengths[sequence]
        cache_scores = jnp.where(visible[None, None, :], cache_scores, NEG_BIG)
        fresh_scores = jnp.where(causal[:, None, :], fresh_scores, NEG_BIG)
        row_max = jnp.maximum(jnp.max(cache_scores, axis=2), jnp.max(fresh_scores, axis=2))[
            :, :, None
        ]
        cache_exp = jnp.exp(cache_scores - row_max)
        fresh_exp = jnp.exp(fresh_scores - row_max)
        denominator = jnp.sum(cache_exp, axis=2, keepdims=True) + jnp.sum(
            fresh_exp, axis=2, keepdims=True
        )
        cache_probs = (cache_exp / denominator).astype(jnp.bfloat16)
        fresh_probs = (fresh_exp / denominator).astype(jnp.bfloat16)
        latent_out = jnp.einsum(
            "thj,jl->thl", cache_probs, latent_rows, preferred_element_type=jnp.float32
        ) + jnp.einsum("thi,il->thl", fresh_probs, fresh_latent, preferred_element_type=jnp.float32)
        latent_out = latent_out.astype(jnp.bfloat16)
        values = jnp.einsum(
            "thl,hlv->thv", latent_out, value_up, preferred_element_type=jnp.float32
        ).astype(jnp.bfloat16)
        outputs.append(values.reshape(NEW, -1))
    return jnp.concatenate(outputs, axis=0)


def body(
    tokens,
    routes,
    gate_scores,
    gate_weight,
    up_weight,
    down_weight,
    query_nope,
    query_rope,
    key_up,
    value_up,
    latent_cache,
    rope_cache,
    new_latent,
    new_rope,
    lengths,
):
    routed_out = routed_layer(tokens, routes, gate_scores, gate_weight, up_weight, down_weight)
    attention_out = attention_layer(
        query_nope,
        query_rope,
        key_up,
        value_up,
        latent_cache,
        rope_cache,
        new_latent,
        new_rope,
        lengths,
    )
    return (routed_out, attention_out)


def solution(mesh):
    cube = Mesh(mesh.devices.reshape(4, 2, 4, 4), ("z", "core", "x", "y"))
    node, local = ("z", "core"), ("x", "y")
    every = node + local
    in_specs = (
        P(every, None),
        P(every, None),
        P(every, None),
        P(local, None, node),
        P(local, None, node),
        P(local, node, None),
        P(node, local),
        P(node, local),
        P(local, None, None),
        P(local, None, None),
        P(node, None, None),
        P(node, None, None),
        P(node, None),
        P(node, None),
        P(node),
    )
    out_specs = (P(every, None), P(node, local))
    return jax.shard_map(body, mesh=cube, in_specs=in_specs, out_specs=out_specs, check_vma=False)
```

```python
import functools

import jax
import jax.numpy as jnp
import numpy as np
from jax import lax
from jax.experimental import pallas as pl
from jax.experimental.pallas import tpu as pltpu
from jax.sharding import Mesh, PartitionSpec as P

NOPE = 128
ROPE = 64
NEW = 64
CACHE = 4096
EXPERTS = 16
ROUTE_SCALE = 2.5
NEG_BIG = -1e30
AXES = ("z", "core", "x", "y")
SIZES = (4, 2, 4, 4)
RING = 4
ORDERS = ((0, 3, 2), (2, 0, 3))
KERNEL_VMEM = 60 * 1024 * 1024
PACK = 128
DEPTH = 1024
UNITS = 256
HALF = 64
KEY_BLOCK = 1024
HEAD_COUNT = 8
LATENT = 512
LOG2E = 1.4426950408889634


def shift(value, phase, distance):
    pairs = []
    for place in np.ndindex(*SIZES):
        target = list(place)
        axis = ORDERS[place[1]][phase]
        target[axis] = (target[axis] + distance) % RING
        pairs.append((int(np.ravel_multi_index(place, SIZES)), int(np.ravel_multi_index(target, SIZES))))
    return lax.ppermute(value, AXES, pairs)


def widened(value):
    return value.astype(jnp.float32)


def narrowed(value):
    return value.astype(jnp.bfloat16)


def added(*values):
    return sum(widened(value) for value in values)


def with_other_core(value):
    return lax.ppermute(value, "core", [(0, 1), (1, 0)])


def expert_kernel(expert_ref, *refs, sources, outputs):
    row_hbm = refs[:sources]
    gate_hbm, up_hbm, gate_other_hbm, up_other_hbm, down_hbm, down_other_hbm = refs[sources : sources + 6]
    out_refs = refs[sources + 6 : sources + 6 + outputs]
    rows_ref, weight_ref, down_ref, sums_ref, hidden_ref, row_sem, weight_sem, down_sem = refs[sources + 6 + outputs :]
    width = weight_ref.shape[0]
    steps = width // DEPTH
    span = rows_ref.shape[0] // sources
    row_copies = [
        pltpu.make_async_copy(source, rows_ref.at[pl.ds(i * span, span)], row_sem.at[i])
        for i, source in enumerate(row_hbm)
    ]
    down_copies = [
        pltpu.make_async_copy(source, down_ref.at[pl.ds(i * UNITS, UNITS)], down_sem.at[i])
        for i, source in enumerate((down_hbm, down_other_hbm))
    ]
    matrices = (gate_hbm, gate_other_hbm, up_hbm, up_other_hbm)

    def weight_copy(matrix, step):
        part = pl.ds(step * DEPTH, DEPTH)
        return pltpu.make_async_copy(
            matrices[matrix].at[part],
            weight_ref.at[part, pl.ds(matrix * UNITS, UNITS)],
            weight_sem.at[matrix, step],
        )

    for copy in row_copies:
        copy.start()
    for step in range(steps):
        for matrix in range(4):
            weight_copy(matrix, step).start()
    for copy in down_copies:
        copy.start()
    for copy in row_copies:
        copy.wait()
    sums_ref[...] = jnp.zeros_like(sums_ref)

    @pl.loop(0, steps)
    def _(step):
        part = pl.ds(pl.multiple_of(step * DEPTH, DEPTH), DEPTH)
        for matrix in range(4):
            weight_copy(matrix, step).wait()
        sums_ref[...] += jnp.dot(rows_ref[:, part], weight_ref[part, :], preferred_element_type=jnp.float32)

    extra = rows_ref[:, width : width + PACK].astype(jnp.float32)
    lane = lax.broadcasted_iota(jnp.int32, extra.shape, 1)
    pick = (lane % EXPERTS == expert_ref[0]) & (lane < 2 * EXPERTS)
    coefficient = jnp.sum(jnp.where(pick, extra, 0.0), axis=1, keepdims=True)
    gate, up = sums_ref[:, : 2 * UNITS], sums_ref[:, 2 * UNITS :]
    hidden = gate / (1.0 + jnp.exp(-gate)) * up * coefficient
    hidden_ref[...] = jnp.where(coefficient > 0, hidden, 0.0).astype(jnp.bfloat16)
    for copy in down_copies:
        copy.wait()

    @pl.loop(0, steps)
    def _(step):
        part = pl.ds(pl.multiple_of(step * DEPTH, DEPTH), DEPTH)
        result = jnp.dot(hidden_ref[...], down_ref[:, part], preferred_element_type=jnp.float32).astype(jnp.bfloat16)
        for i, out_ref in enumerate(out_refs):
            out_ref[:, part] = result[i * HALF : (i + 1) * HALF]


def expert_terms(expert, pieces, weights, downs):
    width = weights[0].shape[0]
    rows = sum(piece.shape[0] for piece in pieces)
    outputs = rows // HALF
    anywhere = pl.BlockSpec(memory_space=pl.ANY)
    return pl.pallas_call(
        functools.partial(expert_kernel, sources=len(pieces), outputs=outputs),
        in_specs=[pl.BlockSpec(memory_space=pltpu.SMEM)] + [anywhere] * (len(pieces) + 6),
        out_specs=[pl.BlockSpec(memory_space=pltpu.VMEM)] * outputs,
        out_shape=[jax.ShapeDtypeStruct((HALF, width), jnp.bfloat16)] * outputs,
        scratch_shapes=[
            pltpu.VMEM((rows, width + PACK), jnp.bfloat16),
            pltpu.VMEM((width, 4 * UNITS), jnp.bfloat16),
            pltpu.VMEM((2 * UNITS, width), jnp.bfloat16),
            pltpu.VMEM((rows, 4 * UNITS), jnp.float32),
            pltpu.VMEM((rows, 2 * UNITS), jnp.bfloat16),
            pltpu.SemaphoreType.DMA((len(pieces),)),
            pltpu.SemaphoreType.DMA((4, width // DEPTH)),
            pltpu.SemaphoreType.DMA((2,)),
        ],
        compiler_params=pltpu.CompilerParams(vmem_limit_bytes=KERNEL_VMEM),
        cost_estimate=pl.CostEstimate(
            flops=6 * rows * width * UNITS * 2, bytes_accessed=12 * width * UNITS + 4 * rows * width, transcendentals=0
        ),
        name="expert",
    )(expert, *pieces, *weights, *downs)


def pack_kernel(tokens_ref, routes_ref, scores_ref, out_ref):
    rows, width = tokens_ref.shape
    out_ref[:, :width] = tokens_ref[...]
    scores = scores_ref[...]
    weights = scores / jnp.sum(scores, axis=1, keepdims=True) * ROUTE_SCALE
    lane = lax.broadcasted_iota(jnp.int32, (rows, PACK), 1)
    dense = jnp.zeros((rows, PACK), jnp.float32)
    for choice in range(scores.shape[1]):
        named = routes_ref[:, choice : choice + 1] == lane % EXPERTS
        dense += jnp.where(named, weights[:, choice : choice + 1], 0.0)
    high = dense.astype(jnp.bfloat16).astype(jnp.float32)
    extra = jnp.where(lane < EXPERTS, high, jnp.where(lane < 2 * EXPERTS, dense - high, 0.0))
    out_ref[:, width:] = extra.astype(jnp.bfloat16)


def packed_rows(tokens, routes, gate_scores):
    rows, width = tokens.shape
    return pl.pallas_call(
        pack_kernel,
        out_shape=jax.ShapeDtypeStruct((rows, width + PACK), jnp.bfloat16),
        name="pack",
    )(tokens, routes, gate_scores)


def attention_kernel(
    sequence, length_ref, nope_ref, rope_ref, key_up_ref, value_up_ref, latent_ref, rope_key_ref,
    new_latent_ref, new_rope_ref, out_ref, query_ref, query_rope_ref, top_ref, sum_ref, total_ref,
):
    step = pl.program_id(0)
    length = length_ref[0]
    scale = (NOPE + ROPE) ** (-0.5) * LOG2E
    contract_last = (((1,), (1,)), ((), ()))

    def absorb(keys, rope_keys, values, bias):
        scores = lax.dot_general(query_ref[...], keys, contract_last, preferred_element_type=jnp.float32)
        scores += jnp.dot(query_rope_ref[...], rope_keys, preferred_element_type=jnp.float32)
        scores = scores * scale + bias
        old_top = top_ref[...]
        top = jnp.maximum(old_top, jnp.max(scores, axis=1, keepdims=True))
        shrink = jnp.exp2(old_top - top)
        probs = jnp.exp2(scores - top)
        top_ref[...] = top
        sum_ref[...] = sum_ref[...] * shrink + jnp.sum(probs, axis=1, keepdims=True)
        total_ref[...] = total_ref[...] * shrink + jnp.dot(
            probs.astype(jnp.bfloat16), values, preferred_element_type=jnp.float32
        )

    @pl.when(step == 0)
    def _():
        for head in range(HEAD_COUNT):
            query_ref[head * NEW : (head + 1) * NEW, :] = jnp.dot(
                nope_ref[:, head * NOPE : (head + 1) * NOPE], key_up_ref[head], preferred_element_type=jnp.float32
            ).astype(jnp.bfloat16)
            query_rope_ref[head * NEW : (head + 1) * NEW, :] = rope_ref[:, head * ROPE : (head + 1) * ROPE]
        top_ref[...] = jnp.full_like(top_ref, NEG_BIG)
        sum_ref[...] = jnp.zeros_like(sum_ref)
        total_ref[...] = jnp.zeros_like(total_ref)
        position = lax.broadcasted_iota(jnp.int32, (HEAD_COUNT * NEW, NEW), 0) % NEW
        fresh = lax.broadcasted_iota(jnp.int32, (HEAD_COUNT * NEW, NEW), 1)
        bias = jnp.where(fresh <= position, 0.0, NEG_BIG)
        absorb(new_latent_ref[...], new_rope_ref[:, sequence * NEW : (sequence + 1) * NEW], new_latent_ref[...], bias)

    @pl.when(step * KEY_BLOCK < length)
    def _():
        slot = step * KEY_BLOCK + lax.broadcasted_iota(jnp.int32, (1, KEY_BLOCK), 1)
        bias = jnp.where(slot < length, 0.0, NEG_BIG)
        absorb(latent_ref[...], rope_key_ref[...], latent_ref[...], bias)

    @pl.when(step == pl.num_programs(0) - 1)
    def _():
        latent_out = (total_ref[...] / sum_ref[...]).astype(jnp.bfloat16)
        for head in range(HEAD_COUNT):
            out_ref[:, head * NOPE : (head + 1) * NOPE] = jnp.dot(
                latent_out[head * NEW : (head + 1) * NEW], value_up_ref[head], preferred_element_type=jnp.float32
            ).astype(jnp.bfloat16)


def attend(sequence, length, nope, rope, key_up, value_up, latent_cache, rope_cache, new_latent, new_rope):
    rows = HEAD_COUNT * NEW

    def whole(*shape):
        return pl.BlockSpec(shape, lambda step, length: (0,) * len(shape))

    def live(step, length):
        return (sequence, jnp.minimum(step, (length[0] + KEY_BLOCK - 1) // KEY_BLOCK - 1), 0)

    def live_last(step, length):
        sequence_place, block, column = live(step, length)
        return (sequence_place, column, block)

    def own(*shape):
        return pl.BlockSpec(shape, lambda step, length: (sequence,) + (0,) * (len(shape) - 1))

    return pl.pallas_call(
        functools.partial(attention_kernel, sequence),
        grid_spec=pltpu.PrefetchScalarGridSpec(
            num_scalar_prefetch=1,
            grid=(CACHE // KEY_BLOCK,),
            in_specs=[
                own(NEW, HEAD_COUNT * NOPE),
                own(NEW, HEAD_COUNT * ROPE),
                whole(HEAD_COUNT, NOPE, LATENT),
                whole(HEAD_COUNT, LATENT, NOPE),
                pl.BlockSpec((None, KEY_BLOCK, LATENT), live),
                pl.BlockSpec((None, ROPE, KEY_BLOCK), live_last),
                own(NEW, LATENT),
                pl.BlockSpec((ROPE, 2 * NEW), lambda step, length: (0, 0)),
            ],
            out_specs=whole(NEW, HEAD_COUNT * NOPE),
            scratch_shapes=[
                pltpu.VMEM((rows, LATENT), jnp.bfloat16),
                pltpu.VMEM((rows, ROPE), jnp.bfloat16),
                pltpu.VMEM((rows, 1), jnp.float32),
                pltpu.VMEM((rows, 1), jnp.float32),
                pltpu.VMEM((rows, LATENT), jnp.float32),
            ],
        ),
        out_shape=jax.ShapeDtypeStruct((NEW, HEAD_COUNT * NOPE), jnp.bfloat16),
        compiler_params=pltpu.CompilerParams(vmem_limit_bytes=KERNEL_VMEM),
        cost_estimate=pl.CostEstimate(flops=6_000_000_000, bytes_accessed=8_000_000, transcendentals=2_100_000),
        name="attend",
    )(length, nope, rope, key_up, value_up, latent_cache, rope_cache, new_latent, new_rope)


def body(
    tokens,
    routes,
    gate_scores,
    gate_weight,
    up_weight,
    down_weight,
    query_nope,
    query_rope,
    key_up,
    value_up,
    latent_cache,
    rope_cache,
    new_latent,
    new_rope,
    lengths,
):
    packed = packed_rows(tokens, routes, gate_scores)
    small = jnp.concatenate([packed] + [shift(packed, 0, -distance) for distance in (1, 2, 3)], axis=0)
    small, gate_weight, up_weight, down_weight = lax.optimization_barrier(
        (small, gate_weight, up_weight, down_weight)
    )
    gate_part, up_part, down_part = gate_weight[0], up_weight[0], down_weight[0]
    weights = (gate_part, up_part, with_other_core(gate_part), with_other_core(up_part))
    downs = (down_part, with_other_core(down_part))
    expert = (lax.axis_index("x") * RING + lax.axis_index("y")).astype(jnp.int32)[None]
    rope_keys, new_rope_keys = jnp.swapaxes(rope_cache, 1, 2), new_rope.T

    def attention(sequence, length):
        return attend(
            sequence, length, query_nope, query_rope, key_up, value_up, latent_cache, rope_keys, new_latent, new_rope_keys
        )

    half = small.shape[0] // 2
    above, below = shift(small, 1, -1), shift(small, 1, 1)
    far_low, far_high = shift(below[:half], 1, 1), shift(above[half:], 1, -1)
    own = jnp.concatenate([small, above, far_low, far_high, below], axis=0)
    above, below = shift(own, 2, -1), shift(own, 2, 1)
    own, lengths = lax.optimization_barrier((own, lengths))
    own_terms = expert_terms(expert, [own], weights, downs)
    first_attention = attention(0, lengths[:1])
    above, below, own_terms, first_attention = lax.optimization_barrier((above, below, own_terms, first_attention))
    far_low, far_high = shift(below[:HALF], 2, 1), shift(above[HALF:], 2, -1)
    above_low, above_high, below_low, below_high = expert_terms(expert, [above, below], weights, downs)
    near_high, near_low = shift(above_high, 2, 1), shift(below_low, 2, -1)
    far_low, far_high, above_high, below_low = lax.optimization_barrier((far_low, far_high, above_high, below_low))
    far_terms = expert_terms(expert, [far_low, far_high], weights, downs)
    far_terms, near_high, near_low = lax.optimization_barrier((far_terms, near_high, near_low))
    from_below, from_above = shift(far_terms[0], 2, 1), shift(far_terms[1], 2, -1)
    far_terms, lengths = lax.optimization_barrier((far_terms, lengths))
    second_attention = attention(1, lengths[1:])
    from_below, from_above, second_attention = lax.optimization_barrier((from_below, from_above, second_attention))
    from_below = shift(narrowed(added(above_low, from_below)), 2, 1)
    from_above = shift(narrowed(added(below_high, from_above)), 2, -1)
    low = added(own_terms[0], near_low, from_below)
    high = added(own_terms[1], near_high, from_above)

    size = HALF // 2
    half = size // 2
    above, far, below = low[size:], high[:size], high[size:]
    up_first = narrowed(jnp.concatenate([far[:half], above[half:]], axis=0))
    down_first = narrowed(jnp.concatenate([far[half:], below[:half]], axis=0))
    from_below, from_above = shift(up_first, 1, 1), shift(down_first, 1, -1)
    up_second = shift(narrowed(added(above[:half], from_below[:half])), 1, 1)
    down_second = shift(narrowed(added(below[half:], from_above[:half])), 1, -1)
    total = low[:size] + jnp.concatenate(
        [added(up_second, from_above[half:]), added(down_second, from_below[half:])], axis=0
    )

    total = narrowed(total)
    rows = tokens.shape[0]
    arrived = [shift(total[distance * rows : (distance + 1) * rows], 0, distance) for distance in (1, 2, 3)]
    routed_out = narrowed(added(total[:rows], *arrived))
    return (routed_out, jnp.concatenate([first_attention, second_attention], axis=0))


def solution(mesh):
    cube = Mesh(mesh.devices.reshape(4, 2, 4, 4), ("z", "core", "x", "y"))
    node, local = ("z", "core"), ("x", "y")
    every = node + local
    in_specs = (
        P(every, None),
        P(every, None),
        P(every, None),
        P(local, None, node),
        P(local, None, node),
        P(local, node, None),
        P(node, local),
        P(node, local),
        P(local, None, None),
        P(local, None, None),
        P(node, None, None),
        P(node, None, None),
        P(node, None),
        P(node, None),
        P(node),
    )
    out_specs = (P(every, None), P(node, local))
    return jax.shard_map(body, mesh=cube, in_specs=in_specs, out_specs=out_specs, check_vma=False)
```

```python
import functools

import jax
import jax.numpy as jnp
import numpy as np
from jax import lax
from jax.experimental import pallas as pl
from jax.experimental.pallas import tpu as pltpu
from jax.sharding import Mesh, PartitionSpec as P

NOPE = 128
ROPE = 64
NEW = 64
CACHE = 4096
EXPERTS = 16
ROUTE_SCALE = 2.5
NEG_BIG = -1e30
AXES = ("z", "core", "x", "y")
SIZES = (4, 2, 4, 4)
RING = 4
ORDERS = ((0, 3, 2), (2, 0, 3))
KERNEL_VMEM = 28 * 1024 * 1024
PACK = 128
DEPTH = 1024
UNITS = 256
HALF = 64
KEY_BLOCK = 1024
HEAD_COUNT = 8
PARTS = 2
LATENT = 512
LOG2E = 1.4426950408889634


def shift(value, phase, distance):
    pairs = []
    for place in np.ndindex(*SIZES):
        target = list(place)
        axis = ORDERS[place[1]][phase]
        target[axis] = (target[axis] + distance) % RING
        pairs.append((int(np.ravel_multi_index(place, SIZES)), int(np.ravel_multi_index(target, SIZES))))
    return lax.ppermute(value, AXES, pairs)


def widened(value):
    return value.astype(jnp.float32)


def narrowed(value):
    return value.astype(jnp.bfloat16)


def added(*values):
    return sum(widened(value) for value in values)


def with_other_core(value):
    return lax.ppermute(value, "core", [(0, 1), (1, 0)])


def expert_kernel(expert_ref, *refs, sources, outputs):
    row_hbm = refs[:sources]
    both_ref, both_other_ref, down_ref, down_other_ref = refs[sources : sources + 4]
    out_refs = refs[sources + 4 : sources + 4 + outputs]
    rows_ref, sums_ref, hidden_ref, row_sem = refs[sources + 4 + outputs :]
    width = both_ref.shape[0]
    steps = width // DEPTH
    span = rows_ref.shape[0] // sources
    row_copies = [
        pltpu.make_async_copy(source, rows_ref.at[pl.ds(i * span, span)], row_sem.at[i])
        for i, source in enumerate(row_hbm)
    ]
    for copy in row_copies:
        copy.start()
    sums_ref[...] = jnp.zeros_like(sums_ref)
    for copy in row_copies:
        copy.wait()

    @pl.loop(0, steps)
    def _(step):
        part = pl.ds(pl.multiple_of(step * DEPTH, DEPTH), DEPTH)
        piece = rows_ref[:, part]
        for i, matrix in enumerate((both_ref, both_other_ref)):
            sums_ref[i] += jnp.dot(piece, matrix[part, :], preferred_element_type=jnp.float32)

    extra = rows_ref[:, width : width + PACK].astype(jnp.float32)
    lane = lax.broadcasted_iota(jnp.int32, extra.shape, 1)
    pick = (lane % EXPERTS == expert_ref[0]) & (lane < 2 * EXPERTS)
    coefficient = jnp.sum(jnp.where(pick, extra, 0.0), axis=1, keepdims=True)
    for i in range(2):
        gate, up = sums_ref[i, :, :UNITS], sums_ref[i, :, UNITS:]
        hidden = gate / (1.0 + jnp.exp(-gate)) * up * coefficient
        hidden_ref[i] = jnp.where(coefficient > 0, hidden, 0.0).astype(jnp.bfloat16)

    @pl.loop(0, steps)
    def _(step):
        part = pl.ds(pl.multiple_of(step * DEPTH, DEPTH), DEPTH)
        result = jnp.dot(hidden_ref[0], down_ref[:, part], preferred_element_type=jnp.float32)
        result += jnp.dot(hidden_ref[1], down_other_ref[:, part], preferred_element_type=jnp.float32)
        result = result.astype(jnp.bfloat16)
        for i, out_ref in enumerate(out_refs):
            out_ref[:, part] = result[i * HALF : (i + 1) * HALF]


def expert_terms(expert, pieces, weights):
    width = weights[0].shape[0]
    rows = sum(piece.shape[0] for piece in pieces)
    outputs = rows // HALF
    weights = [pltpu.with_memory_space_constraint(matrix, pltpu.VMEM) for matrix in weights]
    return pl.pallas_call(
        functools.partial(expert_kernel, sources=len(pieces), outputs=outputs),
        in_specs=[pl.BlockSpec(memory_space=pltpu.SMEM)]
        + [pl.BlockSpec(memory_space=pl.ANY)] * len(pieces)
        + [pl.BlockSpec(memory_space=pltpu.VMEM)] * 4,
        out_specs=[pl.BlockSpec(memory_space=pltpu.VMEM)] * outputs,
        out_shape=[jax.ShapeDtypeStruct((HALF, width), jnp.bfloat16)] * outputs,
        scratch_shapes=[
            pltpu.VMEM((rows, width + PACK), jnp.bfloat16),
            pltpu.VMEM((2, rows, 2 * UNITS), jnp.float32),
            pltpu.VMEM((2, rows, UNITS), jnp.bfloat16),
            pltpu.SemaphoreType.DMA((len(pieces),)),
        ],
        compiler_params=pltpu.CompilerParams(vmem_limit_bytes=KERNEL_VMEM),
        cost_estimate=pl.CostEstimate(
            flops=6 * rows * width * UNITS * 2, bytes_accessed=4 * rows * width, transcendentals=0
        ),
        name="expert",
    )(expert, *pieces, *weights)


def pack_kernel(tokens_ref, routes_ref, scores_ref, out_ref):
    rows, width = tokens_ref.shape
    out_ref[:, :width] = tokens_ref[...]
    scores = scores_ref[...]
    weights = scores / jnp.sum(scores, axis=1, keepdims=True) * ROUTE_SCALE
    lane = lax.broadcasted_iota(jnp.int32, (rows, PACK), 1)
    dense = jnp.zeros((rows, PACK), jnp.float32)
    for choice in range(scores.shape[1]):
        named = routes_ref[:, choice : choice + 1] == lane % EXPERTS
        dense += jnp.where(named, weights[:, choice : choice + 1], 0.0)
    high = dense.astype(jnp.bfloat16).astype(jnp.float32)
    extra = jnp.where(lane < EXPERTS, high, jnp.where(lane < 2 * EXPERTS, dense - high, 0.0))
    out_ref[:, width:] = extra.astype(jnp.bfloat16)


def packed_rows(tokens, routes, gate_scores):
    rows, width = tokens.shape
    return pl.pallas_call(
        pack_kernel,
        out_shape=jax.ShapeDtypeStruct((rows, width + PACK), jnp.bfloat16),
        name="pack",
    )(tokens, routes, gate_scores)


def attention_kernel(
    sequence, length_ref, nope_ref, rope_ref, key_up_ref, value_up_ref, latent_ref, rope_key_ref,
    new_latent_ref, new_rope_ref, out_ref, query_ref, query_rope_ref, top_ref, sum_ref, total_ref,
):
    step = pl.program_id(0)
    length = length_ref[0]
    scale = (NOPE + ROPE) ** (-0.5) * LOG2E
    contract_last = (((1,), (1,)), ((), ()))

    def absorb(keys, rope_keys, values, bias):
        rows = HEAD_COUNT * NEW // PARTS
        parts = [slice(part * rows, (part + 1) * rows) for part in range(PARTS)]
        biases = [bias if bias.shape[0] == 1 else bias[part] for part in parts]
        scores = []
        for part, added_bias in zip(parts, biases):
            score = lax.dot_general(query_ref[part, :], keys, contract_last, preferred_element_type=jnp.float32)
            score += jnp.dot(query_rope_ref[part, :], rope_keys, preferred_element_type=jnp.float32)
            scores.append(score * scale + added_bias)
        for part, score in zip(parts, scores):
            old_top = top_ref[part, :]
            top = jnp.maximum(old_top, jnp.max(score, axis=1, keepdims=True))
            shrink = jnp.exp2(old_top - top)
            probs = jnp.exp2(score - top)
            top_ref[part, :] = top
            sum_ref[part, :] = sum_ref[part, :] * shrink + jnp.sum(probs, axis=1, keepdims=True)
            total_ref[part, :] = total_ref[part, :] * shrink + jnp.dot(
                probs.astype(jnp.bfloat16), values, preferred_element_type=jnp.float32
            )

    @pl.when(step == 0)
    def _():
        for head in range(HEAD_COUNT):
            query_ref[head * NEW : (head + 1) * NEW, :] = jnp.dot(
                nope_ref[:, head * NOPE : (head + 1) * NOPE], key_up_ref[head], preferred_element_type=jnp.float32
            ).astype(jnp.bfloat16)
            query_rope_ref[head * NEW : (head + 1) * NEW, :] = rope_ref[:, head * ROPE : (head + 1) * ROPE]
        top_ref[...] = jnp.full_like(top_ref, NEG_BIG)
        sum_ref[...] = jnp.zeros_like(sum_ref)
        total_ref[...] = jnp.zeros_like(total_ref)
        position = lax.broadcasted_iota(jnp.int32, (HEAD_COUNT * NEW, NEW), 0) % NEW
        fresh = lax.broadcasted_iota(jnp.int32, (HEAD_COUNT * NEW, NEW), 1)
        bias = jnp.where(fresh <= position, 0.0, NEG_BIG)
        absorb(new_latent_ref[...], new_rope_ref[:, sequence * NEW : (sequence + 1) * NEW], new_latent_ref[...], bias)

    @pl.when(step * KEY_BLOCK < length)
    def _():
        slot = step * KEY_BLOCK + lax.broadcasted_iota(jnp.int32, (1, KEY_BLOCK), 1)
        bias = jnp.where(slot < length, 0.0, NEG_BIG)
        absorb(latent_ref[...], rope_key_ref[...], latent_ref[...], bias)

    @pl.when(step == pl.num_programs(0) - 1)
    def _():
        latent_out = (total_ref[...] / sum_ref[...]).astype(jnp.bfloat16)
        for head in range(HEAD_COUNT):
            out_ref[:, head * NOPE : (head + 1) * NOPE] = jnp.dot(
                latent_out[head * NEW : (head + 1) * NEW], value_up_ref[head], preferred_element_type=jnp.float32
            ).astype(jnp.bfloat16)


def attend(sequence, length, nope, rope, key_up, value_up, latent_cache, rope_cache, new_latent, new_rope):
    rows = HEAD_COUNT * NEW

    def whole(*shape):
        return pl.BlockSpec(shape, lambda step, length: (0,) * len(shape))

    def live(step, length):
        return (sequence, jnp.minimum(step, (length[0] + KEY_BLOCK - 1) // KEY_BLOCK - 1), 0)

    def live_last(step, length):
        sequence_place, block, column = live(step, length)
        return (sequence_place, column, block)

    def own(*shape):
        return pl.BlockSpec(shape, lambda step, length: (sequence,) + (0,) * (len(shape) - 1))

    return pl.pallas_call(
        functools.partial(attention_kernel, sequence),
        grid_spec=pltpu.PrefetchScalarGridSpec(
            num_scalar_prefetch=1,
            grid=(CACHE // KEY_BLOCK,),
            in_specs=[
                own(NEW, HEAD_COUNT * NOPE),
                own(NEW, HEAD_COUNT * ROPE),
                whole(HEAD_COUNT, NOPE, LATENT),
                whole(HEAD_COUNT, LATENT, NOPE),
                pl.BlockSpec((None, KEY_BLOCK, LATENT), live),
                pl.BlockSpec((None, ROPE, KEY_BLOCK), live_last),
                own(NEW, LATENT),
                pl.BlockSpec((ROPE, 2 * NEW), lambda step, length: (0, 0)),
            ],
            out_specs=whole(NEW, HEAD_COUNT * NOPE),
            scratch_shapes=[
                pltpu.VMEM((rows, LATENT), jnp.bfloat16),
                pltpu.VMEM((rows, ROPE), jnp.bfloat16),
                pltpu.VMEM((rows, 1), jnp.float32),
                pltpu.VMEM((rows, 1), jnp.float32),
                pltpu.VMEM((rows, LATENT), jnp.float32),
            ],
        ),
        out_shape=jax.ShapeDtypeStruct((NEW, HEAD_COUNT * NOPE), jnp.bfloat16),
        compiler_params=pltpu.CompilerParams(vmem_limit_bytes=KERNEL_VMEM),
        cost_estimate=pl.CostEstimate(flops=6_000_000_000, bytes_accessed=8_000_000, transcendentals=2_100_000),
        name="attend",
    )(length, nope, rope, key_up, value_up, latent_cache, rope_cache, new_latent, new_rope)


def body(
    tokens,
    routes,
    gate_scores,
    gate_weight,
    up_weight,
    down_weight,
    query_nope,
    query_rope,
    key_up,
    value_up,
    latent_cache,
    rope_cache,
    new_latent,
    new_rope,
    lengths,
):
    packed = packed_rows(tokens, routes, gate_scores)
    gathered = [packed] + [shift(packed, 0, -distance) for distance in (1, 2, 3)]
    packed, gate_weight, up_weight = lax.optimization_barrier((packed, gate_weight, up_weight))
    both = jnp.concatenate([gate_weight[0], up_weight[0]], axis=1)
    small = jnp.concatenate(gathered, axis=0)
    small, both, down_part = lax.optimization_barrier((small, both, down_weight[0]))
    weights = (both, with_other_core(both), down_part, with_other_core(down_part))
    expert = (lax.axis_index("x") * RING + lax.axis_index("y")).astype(jnp.int32)[None]
    rope_keys, new_rope_keys = jnp.swapaxes(rope_cache, 1, 2), new_rope.T

    def attention(sequence, length):
        return attend(
            sequence, length, query_nope, query_rope, key_up, value_up, latent_cache, rope_keys, new_latent, new_rope_keys
        )

    above, below = shift(small, 1, -1), shift(small, 1, 1)
    half = small.shape[0] // 2
    own_low = jnp.concatenate([small, above], axis=0)
    below_low, above_low = shift(own_low, 2, 1), shift(own_low, 2, -1)
    far_low, far_high = shift(below[:half], 1, 1), shift(above[half:], 1, -1)
    own_high = jnp.concatenate([far_low, far_high, below], axis=0)
    below_high, above_high = shift(own_high, 2, 1), shift(own_high, 2, -1)
    own_terms = expert_terms(expert, [own_low, own_high], weights)
    far_low, far_high = shift(below_low, 2, 1), shift(above_high, 2, -1)
    above_low, above_high, below_low, below_high, own_terms = lax.optimization_barrier(
        (above_low, above_high, below_low, below_high, own_terms)
    )
    above_low, above_high, below_low, below_high = expert_terms(
        expert, [above_low, above_high, below_low, below_high], weights
    )
    near_high, near_low = shift(above_high, 2, 1), shift(below_low, 2, -1)
    far_low, far_high, above_high, below_low = lax.optimization_barrier((far_low, far_high, above_high, below_low))
    far_terms = expert_terms(expert, [far_low, far_high], weights)
    far_terms, near_high, near_low = lax.optimization_barrier((far_terms, near_high, near_low))
    from_below, from_above = shift(far_terms[0], 2, 1), shift(far_terms[1], 2, -1)
    far_terms, lengths = lax.optimization_barrier((far_terms, lengths))
    first_attention = attention(0, lengths[:1])
    from_below, from_above, first_attention, lengths = lax.optimization_barrier(
        (from_below, from_above, first_attention, lengths)
    )
    from_below = shift(narrowed(added(above_low, from_below)), 2, 1)
    from_above = shift(narrowed(added(below_high, from_above)), 2, -1)
    second_attention = attention(1, lengths[1:])
    from_below, from_above, second_attention = lax.optimization_barrier((from_below, from_above, second_attention))
    low = added(own_terms[0], near_low, from_below)
    high = added(own_terms[1], near_high, from_above)

    size = HALF // 2
    half = size // 2
    above, far, below = low[size:], high[:size], high[size:]
    up_first = narrowed(jnp.concatenate([far[:half], above[half:]], axis=0))
    down_first = narrowed(jnp.concatenate([far[half:], below[:half]], axis=0))
    from_below, from_above = shift(up_first, 1, 1), shift(down_first, 1, -1)
    up_second = shift(narrowed(added(above[:half], from_below[:half])), 1, 1)
    down_second = shift(narrowed(added(below[half:], from_above[:half])), 1, -1)
    total = low[:size] + jnp.concatenate(
        [added(up_second, from_above[half:]), added(down_second, from_below[half:])], axis=0
    )

    total = narrowed(total)
    rows = tokens.shape[0]
    arrived = [shift(total[distance * rows : (distance + 1) * rows], 0, distance) for distance in (1, 2, 3)]
    routed_out = narrowed(added(total[:rows], *arrived))
    return (routed_out, jnp.concatenate([first_attention, second_attention], axis=0))


def solution(mesh):
    cube = Mesh(mesh.devices.reshape(4, 2, 4, 4), ("z", "core", "x", "y"))
    node, local = ("z", "core"), ("x", "y")
    every = node + local
    in_specs = (
        P(every, None),
        P(every, None),
        P(every, None),
        P(local, None, node),
        P(local, None, node),
        P(local, node, None),
        P(node, local),
        P(node, local),
        P(local, None, None),
        P(local, None, None),
        P(node, None, None),
        P(node, None, None),
        P(node, None),
        P(node, None),
        P(node),
    )
    out_specs = (P(every, None), P(node, local))
    return jax.shard_map(body, mesh=cube, in_specs=in_specs, out_specs=out_specs, check_vma=False)
```

```python
import functools

import jax
import jax.numpy as jnp
import numpy as np
from jax import lax
from jax.experimental import pallas as pl
from jax.experimental.pallas import tpu as pltpu
from jax.sharding import Mesh, PartitionSpec as P

NOPE = 128
ROPE = 64
NEW = 64
CACHE = 4096
EXPERTS = 16
ROUTE_SCALE = 2.5
NEG_BIG = -1e30
AXES = ("z", "core", "x", "y")
SIZES = (4, 2, 4, 4)
RING = 4
ORDERS = ((0, 3, 2), (2, 0, 3))
KERNEL_VMEM = 12 * 1024 * 1024
EXPERT_VMEM = 10 * 1024 * 1024
PACK = 128
DEPTH = 1024
UNITS = 256
HALF = 64
KEY_BLOCK = 1024
HEAD_COUNT = 8
PARTS = 2
LATENT = 512
LOG2E = 1.4426950408889634


def shift(value, phase, distance):
    pairs = []
    for place in np.ndindex(*SIZES):
        target = list(place)
        axis = ORDERS[place[1]][phase]
        target[axis] = (target[axis] + distance) % RING
        pairs.append((int(np.ravel_multi_index(place, SIZES)), int(np.ravel_multi_index(target, SIZES))))
    return lax.ppermute(value, AXES, pairs)


def widened(value):
    return value.astype(jnp.float32)


def narrowed(value):
    return value.astype(jnp.bfloat16)


def added(*values):
    return sum(widened(value) for value in values)


def with_other_core(value):
    return lax.ppermute(value, "core", [(0, 1), (1, 0)])


def expert_kernel(*refs, sources, outputs):
    row_hbm = refs[:sources]
    both_ref, both_other_ref, down_ref, down_other_ref = refs[sources : sources + 4]
    out_refs = refs[sources + 4 : sources + 4 + outputs]
    rows_ref, hidden_ref, row_sem = refs[sources + 4 + outputs :]
    width = both_ref.shape[0]
    span = rows_ref.shape[0] // sources
    row_copies = [
        pltpu.make_async_copy(source, rows_ref.at[pl.ds(i * span, span)], row_sem.at[i])
        for i, source in enumerate(row_hbm)
    ]
    for copy in row_copies:
        copy.start()
    for copy in row_copies:
        copy.wait()
    extra = rows_ref[:, width : width + PACK].astype(jnp.float32)
    lane = lax.broadcasted_iota(jnp.int32, extra.shape, 1)
    expert = lax.axis_index("x") * RING + lax.axis_index("y")
    pick = (lane % EXPERTS == expert) & (lane < 2 * EXPERTS)
    coefficient = jnp.sum(jnp.where(pick, extra, 0.0), axis=1, keepdims=True)
    for i, matrix in enumerate((both_ref, both_other_ref)):
        sums = sum(
            jnp.dot(rows_ref[:, k : k + DEPTH], matrix[k : k + DEPTH, :], preferred_element_type=jnp.float32)
            for k in range(0, width, DEPTH)
        )
        gate, up = sums[:, :UNITS], sums[:, UNITS:]
        hidden = gate / (1.0 + jnp.exp(-gate)) * up * coefficient
        hidden_ref[i] = jnp.where(coefficient > 0, hidden, 0.0).astype(jnp.bfloat16)
    for start in range(0, width, DEPTH):
        part = slice(start, start + DEPTH)
        result = jnp.dot(hidden_ref[0], down_ref[:, part], preferred_element_type=jnp.float32)
        result += jnp.dot(hidden_ref[1], down_other_ref[:, part], preferred_element_type=jnp.float32)
        result = result.astype(jnp.bfloat16)
        for i, out_ref in enumerate(out_refs):
            out_ref[:, part] = result[i * HALF : (i + 1) * HALF]


def expert_terms(pieces, weights):
    width = weights[0].shape[0]
    rows = sum(piece.shape[0] for piece in pieces)
    outputs = rows // HALF
    weights = [pltpu.with_memory_space_constraint(matrix, pltpu.VMEM) for matrix in weights]
    return pl.pallas_call(
        functools.partial(expert_kernel, sources=len(pieces), outputs=outputs),
        in_specs=[pl.BlockSpec(memory_space=pl.ANY)] * len(pieces)
        + [pl.BlockSpec(memory_space=pltpu.VMEM)] * 4,
        out_specs=[pl.BlockSpec(memory_space=pltpu.VMEM)] * outputs,
        out_shape=[jax.ShapeDtypeStruct((HALF, width), jnp.bfloat16)] * outputs,
        scratch_shapes=[
            pltpu.VMEM((rows, width + PACK), jnp.bfloat16),
            pltpu.VMEM((2, rows, UNITS), jnp.bfloat16),
            pltpu.SemaphoreType.DMA((len(pieces),)),
        ],
        compiler_params=pltpu.CompilerParams(vmem_limit_bytes=EXPERT_VMEM),
        cost_estimate=pl.CostEstimate(
            flops=6 * rows * width * UNITS * 2, bytes_accessed=4 * rows * width, transcendentals=0
        ),
        name="expert",
    )(*pieces, *weights)


def join_kernel(gate_hbm, up_hbm, out_ref, sem):
    copies = [
        pltpu.make_async_copy(source, out_ref.at[:, pl.ds(i * UNITS, UNITS)], sem.at[i])
        for i, source in enumerate((gate_hbm, up_hbm))
    ]
    for copy in copies:
        copy.start()
    for copy in copies:
        copy.wait()


def joined(gate, up):
    return pl.pallas_call(
        join_kernel,
        in_specs=[pl.BlockSpec(memory_space=pl.ANY)] * 2,
        out_specs=pl.BlockSpec(memory_space=pltpu.VMEM),
        out_shape=pltpu.VMEM((gate.shape[0], 2 * UNITS), jnp.bfloat16),
        scratch_shapes=[pltpu.SemaphoreType.DMA((2,))],
        compiler_params=pltpu.CompilerParams(vmem_limit_bytes=KERNEL_VMEM),
        cost_estimate=pl.CostEstimate(flops=0, bytes_accessed=8 * gate.shape[0] * UNITS, transcendentals=0),
        name="join",
    )(*(pltpu.with_memory_space_constraint(value, pltpu.HBM) for value in (gate, up)))


def pack_kernel(tokens_ref, routes_ref, scores_ref, out_ref):
    rows, width = tokens_ref.shape
    out_ref[:, :width] = tokens_ref[...]
    scores = scores_ref[...]
    weights = scores / jnp.sum(scores, axis=1, keepdims=True) * ROUTE_SCALE
    lane = lax.broadcasted_iota(jnp.int32, (rows, PACK), 1)
    dense = jnp.zeros((rows, PACK), jnp.float32)
    for choice in range(scores.shape[1]):
        named = routes_ref[:, choice : choice + 1] == lane % EXPERTS
        dense += jnp.where(named, weights[:, choice : choice + 1], 0.0)
    high = dense.astype(jnp.bfloat16).astype(jnp.float32)
    extra = jnp.where(lane < EXPERTS, high, jnp.where(lane < 2 * EXPERTS, dense - high, 0.0))
    out_ref[:, width:] = extra.astype(jnp.bfloat16)


def packed_rows(tokens, routes, gate_scores):
    rows, width = tokens.shape
    return pl.pallas_call(
        pack_kernel,
        out_shape=jax.ShapeDtypeStruct((rows, width + PACK), jnp.bfloat16),
        compiler_params=pltpu.CompilerParams(vmem_limit_bytes=KERNEL_VMEM),
        name="pack",
    )(tokens, routes, gate_scores)


def attention_kernel(
    sequence, length_ref, nope_ref, rope_ref, key_up_ref, value_up_ref, latent_ref, rope_key_ref,
    new_latent_ref, new_rope_ref, out_ref, query_ref, query_rope_ref, top_ref, sum_ref, total_ref,
):
    step = pl.program_id(0)
    length = length_ref[0]
    scale = (NOPE + ROPE) ** (-0.5) * LOG2E
    contract_last = (((1,), (1,)), ((), ()))

    def absorb(keys, rope_keys, values, bias):
        rows = HEAD_COUNT * NEW // PARTS
        parts = [slice(part * rows, (part + 1) * rows) for part in range(PARTS)]
        biases = [bias if bias.shape[0] == 1 else bias[part] for part in parts]
        scores = []
        for part, added_bias in zip(parts, biases):
            score = lax.dot_general(query_ref[part, :], keys, contract_last, preferred_element_type=jnp.float32)
            score += jnp.dot(query_rope_ref[part, :], rope_keys, preferred_element_type=jnp.float32)
            scores.append(score * scale + added_bias)
        for part, score in zip(parts, scores):
            old_top = top_ref[part, :]
            top = jnp.maximum(old_top, jnp.max(score, axis=1, keepdims=True))
            shrink = jnp.exp2(old_top - top)
            probs = jnp.exp2(score - top)
            top_ref[part, :] = top
            sum_ref[part, :] = sum_ref[part, :] * shrink + jnp.sum(probs, axis=1, keepdims=True)
            total_ref[part, :] = total_ref[part, :] * shrink + jnp.dot(
                probs.astype(jnp.bfloat16), values, preferred_element_type=jnp.float32
            )

    @pl.when(step == 0)
    def _():
        for head in range(HEAD_COUNT):
            query_ref[head * NEW : (head + 1) * NEW, :] = jnp.dot(
                nope_ref[:, head * NOPE : (head + 1) * NOPE], key_up_ref[head], preferred_element_type=jnp.float32
            ).astype(jnp.bfloat16)
            query_rope_ref[head * NEW : (head + 1) * NEW, :] = rope_ref[:, head * ROPE : (head + 1) * ROPE]
        top_ref[...] = jnp.full_like(top_ref, NEG_BIG)
        sum_ref[...] = jnp.zeros_like(sum_ref)
        total_ref[...] = jnp.zeros_like(total_ref)
        position = lax.broadcasted_iota(jnp.int32, (HEAD_COUNT * NEW, NEW), 0) % NEW
        fresh = lax.broadcasted_iota(jnp.int32, (HEAD_COUNT * NEW, NEW), 1)
        bias = jnp.where(fresh <= position, 0.0, NEG_BIG)
        absorb(new_latent_ref[...], new_rope_ref[:, sequence * NEW : (sequence + 1) * NEW], new_latent_ref[...], bias)

    @pl.when(step * KEY_BLOCK < length)
    def _():
        slot = step * KEY_BLOCK + lax.broadcasted_iota(jnp.int32, (1, KEY_BLOCK), 1)
        bias = jnp.where(slot < length, 0.0, NEG_BIG)
        absorb(latent_ref[...], rope_key_ref[...], latent_ref[...], bias)

    @pl.when(step == pl.num_programs(0) - 1)
    def _():
        latent_out = (total_ref[...] / sum_ref[...]).astype(jnp.bfloat16)
        for head in range(HEAD_COUNT):
            out_ref[:, head * NOPE : (head + 1) * NOPE] = jnp.dot(
                latent_out[head * NEW : (head + 1) * NEW], value_up_ref[head], preferred_element_type=jnp.float32
            ).astype(jnp.bfloat16)


def attend(sequence, length, nope, rope, key_up, value_up, latent_cache, rope_cache, new_latent, new_rope):
    rows = HEAD_COUNT * NEW

    def whole(*shape):
        return pl.BlockSpec(shape, lambda step, length: (0,) * len(shape))

    def live(step, length):
        return (sequence, jnp.minimum(step, (length[0] + KEY_BLOCK - 1) // KEY_BLOCK - 1), 0)

    def live_last(step, length):
        sequence_place, block, column = live(step, length)
        return (sequence_place, column, block)

    def own(*shape):
        return pl.BlockSpec(shape, lambda step, length: (sequence,) + (0,) * (len(shape) - 1))

    return pl.pallas_call(
        functools.partial(attention_kernel, sequence),
        grid_spec=pltpu.PrefetchScalarGridSpec(
            num_scalar_prefetch=1,
            grid=(CACHE // KEY_BLOCK,),
            in_specs=[
                own(NEW, HEAD_COUNT * NOPE),
                own(NEW, HEAD_COUNT * ROPE),
                whole(HEAD_COUNT, NOPE, LATENT),
                whole(HEAD_COUNT, LATENT, NOPE),
                pl.BlockSpec((None, KEY_BLOCK, LATENT), live),
                pl.BlockSpec((None, ROPE, KEY_BLOCK), live_last),
                own(NEW, LATENT),
                pl.BlockSpec((ROPE, 2 * NEW), lambda step, length: (0, 0)),
            ],
            out_specs=whole(NEW, HEAD_COUNT * NOPE),
            scratch_shapes=[
                pltpu.VMEM((rows, LATENT), jnp.bfloat16),
                pltpu.VMEM((rows, ROPE), jnp.bfloat16),
                pltpu.VMEM((rows, 1), jnp.float32),
                pltpu.VMEM((rows, 1), jnp.float32),
                pltpu.VMEM((rows, LATENT), jnp.float32),
            ],
        ),
        out_shape=jax.ShapeDtypeStruct((NEW, HEAD_COUNT * NOPE), jnp.bfloat16),
        compiler_params=pltpu.CompilerParams(vmem_limit_bytes=KERNEL_VMEM),
        cost_estimate=pl.CostEstimate(flops=6_000_000_000, bytes_accessed=8_000_000, transcendentals=2_100_000),
        name="attend",
    )(length, nope, rope, key_up, value_up, latent_cache, rope_cache, new_latent, new_rope)


def body(
    tokens,
    routes,
    gate_scores,
    gate_weight,
    up_weight,
    down_weight,
    query_nope,
    query_rope,
    key_up,
    value_up,
    latent_cache,
    rope_cache,
    new_latent,
    new_rope,
    lengths,
):
    packed = packed_rows(tokens, routes, gate_scores)
    gathered = [packed] + [shift(packed, 0, -distance) for distance in (1, 2, 3)]
    packed, gate_weight, up_weight = lax.optimization_barrier((packed, gate_weight, up_weight))
    both = joined(gate_weight[0], up_weight[0])
    small = jnp.concatenate(gathered, axis=0)
    small, both, down_part = lax.optimization_barrier((small, both, down_weight[0]))
    weights = (both, with_other_core(both), down_part, with_other_core(down_part))
    rope_keys, new_rope_keys = jnp.swapaxes(rope_cache, 1, 2), new_rope.T

    def attention(sequence, length):
        return attend(
            sequence, length, query_nope, query_rope, key_up, value_up, latent_cache, rope_keys, new_latent, new_rope_keys
        )

    above, below = shift(small, 1, -1), shift(small, 1, 1)
    half = small.shape[0] // 2
    own_low = jnp.concatenate([small, above], axis=0)
    below_low, above_low = shift(own_low, 2, 1), shift(own_low, 2, -1)
    far_low, far_high = shift(below[:half], 1, 1), shift(above[half:], 1, -1)
    own_high = jnp.concatenate([far_low, far_high, below], axis=0)
    below_high, above_high = shift(own_high, 2, 1), shift(own_high, 2, -1)
    own_terms = expert_terms([own_low, own_high], weights)
    below_low, above_high, own_terms = lax.optimization_barrier((below_low, above_high, own_terms))
    far_low, far_high = shift(below_low, 2, 1), shift(above_high, 2, -1)
    above_low, above_high, below_low, below_high = expert_terms(
        [above_low, above_high, below_low, below_high], weights
    )
    near_high, near_low = shift(above_high, 2, 1), shift(below_low, 2, -1)
    far_low, far_high, above_high, below_low = lax.optimization_barrier((far_low, far_high, above_high, below_low))
    far_terms = expert_terms([far_low, far_high], weights)
    far_terms, near_high, near_low = lax.optimization_barrier((far_terms, near_high, near_low))
    from_below, from_above = shift(far_terms[0], 2, 1), shift(far_terms[1], 2, -1)
    far_terms, lengths = lax.optimization_barrier((far_terms, lengths))
    first_attention = attention(0, lengths[:1])
    from_below, from_above, first_attention, lengths = lax.optimization_barrier(
        (from_below, from_above, first_attention, lengths)
    )
    from_below = shift(narrowed(added(above_low, from_below)), 2, 1)
    from_above = shift(narrowed(added(below_high, from_above)), 2, -1)
    second_attention = attention(1, lengths[1:])
    from_below, from_above, second_attention = lax.optimization_barrier((from_below, from_above, second_attention))
    low = added(own_terms[0], near_low, from_below)
    high = added(own_terms[1], near_high, from_above)

    size = HALF // 2
    half = size // 2
    above, far, below = low[size:], high[:size], high[size:]
    up_first = narrowed(jnp.concatenate([far[:half], above[half:]], axis=0))
    down_first = narrowed(jnp.concatenate([far[half:], below[:half]], axis=0))
    from_below, from_above = shift(up_first, 1, 1), shift(down_first, 1, -1)
    up_second = narrowed(added(above[:half], from_below[:half]))
    down_second = narrowed(added(below[half:], from_above[:half]))
    up_second, down_second = lax.optimization_barrier((up_second, down_second))
    up_second, down_second = shift(up_second, 1, 1), shift(down_second, 1, -1)
    total = low[:size] + jnp.concatenate(
        [added(up_second, from_above[half:]), added(down_second, from_below[half:])], axis=0
    )

    total = narrowed(total)
    rows = tokens.shape[0]
    arrived = [shift(total[distance * rows : (distance + 1) * rows], 0, distance) for distance in (1, 2, 3)]
    routed_out = narrowed(added(total[:rows], *arrived))
    return (routed_out, jnp.concatenate([first_attention, second_attention], axis=0))


def solution(mesh):
    cube = Mesh(mesh.devices.reshape(4, 2, 4, 4), ("z", "core", "x", "y"))
    node, local = ("z", "core"), ("x", "y")
    every = node + local
    in_specs = (
        P(every, None),
        P(every, None),
        P(every, None),
        P(local, None, node),
        P(local, None, node),
        P(local, node, None),
        P(node, local),
        P(node, local),
        P(local, None, None),
        P(local, None, None),
        P(node, None, None),
        P(node, None, None),
        P(node, None),
        P(node, None),
        P(node),
    )
    out_specs = (P(every, None), P(node, local))
    return jax.shard_map(body, mesh=cube, in_specs=in_specs, out_specs=out_specs, check_vma=False)
```

```python
import functools

import jax
import jax.numpy as jnp
import numpy as np
from jax import lax
from jax.experimental import pallas as pl
from jax.experimental.pallas import tpu as pltpu
from jax.sharding import Mesh, PartitionSpec as P

NOPE = 128
ROPE = 64
NEW = 64
CACHE = 4096
EXPERTS = 16
ROUTE_SCALE = 2.5
NEG_BIG = -1e30
AXES = ("z", "core", "x", "y")
SIZES = (4, 2, 4, 4)
RING = 4
ORDERS = ((0, 3, 2), (2, 0, 3))
KERNEL_VMEM = 12 * 1024 * 1024
EXPERT_VMEM = 10 * 1024 * 1024
PACK = 128
DEPTH = 512
UNITS = 256
HALF = 64
KEY_BLOCK = 1024
HEAD_COUNT = 8
PARTS = 2
LATENT = 512
LOG2E = 1.4426950408889634


def shift(value, phase, distance):
    pairs = []
    for place in np.ndindex(*SIZES):
        target = list(place)
        axis = ORDERS[place[1]][phase]
        target[axis] = (target[axis] + distance) % RING
        pairs.append((int(np.ravel_multi_index(place, SIZES)), int(np.ravel_multi_index(target, SIZES))))
    return lax.ppermute(value, AXES, pairs)


def widened(value):
    return value.astype(jnp.float32)


def narrowed(value):
    return value.astype(jnp.bfloat16)


def added(*values):
    return sum(widened(value) for value in values)


def with_other_core(value):
    return lax.ppermute(value, "core", [(0, 1), (1, 0)])


def expert_kernel(*refs, sources, outputs):
    row_hbm = refs[:sources]
    matrices = refs[sources : sources + 2]
    out_refs = refs[sources + 2 : sources + 2 + outputs]
    rows_ref, hidden_ref, row_sem = refs[sources + 2 + outputs :]
    width = out_refs[0].shape[1]
    span = rows_ref.shape[0] // sources
    row_copies = [
        pltpu.make_async_copy(source, rows_ref.at[pl.ds(i * span, span)], row_sem.at[i])
        for i, source in enumerate(row_hbm)
    ]
    for copy in row_copies:
        copy.start()
    for copy in row_copies:
        copy.wait()
    extra = rows_ref[:, width : width + PACK].astype(jnp.float32)
    lane = lax.broadcasted_iota(jnp.int32, extra.shape, 1)
    expert = lax.axis_index("x") * RING + lax.axis_index("y")
    pick = (lane % EXPERTS == expert) & (lane < 2 * EXPERTS)
    coefficient = jnp.sum(jnp.where(pick, extra, 0.0), axis=1, keepdims=True)
    for i, matrix in enumerate(matrices):
        sums = sum(
            jnp.dot(rows_ref[:, k : k + 2 * DEPTH], matrix[k : k + 2 * DEPTH, :], preferred_element_type=jnp.float32)
            for k in range(0, width, 2 * DEPTH)
        )
        gate, up = sums[:, :UNITS], sums[:, UNITS:]
        hidden = gate / (1.0 + jnp.exp(-gate)) * up * coefficient
        hidden_ref[i] = jnp.where(coefficient > 0, hidden, 0.0).astype(jnp.bfloat16)
    for block in range(width // DEPTH):
        part, place = slice(block * DEPTH, (block + 1) * DEPTH), slice(width + block * UNITS, width + (block + 1) * UNITS)
        result = jnp.dot(hidden_ref[0], matrices[0][place, :], preferred_element_type=jnp.float32)
        result += jnp.dot(hidden_ref[1], matrices[1][place, :], preferred_element_type=jnp.float32)
        result = result.astype(jnp.bfloat16)
        for i, out_ref in enumerate(out_refs):
            out_ref[:, part] = result[i * HALF : (i + 1) * HALF]


def expert_terms(pieces, weights):
    width = pieces[0].shape[1] - PACK
    rows = sum(piece.shape[0] for piece in pieces)
    outputs = rows // HALF
    weights = [pltpu.with_memory_space_constraint(matrix, pltpu.VMEM) for matrix in weights]
    return pl.pallas_call(
        functools.partial(expert_kernel, sources=len(pieces), outputs=outputs),
        in_specs=[pl.BlockSpec(memory_space=pl.ANY)] * len(pieces)
        + [pl.BlockSpec(memory_space=pltpu.VMEM)] * 2,
        out_specs=[pl.BlockSpec(memory_space=pltpu.VMEM)] * outputs,
        out_shape=[jax.ShapeDtypeStruct((HALF, width), jnp.bfloat16)] * outputs,
        scratch_shapes=[
            pltpu.VMEM((rows, width + PACK), jnp.bfloat16),
            pltpu.VMEM((2, rows, UNITS), jnp.bfloat16),
            pltpu.SemaphoreType.DMA((len(pieces),)),
        ],
        compiler_params=pltpu.CompilerParams(vmem_limit_bytes=EXPERT_VMEM),
        cost_estimate=pl.CostEstimate(
            flops=6 * rows * width * UNITS * 2, bytes_accessed=4 * rows * width, transcendentals=0
        ),
        name="expert",
    )(*pieces, *weights)


def join_kernel(gate_hbm, up_hbm, down_hbm, out_ref, sem):
    width = gate_hbm.shape[0]
    copies = [
        pltpu.make_async_copy(source, out_ref.at[pl.ds(0, width), pl.ds(i * UNITS, UNITS)], sem.at[i])
        for i, source in enumerate((gate_hbm, up_hbm))
    ]
    for i in range(width // DEPTH):
        part = out_ref.at[pl.ds(width + i * UNITS, UNITS)]
        copies.append(pltpu.make_async_copy(down_hbm.at[:, pl.ds(i * DEPTH, DEPTH)], part, sem.at[2 + i]))
    for copy in copies:
        copy.start()
    for copy in copies:
        copy.wait()


def joined(gate, up, down):
    width = gate.shape[0]
    blocks = width // DEPTH
    matrices = [pltpu.with_memory_space_constraint(matrix, pltpu.HBM) for matrix in (gate, up, down)]
    return pl.pallas_call(
        join_kernel,
        in_specs=[pl.BlockSpec(memory_space=pl.ANY)] * 3,
        out_specs=pl.BlockSpec(memory_space=pltpu.VMEM),
        out_shape=pltpu.VMEM((width + blocks * UNITS, DEPTH), jnp.bfloat16),
        scratch_shapes=[pltpu.SemaphoreType.DMA((2 + blocks,))],
        compiler_params=pltpu.CompilerParams(vmem_limit_bytes=KERNEL_VMEM),
        cost_estimate=pl.CostEstimate(flops=0, bytes_accessed=12 * width * UNITS, transcendentals=0),
        name="join",
    )(*matrices)


def pack_kernel(tokens_ref, routes_ref, scores_ref, out_ref):
    rows, width = tokens_ref.shape
    out_ref[:, :width] = tokens_ref[...]
    scores = scores_ref[...]
    weights = scores / jnp.sum(scores, axis=1, keepdims=True) * ROUTE_SCALE
    lane = lax.broadcasted_iota(jnp.int32, (rows, PACK), 1)
    dense = jnp.zeros((rows, PACK), jnp.float32)
    for choice in range(scores.shape[1]):
        named = routes_ref[:, choice : choice + 1] == lane % EXPERTS
        dense += jnp.where(named, weights[:, choice : choice + 1], 0.0)
    high = dense.astype(jnp.bfloat16).astype(jnp.float32)
    extra = jnp.where(lane < EXPERTS, high, jnp.where(lane < 2 * EXPERTS, dense - high, 0.0))
    out_ref[:, width:] = extra.astype(jnp.bfloat16)


def packed_rows(tokens, routes, gate_scores):
    rows, width = tokens.shape
    return pl.pallas_call(
        pack_kernel,
        out_shape=jax.ShapeDtypeStruct((rows, width + PACK), jnp.bfloat16),
        compiler_params=pltpu.CompilerParams(vmem_limit_bytes=KERNEL_VMEM),
        name="pack",
    )(*(pltpu.with_memory_space_constraint(value, pltpu.HBM) for value in (tokens, routes, gate_scores)))


def attention_kernel(
    sequence, length_ref, nope_ref, rope_ref, key_up_ref, value_up_ref, latent_ref, rope_key_ref,
    new_latent_ref, new_rope_ref, out_ref, query_ref, query_rope_ref, top_ref, sum_ref, total_ref,
):
    step = pl.program_id(0)
    length = length_ref[0]
    scale = (NOPE + ROPE) ** (-0.5) * LOG2E
    contract_last = (((1,), (1,)), ((), ()))

    def absorb(keys, rope_keys, values, bias):
        rows = HEAD_COUNT * NEW // PARTS
        parts = [slice(part * rows, (part + 1) * rows) for part in range(PARTS)]
        biases = [bias if bias.shape[0] == 1 else bias[part] for part in parts]
        scores = []
        for part, added_bias in zip(parts, biases):
            score = lax.dot_general(query_ref[part, :], keys, contract_last, preferred_element_type=jnp.float32)
            score += jnp.dot(query_rope_ref[part, :], rope_keys, preferred_element_type=jnp.float32)
            scores.append(score * scale + added_bias)
        for part, score in zip(parts, scores):
            old_top = top_ref[part, :]
            top = jnp.maximum(old_top, jnp.max(score, axis=1, keepdims=True))
            shrink = jnp.exp2(old_top - top)
            probs = jnp.exp2(score - top)
            top_ref[part, :] = top
            sum_ref[part, :] = sum_ref[part, :] * shrink + jnp.sum(probs, axis=1, keepdims=True)
            total_ref[part, :] = total_ref[part, :] * shrink + jnp.dot(
                probs.astype(jnp.bfloat16), values, preferred_element_type=jnp.float32
            )

    @pl.when(step == 0)
    def _():
        for head in range(HEAD_COUNT):
            query_ref[head * NEW : (head + 1) * NEW, :] = jnp.dot(
                nope_ref[:, head * NOPE : (head + 1) * NOPE], key_up_ref[head], preferred_element_type=jnp.float32
            ).astype(jnp.bfloat16)
            query_rope_ref[head * NEW : (head + 1) * NEW, :] = rope_ref[:, head * ROPE : (head + 1) * ROPE]
        top_ref[...] = jnp.full_like(top_ref, NEG_BIG)
        sum_ref[...] = jnp.zeros_like(sum_ref)
        total_ref[...] = jnp.zeros_like(total_ref)
        position = lax.broadcasted_iota(jnp.int32, (HEAD_COUNT * NEW, NEW), 0) % NEW
        fresh = lax.broadcasted_iota(jnp.int32, (HEAD_COUNT * NEW, NEW), 1)
        bias = jnp.where(fresh <= position, 0.0, NEG_BIG)
        absorb(new_latent_ref[...], new_rope_ref[:, sequence * NEW : (sequence + 1) * NEW], new_latent_ref[...], bias)

    @pl.when(step * KEY_BLOCK < length)
    def _():
        slot = step * KEY_BLOCK + lax.broadcasted_iota(jnp.int32, (1, KEY_BLOCK), 1)
        bias = jnp.where(slot < length, 0.0, NEG_BIG)
        absorb(latent_ref[...], rope_key_ref[...], latent_ref[...], bias)

    @pl.when(step == pl.num_programs(0) - 1)
    def _():
        latent_out = (total_ref[...] / sum_ref[...]).astype(jnp.bfloat16)
        for head in range(HEAD_COUNT):
            out_ref[:, head * NOPE : (head + 1) * NOPE] = jnp.dot(
                latent_out[head * NEW : (head + 1) * NEW], value_up_ref[head], preferred_element_type=jnp.float32
            ).astype(jnp.bfloat16)


def attend(sequence, length, nope, rope, key_up, value_up, latent_cache, rope_cache, new_latent, new_rope):
    rows = HEAD_COUNT * NEW

    def whole(*shape):
        return pl.BlockSpec(shape, lambda step, length: (0,) * len(shape))

    def live(step, length):
        return (sequence, jnp.minimum(step, (length[0] + KEY_BLOCK - 1) // KEY_BLOCK - 1), 0)

    def live_last(step, length):
        sequence_place, block, column = live(step, length)
        return (sequence_place, column, block)

    def own(*shape):
        return pl.BlockSpec(shape, lambda step, length: (sequence,) + (0,) * (len(shape) - 1))

    return pl.pallas_call(
        functools.partial(attention_kernel, sequence),
        grid_spec=pltpu.PrefetchScalarGridSpec(
            num_scalar_prefetch=1,
            grid=(CACHE // KEY_BLOCK,),
            in_specs=[
                own(NEW, HEAD_COUNT * NOPE),
                own(NEW, HEAD_COUNT * ROPE),
                whole(HEAD_COUNT, NOPE, LATENT),
                whole(HEAD_COUNT, LATENT, NOPE),
                pl.BlockSpec((None, KEY_BLOCK, LATENT), live),
                pl.BlockSpec((None, ROPE, KEY_BLOCK), live_last),
                own(NEW, LATENT),
                pl.BlockSpec((ROPE, 2 * NEW), lambda step, length: (0, 0)),
            ],
            out_specs=whole(NEW, HEAD_COUNT * NOPE),
            scratch_shapes=[
                pltpu.VMEM((rows, LATENT), jnp.bfloat16),
                pltpu.VMEM((rows, ROPE), jnp.bfloat16),
                pltpu.VMEM((rows, 1), jnp.float32),
                pltpu.VMEM((rows, 1), jnp.float32),
                pltpu.VMEM((rows, LATENT), jnp.float32),
            ],
        ),
        out_shape=jax.ShapeDtypeStruct((NEW, HEAD_COUNT * NOPE), jnp.bfloat16),
        compiler_params=pltpu.CompilerParams(vmem_limit_bytes=KERNEL_VMEM),
        cost_estimate=pl.CostEstimate(flops=6_000_000_000, bytes_accessed=8_000_000, transcendentals=2_100_000),
        name="attend",
    )(length, nope, rope, key_up, value_up, latent_cache, rope_cache, new_latent, new_rope)


def body(
    tokens,
    routes,
    gate_scores,
    gate_weight,
    up_weight,
    down_weight,
    query_nope,
    query_rope,
    key_up,
    value_up,
    latent_cache,
    rope_cache,
    new_latent,
    new_rope,
    lengths,
):
    packed = packed_rows(tokens, routes, gate_scores)
    gathered = [packed] + [shift(packed, 0, -distance) for distance in (1, 2, 3)]
    packed, gate_weight, up_weight, down_weight = lax.optimization_barrier(
        (packed, gate_weight, up_weight, down_weight)
    )
    own_weights = joined(gate_weight[0], up_weight[0], down_weight[0])
    small = jnp.concatenate(gathered, axis=0)
    small, own_weights = lax.optimization_barrier((small, own_weights))
    weights = (own_weights, with_other_core(own_weights))
    rope_keys, new_rope_keys = jnp.swapaxes(rope_cache, 1, 2), new_rope.T

    def attention(sequence, length):
        return attend(
            sequence, length, query_nope, query_rope, key_up, value_up, latent_cache, rope_keys, new_latent, new_rope_keys
        )

    above, below = shift(small, 1, -1), shift(small, 1, 1)
    half = small.shape[0] // 2
    own_low = jnp.concatenate([small, above], axis=0)
    below_low, above_low = shift(own_low, 2, 1), shift(own_low, 2, -1)
    far_low, far_high = lax.optimization_barrier((below[:half], above[half:]))
    far_low, far_high = shift(far_low, 1, 1), shift(far_high, 1, -1)
    own_high = jnp.concatenate([far_low, far_high, below], axis=0)
    below_high, above_high = shift(own_high, 2, 1), shift(own_high, 2, -1)
    own_low, own_high, below_low, above_low = lax.optimization_barrier((own_low, own_high, below_low, above_low))
    own_terms = expert_terms([own_low, own_high], weights)
    below_low, above_high, own_terms = lax.optimization_barrier((below_low, above_high, own_terms))
    far_low, far_high = shift(below_low, 2, 1), shift(above_high, 2, -1)
    above_low, above_high, below_low, below_high = expert_terms(
        [above_low, above_high, below_low, below_high], weights
    )
    near_high, near_low = shift(above_high, 2, 1), shift(below_low, 2, -1)
    far_low, far_high, above_high, below_low = lax.optimization_barrier((far_low, far_high, above_high, below_low))
    far_terms = expert_terms([far_low, far_high], weights)
    from_below, from_above = shift(far_terms[0], 2, 1), shift(far_terms[1], 2, -1)
    far_terms, near_high, near_low, lengths = lax.optimization_barrier((far_terms, near_high, near_low, lengths))
    first_attention = attention(0, lengths[:1])
    from_below, from_above, first_attention, lengths = lax.optimization_barrier(
        (from_below, from_above, first_attention, lengths)
    )
    from_below = shift(narrowed(added(above_low, from_below)), 2, 1)
    from_above = shift(narrowed(added(below_high, from_above)), 2, -1)
    second_attention = attention(1, lengths[1:])
    from_below, from_above, second_attention = lax.optimization_barrier((from_below, from_above, second_attention))
    low = added(own_terms[0], near_low, from_below)
    high = added(own_terms[1], near_high, from_above)

    size = HALF // 2
    half = size // 2
    above, far, below = low[size:], high[:size], high[size:]
    up_first = narrowed(jnp.concatenate([far[:half], above[half:]], axis=0))
    down_first = narrowed(jnp.concatenate([far[half:], below[:half]], axis=0))
    from_below, from_above = shift(up_first, 1, 1), shift(down_first, 1, -1)
    up_second = narrowed(added(above[:half], from_below[:half]))
    down_second = narrowed(added(below[half:], from_above[:half]))
    up_second, down_second = lax.optimization_barrier((up_second, down_second))
    up_second, down_second = shift(up_second, 1, 1), shift(down_second, 1, -1)
    total = low[:size] + jnp.concatenate(
        [added(up_second, from_above[half:]), added(down_second, from_below[half:])], axis=0
    )

    total = narrowed(total)
    rows = tokens.shape[0]
    arrived = [shift(total[distance * rows : (distance + 1) * rows], 0, distance) for distance in (1, 2, 3)]
    routed_out = narrowed(added(total[:rows], *arrived))
    return (routed_out, jnp.concatenate([first_attention, second_attention], axis=0))


def solution(mesh):
    cube = Mesh(mesh.devices.reshape(4, 2, 4, 4), ("z", "core", "x", "y"))
    node, local = ("z", "core"), ("x", "y")
    every = node + local
    in_specs = (
        P(every, None),
        P(every, None),
        P(every, None),
        P(local, None, node),
        P(local, None, node),
        P(local, node, None),
        P(node, local),
        P(node, local),
        P(local, None, None),
        P(local, None, None),
        P(node, None, None),
        P(node, None, None),
        P(node, None),
        P(node, None),
        P(node),
    )
    out_specs = (P(every, None), P(node, local))
    return jax.shard_map(body, mesh=cube, in_specs=in_specs, out_specs=out_specs, check_vma=False)
```

```python
import functools

import jax
import jax.numpy as jnp
import numpy as np
from jax import lax
from jax.experimental import pallas as pl
from jax.experimental.pallas import tpu as pltpu
from jax.sharding import Mesh, PartitionSpec as P

NOPE = 128
ROPE = 64
NEW = 64
CACHE = 4096
EXPERTS = 16
ROUTE_SCALE = 2.5
NEG_BIG = -1e30
AXES = ("z", "core", "x", "y")
SIZES = (4, 2, 4, 4)
RING = 4
ORDERS = ((0, 3, 2), (2, 0, 3))
KERNEL_VMEM = 12 * 1024 * 1024
EXPERT_VMEM = 10 * 1024 * 1024
PACK = 128
DEPTH = 512
UNITS = 256
HALF = 64
KEY_BLOCK = 1024
HEAD_COUNT = 8
PARTS = 2
LATENT = 512
LOG2E = 1.4426950408889634


def shift(value, phase, distance):
    pairs = []
    for place in np.ndindex(*SIZES):
        target = list(place)
        axis = ORDERS[place[1]][phase]
        target[axis] = (target[axis] + distance) % RING
        pairs.append((int(np.ravel_multi_index(place, SIZES)), int(np.ravel_multi_index(target, SIZES))))
    return lax.ppermute(value, AXES, pairs)


def widened(value):
    return value.astype(jnp.float32)


def narrowed(value):
    return value.astype(jnp.bfloat16)


def added(*values):
    return sum(widened(value) for value in values)


def with_other_core(value):
    return lax.ppermute(value, "core", [(0, 1), (1, 0)])


def expert_kernel(*refs, sources, outputs):
    row_hbm = refs[:sources]
    matrices = refs[sources : sources + 2]
    out_refs = refs[sources + 2 : sources + 2 + outputs]
    rows_ref, hidden_ref, row_sem = refs[sources + 2 + outputs :]
    width = out_refs[0].shape[1]
    span = rows_ref.shape[0] // sources
    row_copies = [
        pltpu.make_async_copy(source, rows_ref.at[pl.ds(i * span, span)], row_sem.at[i])
        for i, source in enumerate(row_hbm)
    ]
    for copy in row_copies:
        copy.start()
    for copy in row_copies:
        copy.wait()
    extra = rows_ref[:, width : width + PACK].astype(jnp.float32)
    lane = lax.broadcasted_iota(jnp.int32, extra.shape, 1)
    expert = lax.axis_index("x") * RING + lax.axis_index("y")
    pick = (lane % EXPERTS == expert) & (lane < 2 * EXPERTS)
    coefficient = jnp.sum(jnp.where(pick, extra, 0.0), axis=1, keepdims=True)
    for i, matrix in enumerate(matrices):
        sums = sum(
            jnp.dot(rows_ref[:, k : k + 2 * DEPTH], matrix[k : k + 2 * DEPTH, :], preferred_element_type=jnp.float32)
            for k in range(0, width, 2 * DEPTH)
        )
        gate, up = sums[:, :UNITS], sums[:, UNITS:]
        hidden = gate / (1.0 + jnp.exp(-gate)) * up * coefficient
        hidden_ref[i] = jnp.where(coefficient > 0, hidden, 0.0).astype(jnp.bfloat16)
    for block in range(width // DEPTH):
        part, place = slice(block * DEPTH, (block + 1) * DEPTH), slice(width + block * UNITS, width + (block + 1) * UNITS)
        result = jnp.dot(hidden_ref[0], matrices[0][place, :], preferred_element_type=jnp.float32)
        result += jnp.dot(hidden_ref[1], matrices[1][place, :], preferred_element_type=jnp.float32)
        result = result.astype(jnp.bfloat16)
        for i, out_ref in enumerate(out_refs):
            out_ref[:, part] = result[i * HALF : (i + 1) * HALF]


def expert_terms(pieces, weights):
    width = pieces[0].shape[1] - PACK
    rows = sum(piece.shape[0] for piece in pieces)
    outputs = rows // HALF
    weights = [pltpu.with_memory_space_constraint(matrix, pltpu.VMEM) for matrix in weights]
    return pl.pallas_call(
        functools.partial(expert_kernel, sources=len(pieces), outputs=outputs),
        in_specs=[pl.BlockSpec(memory_space=pl.ANY)] * len(pieces)
        + [pl.BlockSpec(memory_space=pltpu.VMEM)] * 2,
        out_specs=[pl.BlockSpec(memory_space=pltpu.VMEM)] * outputs,
        out_shape=[jax.ShapeDtypeStruct((HALF, width), jnp.bfloat16)] * outputs,
        scratch_shapes=[
            pltpu.VMEM((rows, width + PACK), jnp.bfloat16),
            pltpu.VMEM((2, rows, UNITS), jnp.bfloat16),
            pltpu.SemaphoreType.DMA((len(pieces),)),
        ],
        compiler_params=pltpu.CompilerParams(vmem_limit_bytes=EXPERT_VMEM),
        cost_estimate=pl.CostEstimate(
            flops=6 * rows * width * UNITS * 2, bytes_accessed=4 * rows * width, transcendentals=0
        ),
        name="expert",
    )(*pieces, *weights)


def join_kernel(gate_hbm, up_hbm, down_hbm, out_ref, sem):
    width = gate_hbm.shape[0]
    copies = [
        pltpu.make_async_copy(source, out_ref.at[pl.ds(0, width), pl.ds(i * UNITS, UNITS)], sem.at[i])
        for i, source in enumerate((gate_hbm, up_hbm))
    ]
    for i in range(width // DEPTH):
        part = out_ref.at[pl.ds(width + i * UNITS, UNITS)]
        copies.append(pltpu.make_async_copy(down_hbm.at[:, pl.ds(i * DEPTH, DEPTH)], part, sem.at[2 + i]))
    for copy in copies:
        copy.start()
    for copy in copies:
        copy.wait()


def joined(gate, up, down):
    width = gate.shape[0]
    blocks = width // DEPTH
    matrices = [pltpu.with_memory_space_constraint(matrix, pltpu.HBM) for matrix in (gate, up, down)]
    return pl.pallas_call(
        join_kernel,
        in_specs=[pl.BlockSpec(memory_space=pl.ANY)] * 3,
        out_specs=pl.BlockSpec(memory_space=pltpu.VMEM),
        out_shape=pltpu.VMEM((width + blocks * UNITS, DEPTH), jnp.bfloat16),
        scratch_shapes=[pltpu.SemaphoreType.DMA((2 + blocks,))],
        compiler_params=pltpu.CompilerParams(vmem_limit_bytes=KERNEL_VMEM),
        cost_estimate=pl.CostEstimate(flops=0, bytes_accessed=12 * width * UNITS, transcendentals=0),
        name="join",
    )(*matrices)


def pack_kernel(tokens_ref, routes_ref, scores_ref, out_ref):
    rows, width = tokens_ref.shape
    out_ref[:, :width] = tokens_ref[...]
    scores = scores_ref[...]
    weights = scores / jnp.sum(scores, axis=1, keepdims=True) * ROUTE_SCALE
    lane = lax.broadcasted_iota(jnp.int32, (rows, PACK), 1)
    dense = jnp.zeros((rows, PACK), jnp.float32)
    for choice in range(scores.shape[1]):
        named = routes_ref[:, choice : choice + 1] == lane % EXPERTS
        dense += jnp.where(named, weights[:, choice : choice + 1], 0.0)
    high = dense.astype(jnp.bfloat16).astype(jnp.float32)
    extra = jnp.where(lane < EXPERTS, high, jnp.where(lane < 2 * EXPERTS, dense - high, 0.0))
    out_ref[:, width:] = extra.astype(jnp.bfloat16)


def packed_rows(tokens, routes, gate_scores):
    rows, width = tokens.shape
    return pl.pallas_call(
        pack_kernel,
        out_shape=jax.ShapeDtypeStruct((rows, width + PACK), jnp.bfloat16),
        compiler_params=pltpu.CompilerParams(vmem_limit_bytes=KERNEL_VMEM),
        name="pack",
    )(*(pltpu.with_memory_space_constraint(value, pltpu.HBM) for value in (tokens, routes, gate_scores)))


def attention_kernel(
    sequence, length_ref, nope_ref, rope_ref, key_up_ref, value_up_ref, latent_ref, rope_key_ref,
    new_latent_ref, new_rope_ref, out_ref, query_ref, query_rope_ref, top_ref, sum_ref, total_ref,
):
    step = pl.program_id(0)
    length = length_ref[0]
    scale = (NOPE + ROPE) ** (-0.5) * LOG2E
    contract_last = (((1,), (1,)), ((), ()))

    def absorb(keys, rope_keys, values, bias):
        rows = HEAD_COUNT * NEW // PARTS
        parts = [slice(part * rows, (part + 1) * rows) for part in range(PARTS)]
        biases = [bias if bias.shape[0] == 1 else bias[part] for part in parts]
        scores = []
        for part, added_bias in zip(parts, biases):
            score = lax.dot_general(query_ref[part, :], keys, contract_last, preferred_element_type=jnp.float32)
            score += jnp.dot(query_rope_ref[part, :], rope_keys, preferred_element_type=jnp.float32)
            scores.append(score * scale + added_bias)
        for part, score in zip(parts, scores):
            old_top = top_ref[part, :]
            top = jnp.maximum(old_top, jnp.max(score, axis=1, keepdims=True))
            shrink = jnp.exp2(old_top - top)
            probs = jnp.exp2(score - top)
            top_ref[part, :] = top
            sum_ref[part, :] = sum_ref[part, :] * shrink + jnp.sum(probs, axis=1, keepdims=True)
            total_ref[part, :] = total_ref[part, :] * shrink + jnp.dot(
                probs.astype(jnp.bfloat16), values, preferred_element_type=jnp.float32
            )

    @pl.when(step == 0)
    def _():
        for head in range(HEAD_COUNT):
            query_ref[head * NEW : (head + 1) * NEW, :] = jnp.dot(
                nope_ref[:, head * NOPE : (head + 1) * NOPE], key_up_ref[head], preferred_element_type=jnp.float32
            ).astype(jnp.bfloat16)
            query_rope_ref[head * NEW : (head + 1) * NEW, :] = rope_ref[:, head * ROPE : (head + 1) * ROPE]
        top_ref[...] = jnp.full_like(top_ref, NEG_BIG)
        sum_ref[...] = jnp.zeros_like(sum_ref)
        total_ref[...] = jnp.zeros_like(total_ref)
        position = lax.broadcasted_iota(jnp.int32, (HEAD_COUNT * NEW, NEW), 0) % NEW
        fresh = lax.broadcasted_iota(jnp.int32, (HEAD_COUNT * NEW, NEW), 1)
        bias = jnp.where(fresh <= position, 0.0, NEG_BIG)
        absorb(new_latent_ref[...], new_rope_ref[:, sequence * NEW : (sequence + 1) * NEW], new_latent_ref[...], bias)

    @pl.when(step * KEY_BLOCK < length)
    def _():
        slot = step * KEY_BLOCK + lax.broadcasted_iota(jnp.int32, (1, KEY_BLOCK), 1)
        bias = jnp.where(slot < length, 0.0, NEG_BIG)
        absorb(latent_ref[...], rope_key_ref[...], latent_ref[...], bias)

    @pl.when(step == pl.num_programs(0) - 1)
    def _():
        latent_out = (total_ref[...] / sum_ref[...]).astype(jnp.bfloat16)
        for head in range(HEAD_COUNT):
            out_ref[:, head * NOPE : (head + 1) * NOPE] = jnp.dot(
                latent_out[head * NEW : (head + 1) * NEW], value_up_ref[head], preferred_element_type=jnp.float32
            ).astype(jnp.bfloat16)


def attend(sequence, length, nope, rope, key_up, value_up, latent_cache, rope_cache, new_latent, new_rope):
    rows = HEAD_COUNT * NEW

    def whole(*shape):
        return pl.BlockSpec(shape, lambda step, length: (0,) * len(shape))

    def live(step, length):
        return (sequence, jnp.minimum(step, (length[0] + KEY_BLOCK - 1) // KEY_BLOCK - 1), 0)

    def live_last(step, length):
        sequence_place, block, column = live(step, length)
        return (sequence_place, column, block)

    def own(*shape):
        return pl.BlockSpec(shape, lambda step, length: (sequence,) + (0,) * (len(shape) - 1))

    return pl.pallas_call(
        functools.partial(attention_kernel, sequence),
        grid_spec=pltpu.PrefetchScalarGridSpec(
            num_scalar_prefetch=1,
            grid=(CACHE // KEY_BLOCK,),
            in_specs=[
                own(NEW, HEAD_COUNT * NOPE),
                own(NEW, HEAD_COUNT * ROPE),
                whole(HEAD_COUNT, NOPE, LATENT),
                whole(HEAD_COUNT, LATENT, NOPE),
                pl.BlockSpec((None, KEY_BLOCK, LATENT), live),
                pl.BlockSpec((None, ROPE, KEY_BLOCK), live_last),
                own(NEW, LATENT),
                pl.BlockSpec((ROPE, 2 * NEW), lambda step, length: (0, 0)),
            ],
            out_specs=whole(NEW, HEAD_COUNT * NOPE),
            scratch_shapes=[
                pltpu.VMEM((rows, LATENT), jnp.bfloat16),
                pltpu.VMEM((rows, ROPE), jnp.bfloat16),
                pltpu.VMEM((rows, 1), jnp.float32),
                pltpu.VMEM((rows, 1), jnp.float32),
                pltpu.VMEM((rows, LATENT), jnp.float32),
            ],
        ),
        out_shape=jax.ShapeDtypeStruct((NEW, HEAD_COUNT * NOPE), jnp.bfloat16),
        compiler_params=pltpu.CompilerParams(vmem_limit_bytes=KERNEL_VMEM),
        cost_estimate=pl.CostEstimate(flops=6_000_000_000, bytes_accessed=8_000_000, transcendentals=2_100_000),
        name="attend",
    )(length, nope, rope, key_up, value_up, latent_cache, rope_cache, new_latent, new_rope)


def body(
    tokens,
    routes,
    gate_scores,
    gate_weight,
    up_weight,
    down_weight,
    query_nope,
    query_rope,
    key_up,
    value_up,
    latent_cache,
    rope_cache,
    new_latent,
    new_rope,
    lengths,
):
    packed = packed_rows(tokens, routes, gate_scores)
    gathered = [packed] + [shift(packed, 0, -distance) for distance in (1, 2, 3)]
    packed, gate_weight, up_weight, down_weight = lax.optimization_barrier(
        (packed, gate_weight, up_weight, down_weight)
    )
    own_weights = joined(gate_weight[0], up_weight[0], down_weight[0])
    small = jnp.concatenate(gathered, axis=0)
    small, own_weights = lax.optimization_barrier((small, own_weights))
    weights = (own_weights, with_other_core(own_weights))
    rope_keys, new_rope_keys = jnp.swapaxes(rope_cache, 1, 2), new_rope.T
    latent_cache = pltpu.with_memory_space_constraint(latent_cache, pltpu.HBM)

    def attention(sequence, length):
        return attend(
            sequence, length, query_nope, query_rope, key_up, value_up, latent_cache, rope_keys, new_latent, new_rope_keys
        )

    above, below = shift(small, 1, -1), shift(small, 1, 1)
    own_low = jnp.concatenate([small, above], axis=0)
    below_low, above_low = shift(own_low, 2, 1), shift(own_low, 2, -1)
    own_high = jnp.concatenate([shift(below, 1, 1), below], axis=0)
    below_high, above_high = shift(own_high, 2, 1), shift(own_high, 2, -1)
    own_high, lengths = lax.optimization_barrier((own_high, lengths))
    first_attention = attention(0, lengths[:1])
    own_low, own_high, below_low, above_low, first_attention = lax.optimization_barrier(
        (own_low, own_high, below_low, above_low, first_attention)
    )
    own_terms = expert_terms([own_low, own_high], weights)
    below_low, above_high, own_terms = lax.optimization_barrier((below_low, above_high, own_terms))
    far_low, far_high = shift(below_low, 2, 1), shift(above_high, 2, -1)
    above_low, above_high, below_low, below_high = expert_terms(
        [above_low, above_high, below_low, below_high], weights
    )
    near_high, near_low = shift(above_high, 2, 1), shift(below_low, 2, -1)
    far_low, far_high, above_high, below_low = lax.optimization_barrier((far_low, far_high, above_high, below_low))
    far_terms = expert_terms([far_low, far_high], weights)
    from_below, from_above = shift(far_terms[0], 2, 1), shift(far_terms[1], 2, -1)
    far_terms, near_high, near_low, lengths = lax.optimization_barrier((far_terms, near_high, near_low, lengths))
    second_attention = attention(1, lengths[1:])
    from_below, from_above, second_attention = lax.optimization_barrier((from_below, from_above, second_attention))
    from_below = shift(narrowed(added(above_low, from_below)), 2, 1)
    from_above = shift(narrowed(added(below_high, from_above)), 2, -1)
    low = added(own_terms[0], near_low, from_below)
    high = added(own_terms[1], near_high, from_above)

    size = HALF // 2
    half = size // 2
    above, far, below = low[size:], high[:size], high[size:]
    up_first = narrowed(jnp.concatenate([far[:half], above[half:]], axis=0))
    down_first = narrowed(jnp.concatenate([far[half:], below[:half]], axis=0))
    from_below, from_above = shift(up_first, 1, 1), shift(down_first, 1, -1)
    up_second = narrowed(added(above[:half], from_below[:half]))
    down_second = narrowed(added(below[half:], from_above[:half]))
    up_second, down_second = lax.optimization_barrier((up_second, down_second))
    up_second, down_second = shift(up_second, 1, 1), shift(down_second, 1, -1)
    total = low[:size] + jnp.concatenate(
        [added(up_second, from_above[half:]), added(down_second, from_below[half:])], axis=0
    )

    total = narrowed(total)
    rows = tokens.shape[0]
    arrived = [shift(total[distance * rows : (distance + 1) * rows], 0, distance) for distance in (1, 2, 3)]
    routed_out = narrowed(added(total[:rows], *arrived))
    return (routed_out, jnp.concatenate([first_attention, second_attention], axis=0))


def solution(mesh):
    cube = Mesh(mesh.devices.reshape(4, 2, 4, 4), ("z", "core", "x", "y"))
    node, local = ("z", "core"), ("x", "y")
    every = node + local
    in_specs = (
        P(every, None),
        P(every, None),
        P(every, None),
        P(local, None, node),
        P(local, None, node),
        P(local, node, None),
        P(node, local),
        P(node, local),
        P(local, None, None),
        P(local, None, None),
        P(node, None, None),
        P(node, None, None),
        P(node, None),
        P(node, None),
        P(node),
    )
    out_specs = (P(every, None), P(node, local))
    return jax.shard_map(body, mesh=cube, in_specs=in_specs, out_specs=out_specs, check_vma=False)
```

```python
import functools

import jax
import jax.numpy as jnp
import numpy as np
from jax import lax
from jax.experimental import pallas as pl
from jax.experimental.pallas import tpu as pltpu
from jax.sharding import Mesh, PartitionSpec as P

NOPE = 128
ROPE = 64
NEW = 64
CACHE = 4096
EXPERTS = 16
ROUTE_SCALE = 2.5
NEG_BIG = -1e30
AXES = ("z", "core", "x", "y")
SIZES = (4, 2, 4, 4)
RING = 4
ORDERS = ((0, 3, 2), (2, 0, 3))
KERNEL_VMEM = 12 * 1024 * 1024
EXPERT_VMEM = 10 * 1024 * 1024
PACK = 128
DEPTH = 512
UNITS = 256
HALF = 64
KEY_BLOCK = 1024
HEAD_COUNT = 8
PARTS = 2
LATENT = 512
LOG2E = 1.4426950408889634


def shift(value, phase, distance):
    pairs = []
    for place in np.ndindex(*SIZES):
        target = list(place)
        axis = ORDERS[place[1]][phase]
        target[axis] = (target[axis] + distance) % RING
        pairs.append((int(np.ravel_multi_index(place, SIZES)), int(np.ravel_multi_index(target, SIZES))))
    return lax.ppermute(value, AXES, pairs)


def ring_exchange(value):
    groups = []
    for core in range(2):
        axis = ORDERS[core][0]
        for place in np.ndindex(*(1 if i in (1, axis) else size for i, size in enumerate(SIZES))):
            members = [[core if i == 1 else step if i == axis else p for i, p in enumerate(place)] for step in range(RING)]
            groups.append([int(np.ravel_multi_index(member, SIZES)) for member in members])
    return lax.all_to_all(value, AXES, split_axis=0, concat_axis=0, axis_index_groups=groups, tiled=True)


def widened(value):
    return value.astype(jnp.float32)


def narrowed(value):
    return value.astype(jnp.bfloat16)


def added(*values):
    return sum(widened(value) for value in values)


def with_other_core(value):
    return lax.ppermute(value, "core", [(0, 1), (1, 0)])


def expert_kernel(*refs, sources, outputs):
    row_hbm = refs[:sources]
    matrices = refs[sources : sources + 2]
    out_refs = refs[sources + 2 : sources + 2 + outputs]
    rows_ref, hidden_ref, row_sem = refs[sources + 2 + outputs :]
    width = out_refs[0].shape[1]
    span = rows_ref.shape[0] // sources
    row_copies = [
        pltpu.make_async_copy(source, rows_ref.at[pl.ds(i * span, span)], row_sem.at[i])
        for i, source in enumerate(row_hbm)
    ]
    for copy in row_copies:
        copy.start()
    for copy in row_copies:
        copy.wait()
    extra = rows_ref[:, width : width + PACK].astype(jnp.float32)
    lane = lax.broadcasted_iota(jnp.int32, extra.shape, 1)
    expert = lax.axis_index("x") * RING + lax.axis_index("y")
    pick = (lane % EXPERTS == expert) & (lane < 2 * EXPERTS)
    coefficient = jnp.sum(jnp.where(pick, extra, 0.0), axis=1, keepdims=True)
    for i, matrix in enumerate(matrices):
        sums = sum(
            jnp.dot(rows_ref[:, k : k + 2 * DEPTH], matrix[k : k + 2 * DEPTH, :], preferred_element_type=jnp.float32)
            for k in range(0, width, 2 * DEPTH)
        )
        gate, up = sums[:, :UNITS], sums[:, UNITS:]
        hidden = gate / (1.0 + jnp.exp(-gate)) * up * coefficient
        hidden_ref[i] = jnp.where(coefficient > 0, hidden, 0.0).astype(jnp.bfloat16)
    for block in range(width // DEPTH):
        part, place = slice(block * DEPTH, (block + 1) * DEPTH), slice(width + block * UNITS, width + (block + 1) * UNITS)
        result = jnp.dot(hidden_ref[0], matrices[0][place, :], preferred_element_type=jnp.float32)
        result += jnp.dot(hidden_ref[1], matrices[1][place, :], preferred_element_type=jnp.float32)
        result = result.astype(jnp.bfloat16)
        for i, out_ref in enumerate(out_refs):
            out_ref[:, part] = result[i * HALF : (i + 1) * HALF]


def expert_terms(pieces, weights):
    width = pieces[0].shape[1] - PACK
    rows = sum(piece.shape[0] for piece in pieces)
    outputs = rows // HALF
    weights = [pltpu.with_memory_space_constraint(matrix, pltpu.VMEM) for matrix in weights]
    return pl.pallas_call(
        functools.partial(expert_kernel, sources=len(pieces), outputs=outputs),
        in_specs=[pl.BlockSpec(memory_space=pl.ANY)] * len(pieces)
        + [pl.BlockSpec(memory_space=pltpu.VMEM)] * 2,
        out_specs=[pl.BlockSpec(memory_space=pltpu.VMEM)] * outputs,
        out_shape=[jax.ShapeDtypeStruct((HALF, width), jnp.bfloat16)] * outputs,
        scratch_shapes=[
            pltpu.VMEM((rows, width + PACK), jnp.bfloat16),
            pltpu.VMEM((2, rows, UNITS), jnp.bfloat16),
            pltpu.SemaphoreType.DMA((len(pieces),)),
        ],
        compiler_params=pltpu.CompilerParams(vmem_limit_bytes=EXPERT_VMEM),
        cost_estimate=pl.CostEstimate(
            flops=6 * rows * width * UNITS * 2, bytes_accessed=4 * rows * width, transcendentals=0
        ),
        name="expert",
    )(*pieces, *weights)


def join_kernel(gate_hbm, up_hbm, down_hbm, out_ref, sem):
    width = gate_hbm.shape[0]
    copies = [
        pltpu.make_async_copy(source, out_ref.at[pl.ds(0, width), pl.ds(i * UNITS, UNITS)], sem.at[i])
        for i, source in enumerate((gate_hbm, up_hbm))
    ]
    for i in range(width // DEPTH):
        part = out_ref.at[pl.ds(width + i * UNITS, UNITS)]
        copies.append(pltpu.make_async_copy(down_hbm.at[:, pl.ds(i * DEPTH, DEPTH)], part, sem.at[2 + i]))
    for copy in copies:
        copy.start()
    for copy in copies:
        copy.wait()


def joined(gate, up, down):
    width = gate.shape[0]
    blocks = width // DEPTH
    matrices = [pltpu.with_memory_space_constraint(matrix, pltpu.HBM) for matrix in (gate, up, down)]
    return pl.pallas_call(
        join_kernel,
        in_specs=[pl.BlockSpec(memory_space=pl.ANY)] * 3,
        out_specs=pl.BlockSpec(memory_space=pltpu.VMEM),
        out_shape=pltpu.VMEM((width + blocks * UNITS, DEPTH), jnp.bfloat16),
        scratch_shapes=[pltpu.SemaphoreType.DMA((2 + blocks,))],
        compiler_params=pltpu.CompilerParams(vmem_limit_bytes=KERNEL_VMEM),
        cost_estimate=pl.CostEstimate(flops=0, bytes_accessed=12 * width * UNITS, transcendentals=0),
        name="join",
    )(*matrices)


def placed_sum_kernel(own_ref, up_ref, down_ref, above_ref, below_ref, out_ref):
    first = jnp.where(lax.axis_index("core") == 0, lax.axis_index("z"), lax.axis_index("x"))
    low = added(up_ref[...], above_ref[...])
    high = added(down_ref[...], below_ref[...])
    total = own_ref[...] + jnp.concatenate([low, high], axis=0)
    rows = total.shape[0] // RING
    total = narrowed(total)
    for distance in range(RING):
        place = lax.rem(first + distance, RING)
        out_ref[pl.ds(pl.multiple_of(place * rows, rows), rows), :] = total[distance * rows : (distance + 1) * rows]


def placed_sum(own, up, down, above, below):
    return pl.pallas_call(
        placed_sum_kernel,
        out_shape=jax.ShapeDtypeStruct(own.shape, jnp.bfloat16),
        compiler_params=pltpu.CompilerParams(vmem_limit_bytes=KERNEL_VMEM),
        name="placed_sum",
    )(own, up, down, above, below)


def pack_kernel(tokens_ref, routes_ref, scores_ref, out_ref):
    rows, width = tokens_ref.shape
    out_ref[:, :width] = tokens_ref[...]
    scores = scores_ref[...]
    weights = scores / jnp.sum(scores, axis=1, keepdims=True) * ROUTE_SCALE
    lane = lax.broadcasted_iota(jnp.int32, (rows, PACK), 1)
    dense = jnp.zeros((rows, PACK), jnp.float32)
    for choice in range(scores.shape[1]):
        named = routes_ref[:, choice : choice + 1] == lane % EXPERTS
        dense += jnp.where(named, weights[:, choice : choice + 1], 0.0)
    high = dense.astype(jnp.bfloat16).astype(jnp.float32)
    extra = jnp.where(lane < EXPERTS, high, jnp.where(lane < 2 * EXPERTS, dense - high, 0.0))
    out_ref[:, width:] = extra.astype(jnp.bfloat16)


def packed_rows(tokens, routes, gate_scores):
    rows, width = tokens.shape
    return pl.pallas_call(
        pack_kernel,
        out_shape=jax.ShapeDtypeStruct((rows, width + PACK), jnp.bfloat16),
        compiler_params=pltpu.CompilerParams(vmem_limit_bytes=KERNEL_VMEM),
        name="pack",
    )(*(pltpu.with_memory_space_constraint(value, pltpu.HBM) for value in (tokens, routes, gate_scores)))


def attention_kernel(
    sequence, length_ref, nope_ref, rope_ref, key_up_ref, value_up_ref, latent_ref, rope_key_ref,
    new_latent_ref, new_rope_ref, out_ref, query_ref, query_rope_ref, top_ref, sum_ref, total_ref,
):
    step = pl.program_id(0)
    length = length_ref[0]
    scale = (NOPE + ROPE) ** (-0.5) * LOG2E
    contract_last = (((1,), (1,)), ((), ()))

    def absorb(keys, rope_keys, values, bias):
        rows = HEAD_COUNT * NEW // PARTS
        parts = [slice(part * rows, (part + 1) * rows) for part in range(PARTS)]
        biases = [bias if bias.shape[0] == 1 else bias[part] for part in parts]
        scores = []
        for part, added_bias in zip(parts, biases):
            score = lax.dot_general(query_ref[part, :], keys, contract_last, preferred_element_type=jnp.float32)
            score += jnp.dot(query_rope_ref[part, :], rope_keys, preferred_element_type=jnp.float32)
            scores.append(score * scale + added_bias)
        for part, score in zip(parts, scores):
            old_top = top_ref[part, :]
            top = jnp.maximum(old_top, jnp.max(score, axis=1, keepdims=True))
            shrink = jnp.exp2(old_top - top)
            probs = jnp.exp2(score - top)
            top_ref[part, :] = top
            sum_ref[part, :] = sum_ref[part, :] * shrink + jnp.sum(probs, axis=1, keepdims=True)
            total_ref[part, :] = total_ref[part, :] * shrink + jnp.dot(
                probs.astype(jnp.bfloat16), values, preferred_element_type=jnp.float32
            )

    @pl.when(step == 0)
    def _():
        for head in range(HEAD_COUNT):
            query_ref[head * NEW : (head + 1) * NEW, :] = jnp.dot(
                nope_ref[:, head * NOPE : (head + 1) * NOPE], key_up_ref[head], preferred_element_type=jnp.float32
            ).astype(jnp.bfloat16)
            query_rope_ref[head * NEW : (head + 1) * NEW, :] = rope_ref[:, head * ROPE : (head + 1) * ROPE]
        top_ref[...] = jnp.full_like(top_ref, NEG_BIG)
        sum_ref[...] = jnp.zeros_like(sum_ref)
        total_ref[...] = jnp.zeros_like(total_ref)
        position = lax.broadcasted_iota(jnp.int32, (HEAD_COUNT * NEW, NEW), 0) % NEW
        fresh = lax.broadcasted_iota(jnp.int32, (HEAD_COUNT * NEW, NEW), 1)
        bias = jnp.where(fresh <= position, 0.0, NEG_BIG)
        absorb(new_latent_ref[...], new_rope_ref[:, sequence * NEW : (sequence + 1) * NEW], new_latent_ref[...], bias)

    @pl.when(step * KEY_BLOCK < length)
    def _():
        slot = step * KEY_BLOCK + lax.broadcasted_iota(jnp.int32, (1, KEY_BLOCK), 1)
        bias = jnp.where(slot < length, 0.0, NEG_BIG)
        absorb(latent_ref[...], rope_key_ref[...], latent_ref[...], bias)

    @pl.when(step == pl.num_programs(0) - 1)
    def _():
        latent_out = (total_ref[...] / sum_ref[...]).astype(jnp.bfloat16)
        for head in range(HEAD_COUNT):
            out_ref[:, head * NOPE : (head + 1) * NOPE] = jnp.dot(
                latent_out[head * NEW : (head + 1) * NEW], value_up_ref[head], preferred_element_type=jnp.float32
            ).astype(jnp.bfloat16)


def attend(sequence, length, nope, rope, key_up, value_up, latent_cache, rope_cache, new_latent, new_rope):
    rows = HEAD_COUNT * NEW

    def whole(*shape):
        return pl.BlockSpec(shape, lambda step, length: (0,) * len(shape))

    def live(step, length):
        return (sequence, jnp.minimum(step, (length[0] + KEY_BLOCK - 1) // KEY_BLOCK - 1), 0)

    def live_last(step, length):
        sequence_place, block, column = live(step, length)
        return (sequence_place, column, block)

    def own(*shape):
        return pl.BlockSpec(shape, lambda step, length: (sequence,) + (0,) * (len(shape) - 1))

    return pl.pallas_call(
        functools.partial(attention_kernel, sequence),
        grid_spec=pltpu.PrefetchScalarGridSpec(
            num_scalar_prefetch=1,
            grid=(CACHE // KEY_BLOCK,),
            in_specs=[
                own(NEW, HEAD_COUNT * NOPE),
                own(NEW, HEAD_COUNT * ROPE),
                whole(HEAD_COUNT, NOPE, LATENT),
                whole(HEAD_COUNT, LATENT, NOPE),
                pl.BlockSpec((None, KEY_BLOCK, LATENT), live),
                pl.BlockSpec((None, ROPE, KEY_BLOCK), live_last),
                own(NEW, LATENT),
                pl.BlockSpec((ROPE, 2 * NEW), lambda step, length: (0, 0)),
            ],
            out_specs=whole(NEW, HEAD_COUNT * NOPE),
            scratch_shapes=[
                pltpu.VMEM((rows, LATENT), jnp.bfloat16),
                pltpu.VMEM((rows, ROPE), jnp.bfloat16),
                pltpu.VMEM((rows, 1), jnp.float32),
                pltpu.VMEM((rows, 1), jnp.float32),
                pltpu.VMEM((rows, LATENT), jnp.float32),
            ],
        ),
        out_shape=jax.ShapeDtypeStruct((NEW, HEAD_COUNT * NOPE), jnp.bfloat16),
        compiler_params=pltpu.CompilerParams(vmem_limit_bytes=KERNEL_VMEM),
        cost_estimate=pl.CostEstimate(flops=6_000_000_000, bytes_accessed=8_000_000, transcendentals=2_100_000),
        name="attend",
    )(length, nope, rope, key_up, value_up, latent_cache, rope_cache, new_latent, new_rope)


def body(
    tokens,
    routes,
    gate_scores,
    gate_weight,
    up_weight,
    down_weight,
    query_nope,
    query_rope,
    key_up,
    value_up,
    latent_cache,
    rope_cache,
    new_latent,
    new_rope,
    lengths,
):
    packed = packed_rows(tokens, routes, gate_scores)
    gathered = [packed] + [shift(packed, 0, -distance) for distance in (1, 2, 3)]
    packed, gate_weight, up_weight, down_weight = lax.optimization_barrier(
        (packed, gate_weight, up_weight, down_weight)
    )
    own_weights = joined(gate_weight[0], up_weight[0], down_weight[0])
    small = jnp.concatenate(gathered, axis=0)
    small, own_weights = lax.optimization_barrier((small, own_weights))
    weights = (own_weights, with_other_core(own_weights))
    rope_keys, new_rope_keys = jnp.swapaxes(rope_cache, 1, 2), new_rope.T
    latent_cache = pltpu.with_memory_space_constraint(latent_cache, pltpu.HBM)

    def attention(sequence, length):
        return attend(
            sequence, length, query_nope, query_rope, key_up, value_up, latent_cache, rope_keys, new_latent, new_rope_keys
        )

    above, below = shift(small, 1, -1), shift(small, 1, 1)
    half = small.shape[0] // 2
    own_low = jnp.concatenate([small, above], axis=0)
    below_low, above_low = shift(own_low, 2, 1), shift(own_low, 2, -1)
    far_low, far_high = lax.optimization_barrier((below[:half], above[half:]))
    far_low, far_high = shift(far_low, 1, 1), shift(far_high, 1, -1)
    own_high = jnp.concatenate([far_low, far_high, below], axis=0)
    below_high, above_high = shift(own_high, 2, 1), shift(own_high, 2, -1)
    own_high, lengths = lax.optimization_barrier((own_high, lengths))
    first_attention = attention(0, lengths[:1])
    own_low, own_high, below_low, above_low, first_attention = lax.optimization_barrier(
        (own_low, own_high, below_low, above_low, first_attention)
    )
    own_terms = expert_terms([own_low, own_high], weights)
    below_low, above_high, own_terms = lax.optimization_barrier((below_low, above_high, own_terms))
    far_low, far_high = shift(below_low, 2, 1), shift(above_high, 2, -1)
    above_low, above_high, below_low, below_high = expert_terms(
        [above_low, above_high, below_low, below_high], weights
    )
    near_high, near_low = shift(above_high, 2, 1), shift(below_low, 2, -1)
    far_low, far_high, above_high, below_low = lax.optimization_barrier((far_low, far_high, above_high, below_low))
    far_terms = expert_terms([far_low, far_high], weights)
    from_below, from_above = shift(far_terms[0], 2, 1), shift(far_terms[1], 2, -1)
    far_terms, near_high, near_low, lengths = lax.optimization_barrier((far_terms, near_high, near_low, lengths))
    second_attention = attention(1, lengths[1:])
    from_below, from_above, second_attention = lax.optimization_barrier((from_below, from_above, second_attention))
    from_below = shift(narrowed(added(above_low, from_below)), 2, 1)
    from_above = shift(narrowed(added(below_high, from_above)), 2, -1)
    low = added(own_terms[0], near_low, from_below)
    high = added(own_terms[1], near_high, from_above)

    size = HALF // 2
    half = size // 2
    above, far, below = low[size:], high[:size], high[size:]
    up_first = narrowed(jnp.concatenate([far[:half], above[half:]], axis=0))
    down_first = narrowed(jnp.concatenate([far[half:], below[:half]], axis=0))
    from_below, from_above = shift(up_first, 1, 1), shift(down_first, 1, -1)
    up_second = narrowed(added(above[:half], from_below[:half]))
    down_second = narrowed(added(below[half:], from_above[:half]))
    up_second, down_second = lax.optimization_barrier((up_second, down_second))
    up_second, down_second = shift(up_second, 1, 1), shift(down_second, 1, -1)
    total = placed_sum(low[:size], up_second, down_second, from_above[half:], from_below[half:])
    arrived = ring_exchange(total).reshape(RING, -1, total.shape[1])
    routed_out = narrowed(jnp.sum(widened(arrived), axis=0))
    return (routed_out, jnp.concatenate([first_attention, second_attention], axis=0))


def solution(mesh):
    cube = Mesh(mesh.devices.reshape(4, 2, 4, 4), ("z", "core", "x", "y"))
    node, local = ("z", "core"), ("x", "y")
    every = node + local
    in_specs = (
        P(every, None),
        P(every, None),
        P(every, None),
        P(local, None, node),
        P(local, None, node),
        P(local, node, None),
        P(node, local),
        P(node, local),
        P(local, None, None),
        P(local, None, None),
        P(node, None, None),
        P(node, None, None),
        P(node, None),
        P(node, None),
        P(node),
    )
    out_specs = (P(every, None), P(node, local))
    return jax.shard_map(body, mesh=cube, in_specs=in_specs, out_specs=out_specs, check_vma=False)
```

```python
import functools

import jax
import jax.numpy as jnp
import numpy as np
from jax import lax
from jax.experimental import pallas as pl
from jax.experimental.pallas import tpu as pltpu
from jax.sharding import Mesh, PartitionSpec as P

NOPE = 128
ROPE = 64
NEW = 64
CACHE = 4096
EXPERTS = 16
ROUTE_SCALE = 2.5
NEG_BIG = -1e30
AXES = ("z", "core", "x", "y")
SIZES = (4, 2, 4, 4)
RING = 4
ORDERS = ((0, 3, 2), (2, 0, 3))
KERNEL_VMEM = 12 * 1024 * 1024
EXPERT_VMEM = 10 * 1024 * 1024
PACK = 128
DEPTH = 512
UNITS = 256
HALF = 64
KEY_BLOCK = 1024
HEAD_COUNT = 8
PARTS = 2
LATENT = 512
LOG2E = 1.4426950408889634


def shift(value, phase, distance):
    pairs = []
    for place in np.ndindex(*SIZES):
        target = list(place)
        axis = ORDERS[place[1]][phase]
        target[axis] = (target[axis] + distance) % RING
        pairs.append((int(np.ravel_multi_index(place, SIZES)), int(np.ravel_multi_index(target, SIZES))))
    return lax.ppermute(value, AXES, pairs)


def widened(value):
    return value.astype(jnp.float32)


def narrowed(value):
    return value.astype(jnp.bfloat16)


def added(*values):
    return sum(widened(value) for value in values)


def with_other_core(value):
    return lax.ppermute(value, "core", [(0, 1), (1, 0)])


def expert_kernel(*refs, sources, outputs):
    row_hbm = refs[:sources]
    matrices = refs[sources : sources + 2]
    out_refs = refs[sources + 2 : sources + 2 + outputs]
    rows_ref, hidden_ref, row_sem = refs[sources + 2 + outputs :]
    width = out_refs[0].shape[1]
    span = rows_ref.shape[0] // sources
    row_copies = [
        pltpu.make_async_copy(source, rows_ref.at[pl.ds(i * span, span)], row_sem.at[i])
        for i, source in enumerate(row_hbm)
    ]
    for copy in row_copies:
        copy.start()
    for copy in row_copies:
        copy.wait()
    extra = rows_ref[:, width : width + PACK].astype(jnp.float32)
    lane = lax.broadcasted_iota(jnp.int32, extra.shape, 1)
    expert = lax.axis_index("x") * RING + lax.axis_index("y")
    pick = (lane % EXPERTS == expert) & (lane < 2 * EXPERTS)
    coefficient = jnp.sum(jnp.where(pick, extra, 0.0), axis=1, keepdims=True)
    for i, matrix in enumerate(matrices):
        sums = sum(
            jnp.dot(rows_ref[:, k : k + 2 * DEPTH], matrix[k : k + 2 * DEPTH, :], preferred_element_type=jnp.float32)
            for k in range(0, width, 2 * DEPTH)
        )
        gate, up = sums[:, :UNITS], sums[:, UNITS:]
        hidden = gate / (1.0 + jnp.exp(-gate)) * up * coefficient
        hidden_ref[i] = jnp.where(coefficient > 0, hidden, 0.0).astype(jnp.bfloat16)
    for block in range(width // DEPTH):
        part, place = slice(block * DEPTH, (block + 1) * DEPTH), slice(width + block * UNITS, width + (block + 1) * UNITS)
        result = jnp.dot(hidden_ref[0], matrices[0][place, :], preferred_element_type=jnp.float32)
        result += jnp.dot(hidden_ref[1], matrices[1][place, :], preferred_element_type=jnp.float32)
        result = result.astype(jnp.bfloat16)
        for i, out_ref in enumerate(out_refs):
            out_ref[:, part] = result[i * HALF : (i + 1) * HALF]


def expert_terms(pieces, weights):
    width = pieces[0].shape[1] - PACK
    rows = sum(piece.shape[0] for piece in pieces)
    outputs = rows // HALF
    weights = [pltpu.with_memory_space_constraint(matrix, pltpu.VMEM) for matrix in weights]
    return pl.pallas_call(
        functools.partial(expert_kernel, sources=len(pieces), outputs=outputs),
        in_specs=[pl.BlockSpec(memory_space=pl.ANY)] * len(pieces)
        + [pl.BlockSpec(memory_space=pltpu.VMEM)] * 2,
        out_specs=[pl.BlockSpec(memory_space=pltpu.VMEM)] * outputs,
        out_shape=[jax.ShapeDtypeStruct((HALF, width), jnp.bfloat16)] * outputs,
        scratch_shapes=[
            pltpu.VMEM((rows, width + PACK), jnp.bfloat16),
            pltpu.VMEM((2, rows, UNITS), jnp.bfloat16),
            pltpu.SemaphoreType.DMA((len(pieces),)),
        ],
        compiler_params=pltpu.CompilerParams(vmem_limit_bytes=EXPERT_VMEM),
        cost_estimate=pl.CostEstimate(
            flops=6 * rows * width * UNITS * 2, bytes_accessed=4 * rows * width, transcendentals=0
        ),
        name="expert",
    )(*pieces, *weights)


def join_kernel(gate_hbm, up_hbm, down_hbm, out_ref, sem):
    width = gate_hbm.shape[0]
    copies = [
        pltpu.make_async_copy(source, out_ref.at[pl.ds(0, width), pl.ds(i * UNITS, UNITS)], sem.at[i])
        for i, source in enumerate((gate_hbm, up_hbm))
    ]
    for i in range(width // DEPTH):
        part = out_ref.at[pl.ds(width + i * UNITS, UNITS)]
        copies.append(pltpu.make_async_copy(down_hbm.at[:, pl.ds(i * DEPTH, DEPTH)], part, sem.at[2 + i]))
    for copy in copies:
        copy.start()
    for copy in copies:
        copy.wait()


def joined(gate, up, down):
    width = gate.shape[0]
    blocks = width // DEPTH
    matrices = [pltpu.with_memory_space_constraint(matrix, pltpu.HBM) for matrix in (gate, up, down)]
    return pl.pallas_call(
        join_kernel,
        in_specs=[pl.BlockSpec(memory_space=pl.ANY)] * 3,
        out_specs=pl.BlockSpec(memory_space=pltpu.VMEM),
        out_shape=pltpu.VMEM((width + blocks * UNITS, DEPTH), jnp.bfloat16),
        scratch_shapes=[pltpu.SemaphoreType.DMA((2 + blocks,))],
        compiler_params=pltpu.CompilerParams(vmem_limit_bytes=KERNEL_VMEM),
        cost_estimate=pl.CostEstimate(flops=0, bytes_accessed=12 * width * UNITS, transcendentals=0),
        name="join",
    )(*matrices)


def pack_kernel(tokens_ref, routes_ref, scores_ref, out_ref):
    rows, width = tokens_ref.shape
    out_ref[:, :width] = tokens_ref[...]
    scores = scores_ref[...]
    weights = scores / jnp.sum(scores, axis=1, keepdims=True) * ROUTE_SCALE
    lane = lax.broadcasted_iota(jnp.int32, (rows, PACK), 1)
    dense = jnp.zeros((rows, PACK), jnp.float32)
    for choice in range(scores.shape[1]):
        named = routes_ref[:, choice : choice + 1] == lane % EXPERTS
        dense += jnp.where(named, weights[:, choice : choice + 1], 0.0)
    high = dense.astype(jnp.bfloat16).astype(jnp.float32)
    extra = jnp.where(lane < EXPERTS, high, jnp.where(lane < 2 * EXPERTS, dense - high, 0.0))
    out_ref[:, width:] = extra.astype(jnp.bfloat16)


def packed_rows(tokens, routes, gate_scores):
    rows, width = tokens.shape
    return pl.pallas_call(
        pack_kernel,
        out_shape=jax.ShapeDtypeStruct((rows, width + PACK), jnp.bfloat16),
        compiler_params=pltpu.CompilerParams(vmem_limit_bytes=KERNEL_VMEM),
        name="pack",
    )(*(pltpu.with_memory_space_constraint(value, pltpu.HBM) for value in (tokens, routes, gate_scores)))


def attention_kernel(
    sequence, length_ref, nope_ref, rope_ref, key_up_ref, value_up_ref, latent_ref, rope_key_ref,
    new_latent_ref, new_rope_ref, out_ref, query_ref, query_rope_ref, top_ref, sum_ref, total_ref,
):
    step = pl.program_id(0)
    length = length_ref[0]
    scale = (NOPE + ROPE) ** (-0.5) * LOG2E
    contract_last = (((1,), (1,)), ((), ()))

    def absorb(keys, rope_keys, values, bias):
        rows = HEAD_COUNT * NEW // PARTS
        parts = [slice(part * rows, (part + 1) * rows) for part in range(PARTS)]
        biases = [bias if bias.shape[0] == 1 else bias[part] for part in parts]
        scores = []
        for part, added_bias in zip(parts, biases):
            score = lax.dot_general(query_ref[part, :], keys, contract_last, preferred_element_type=jnp.float32)
            score += jnp.dot(query_rope_ref[part, :], rope_keys, preferred_element_type=jnp.float32)
            scores.append(score * scale + added_bias)
        for part, score in zip(parts, scores):
            old_top = top_ref[part, :]
            top = jnp.maximum(old_top, jnp.max(score, axis=1, keepdims=True))
            shrink = jnp.exp2(old_top - top)
            probs = jnp.exp2(score - top)
            top_ref[part, :] = top
            sum_ref[part, :] = sum_ref[part, :] * shrink + jnp.sum(probs, axis=1, keepdims=True)
            total_ref[part, :] = total_ref[part, :] * shrink + jnp.dot(
                probs.astype(jnp.bfloat16), values, preferred_element_type=jnp.float32
            )

    @pl.when(step == 0)
    def _():
        for head in range(HEAD_COUNT):
            query_ref[head * NEW : (head + 1) * NEW, :] = jnp.dot(
                nope_ref[:, head * NOPE : (head + 1) * NOPE], key_up_ref[head], preferred_element_type=jnp.float32
            ).astype(jnp.bfloat16)
            query_rope_ref[head * NEW : (head + 1) * NEW, :] = rope_ref[:, head * ROPE : (head + 1) * ROPE]
        top_ref[...] = jnp.full_like(top_ref, NEG_BIG)
        sum_ref[...] = jnp.zeros_like(sum_ref)
        total_ref[...] = jnp.zeros_like(total_ref)
        position = lax.broadcasted_iota(jnp.int32, (HEAD_COUNT * NEW, NEW), 0) % NEW
        fresh = lax.broadcasted_iota(jnp.int32, (HEAD_COUNT * NEW, NEW), 1)
        bias = jnp.where(fresh <= position, 0.0, NEG_BIG)
        absorb(new_latent_ref[...], new_rope_ref[:, sequence * NEW : (sequence + 1) * NEW], new_latent_ref[...], bias)

    @pl.when(step * KEY_BLOCK < length)
    def _():
        slot = step * KEY_BLOCK + lax.broadcasted_iota(jnp.int32, (1, KEY_BLOCK), 1)
        bias = jnp.where(slot < length, 0.0, NEG_BIG)
        absorb(latent_ref[...], rope_key_ref[...], latent_ref[...], bias)

    @pl.when(step == pl.num_programs(0) - 1)
    def _():
        latent_out = (total_ref[...] / sum_ref[...]).astype(jnp.bfloat16)
        for head in range(HEAD_COUNT):
            out_ref[:, head * NOPE : (head + 1) * NOPE] = jnp.dot(
                latent_out[head * NEW : (head + 1) * NEW], value_up_ref[head], preferred_element_type=jnp.float32
            ).astype(jnp.bfloat16)


def attend(sequence, length, nope, rope, key_up, value_up, latent_cache, rope_cache, new_latent, new_rope):
    rows = HEAD_COUNT * NEW

    def whole(*shape):
        return pl.BlockSpec(shape, lambda step, length: (0,) * len(shape))

    def live(step, length):
        return (sequence, jnp.minimum(step, (length[0] + KEY_BLOCK - 1) // KEY_BLOCK - 1), 0)

    def live_last(step, length):
        sequence_place, block, column = live(step, length)
        return (sequence_place, column, block)

    def own(*shape):
        return pl.BlockSpec(shape, lambda step, length: (sequence,) + (0,) * (len(shape) - 1))

    return pl.pallas_call(
        functools.partial(attention_kernel, sequence),
        grid_spec=pltpu.PrefetchScalarGridSpec(
            num_scalar_prefetch=1,
            grid=(CACHE // KEY_BLOCK,),
            in_specs=[
                own(NEW, HEAD_COUNT * NOPE),
                own(NEW, HEAD_COUNT * ROPE),
                whole(HEAD_COUNT, NOPE, LATENT),
                whole(HEAD_COUNT, LATENT, NOPE),
                pl.BlockSpec((None, KEY_BLOCK, LATENT), live),
                pl.BlockSpec((None, ROPE, KEY_BLOCK), live_last),
                own(NEW, LATENT),
                pl.BlockSpec((ROPE, 2 * NEW), lambda step, length: (0, 0)),
            ],
            out_specs=whole(NEW, HEAD_COUNT * NOPE),
            scratch_shapes=[
                pltpu.VMEM((rows, LATENT), jnp.bfloat16),
                pltpu.VMEM((rows, ROPE), jnp.bfloat16),
                pltpu.VMEM((rows, 1), jnp.float32),
                pltpu.VMEM((rows, 1), jnp.float32),
                pltpu.VMEM((rows, LATENT), jnp.float32),
            ],
        ),
        out_shape=jax.ShapeDtypeStruct((NEW, HEAD_COUNT * NOPE), jnp.bfloat16),
        compiler_params=pltpu.CompilerParams(vmem_limit_bytes=KERNEL_VMEM),
        cost_estimate=pl.CostEstimate(flops=6_000_000_000, bytes_accessed=8_000_000, transcendentals=2_100_000),
        name="attend",
    )(length, nope, rope, key_up, value_up, latent_cache, rope_cache, new_latent, new_rope)


def body(
    tokens,
    routes,
    gate_scores,
    gate_weight,
    up_weight,
    down_weight,
    query_nope,
    query_rope,
    key_up,
    value_up,
    latent_cache,
    rope_cache,
    new_latent,
    new_rope,
    lengths,
):
    packed = packed_rows(tokens, routes, gate_scores)
    gathered = [packed] + [shift(packed, 0, -distance) for distance in (1, 2, 3)]
    packed, gate_weight, up_weight, down_weight = lax.optimization_barrier(
        (packed, gate_weight, up_weight, down_weight)
    )
    own_weights = joined(gate_weight[0], up_weight[0], down_weight[0])
    small = jnp.concatenate(gathered, axis=0)
    small, own_weights = lax.optimization_barrier((small, own_weights))
    weights = (own_weights, with_other_core(own_weights))
    rope_keys, new_rope_keys = jnp.swapaxes(rope_cache, 1, 2), new_rope.T
    latent_cache = pltpu.with_memory_space_constraint(latent_cache, pltpu.HBM)

    def attention(sequence, length):
        return attend(
            sequence, length, query_nope, query_rope, key_up, value_up, latent_cache, rope_keys, new_latent, new_rope_keys
        )

    above, below = shift(small, 1, -1), shift(small, 1, 1)
    half = small.shape[0] // 2
    own_low = jnp.concatenate([small, above], axis=0)
    below_low, above_low = shift(own_low, 2, 1), shift(own_low, 2, -1)
    far_low, far_high = lax.optimization_barrier((below[:half], above[half:]))
    far_low, far_high = shift(far_low, 1, 1), shift(far_high, 1, -1)
    own_high = jnp.concatenate([far_low, far_high, below], axis=0)
    below_high, above_high = shift(own_high, 2, 1), shift(own_high, 2, -1)
    own_low, own_high, below_low, above_low = lax.optimization_barrier((own_low, own_high, below_low, above_low))
    own_terms = expert_terms([own_low, own_high], weights)
    above_low, relayed, own_terms = lax.optimization_barrier((above_low, below_low, own_terms))
    above_low, below_low = expert_terms([above_low, relayed], weights)
    relayed, above_high, above_low, below_low = lax.optimization_barrier((relayed, above_high, above_low, below_low))
    far_low, far_high = shift(relayed, 2, 1), shift(above_high, 2, -1)
    above_high, below_high = expert_terms([above_high, below_high], weights)
    above_high, below_low = lax.optimization_barrier((above_high, below_low))
    near_high, near_low = shift(above_high, 2, 1), shift(below_low, 2, -1)
    far_low, far_high, above_high, below_low = lax.optimization_barrier((far_low, far_high, above_high, below_low))
    far_terms = expert_terms([far_low, far_high], weights)
    from_below, from_above = shift(far_terms[0], 2, 1), shift(far_terms[1], 2, -1)
    far_terms, near_high, near_low, lengths = lax.optimization_barrier((far_terms, near_high, near_low, lengths))
    first_attention = attention(0, lengths[:1])
    from_below, from_above, first_attention, lengths = lax.optimization_barrier(
        (from_below, from_above, first_attention, lengths)
    )
    from_below = shift(narrowed(added(above_low, from_below)), 2, 1)
    from_above = shift(narrowed(added(below_high, from_above)), 2, -1)
    second_attention = attention(1, lengths[1:])
    from_below, from_above, second_attention = lax.optimization_barrier((from_below, from_above, second_attention))
    low = added(own_terms[0], near_low, from_below)
    high = added(own_terms[1], near_high, from_above)

    size = HALF // 2
    half = size // 2
    above, far, below = low[size:], high[:size], high[size:]
    up_first = narrowed(jnp.concatenate([far[:half], above[half:]], axis=0))
    down_first = narrowed(jnp.concatenate([far[half:], below[:half]], axis=0))
    from_below, from_above = shift(up_first, 1, 1), shift(down_first, 1, -1)
    up_second = narrowed(added(above[:half], from_below[:half]))
    down_second = narrowed(added(below[half:], from_above[:half]))
    up_second, down_second = lax.optimization_barrier((up_second, down_second))
    up_second, down_second = shift(up_second, 1, 1), shift(down_second, 1, -1)
    total = low[:size] + jnp.concatenate(
        [added(up_second, from_above[half:]), added(down_second, from_below[half:])], axis=0
    )

    total = narrowed(total)
    rows = tokens.shape[0]
    arrived = [shift(total[distance * rows : (distance + 1) * rows], 0, distance) for distance in (1, 2, 3)]
    routed_out = narrowed(added(total[:rows], *arrived))
    return (routed_out, jnp.concatenate([first_attention, second_attention], axis=0))


def solution(mesh):
    cube = Mesh(mesh.devices.reshape(4, 2, 4, 4), ("z", "core", "x", "y"))
    node, local = ("z", "core"), ("x", "y")
    every = node + local
    in_specs = (
        P(every, None),
        P(every, None),
        P(every, None),
        P(local, None, node),
        P(local, None, node),
        P(local, node, None),
        P(node, local),
        P(node, local),
        P(local, None, None),
        P(local, None, None),
        P(node, None, None),
        P(node, None, None),
        P(node, None),
        P(node, None),
        P(node),
    )
    out_specs = (P(every, None), P(node, local))
    return jax.shard_map(body, mesh=cube, in_specs=in_specs, out_specs=out_specs, check_vma=False)
```

```python
import functools

import jax
import jax.numpy as jnp
import numpy as np
from jax import lax
from jax.experimental import pallas as pl
from jax.experimental.pallas import tpu as pltpu
from jax.sharding import Mesh, PartitionSpec as P

NOPE = 128
ROPE = 64
NEW = 64
CACHE = 4096
EXPERTS = 16
ROUTE_SCALE = 2.5
NEG_BIG = -1e30
AXES = ("z", "core", "x", "y")
SIZES = (4, 2, 4, 4)
RING = 4
ORDERS = ((0, 3, 2), (2, 0, 3))
KERNEL_VMEM = 12 * 1024 * 1024
EXPERT_VMEM = 10 * 1024 * 1024
PACK = 128
DEPTH = 512
UNITS = 256
HALF = 64
KEY_BLOCK = 1024
HEAD_COUNT = 8
SHORT, LONG = 60, 1
PARTS = 4
LATENT = 512
LOG2E = 1.4426950408889634


def shift(value, phase, distance):
    pairs = []
    for place in np.ndindex(*SIZES):
        target = list(place)
        axis = ORDERS[place[1]][phase]
        target[axis] = (target[axis] + distance) % RING
        pairs.append((int(np.ravel_multi_index(place, SIZES)), int(np.ravel_multi_index(target, SIZES))))
    return lax.ppermute(value, AXES, pairs)


def widened(value):
    return value.astype(jnp.float32)


def narrowed(value):
    return value.astype(jnp.bfloat16)


def added(*values):
    return sum(widened(value) for value in values)


def with_other_core(value):
    return lax.ppermute(value, "core", [(0, 1), (1, 0)])


def expert_kernel(*refs, sources, outputs):
    row_hbm = refs[:sources]
    matrices = refs[sources : sources + 2]
    out_refs = refs[sources + 2 : sources + 2 + outputs]
    rows_ref, hidden_ref, row_sem = refs[sources + 2 + outputs :]
    width = out_refs[0].shape[1]
    span = rows_ref.shape[0] // sources
    row_copies = [
        pltpu.make_async_copy(source, rows_ref.at[pl.ds(i * span, span)], row_sem.at[i])
        for i, source in enumerate(row_hbm)
    ]
    for copy in row_copies:
        copy.start()
    for copy in row_copies:
        copy.wait()
    extra = rows_ref[:, width : width + PACK].astype(jnp.float32)
    lane = lax.broadcasted_iota(jnp.int32, extra.shape, 1)
    expert = lax.axis_index("x") * RING + lax.axis_index("y")
    pick = (lane % EXPERTS == expert) & (lane < 2 * EXPERTS)
    coefficient = jnp.sum(jnp.where(pick, extra, 0.0), axis=1, keepdims=True)
    for i, matrix in enumerate(matrices):
        sums = sum(
            jnp.dot(rows_ref[:, k : k + 2 * DEPTH], matrix[k : k + 2 * DEPTH, :], preferred_element_type=jnp.float32)
            for k in range(0, width, 2 * DEPTH)
        )
        gate, up = sums[:, :UNITS], sums[:, UNITS:]
        hidden = gate / (1.0 + jnp.exp(-gate)) * up * coefficient
        hidden_ref[i] = jnp.where(coefficient > 0, hidden, 0.0).astype(jnp.bfloat16)
    for block in range(width // DEPTH):
        part, place = slice(block * DEPTH, (block + 1) * DEPTH), slice(width + block * UNITS, width + (block + 1) * UNITS)
        result = jnp.dot(hidden_ref[0], matrices[0][place, :], preferred_element_type=jnp.float32)
        result += jnp.dot(hidden_ref[1], matrices[1][place, :], preferred_element_type=jnp.float32)
        result = result.astype(jnp.bfloat16)
        for i, out_ref in enumerate(out_refs):
            out_ref[:, part] = result[i * HALF : (i + 1) * HALF]


def expert_terms(pieces, weights):
    width = pieces[0].shape[1] - PACK
    rows = sum(piece.shape[0] for piece in pieces)
    outputs = rows // HALF
    weights = [pltpu.with_memory_space_constraint(matrix, pltpu.VMEM) for matrix in weights]
    return pl.pallas_call(
        functools.partial(expert_kernel, sources=len(pieces), outputs=outputs),
        in_specs=[pl.BlockSpec(memory_space=pl.ANY)] * len(pieces)
        + [pl.BlockSpec(memory_space=pltpu.VMEM)] * 2,
        out_specs=[pl.BlockSpec(memory_space=pltpu.VMEM)] * outputs,
        out_shape=[jax.ShapeDtypeStruct((HALF, width), jnp.bfloat16)] * outputs,
        scratch_shapes=[
            pltpu.VMEM((rows, width + PACK), jnp.bfloat16),
            pltpu.VMEM((2, rows, UNITS), jnp.bfloat16),
            pltpu.SemaphoreType.DMA((len(pieces),)),
        ],
        compiler_params=pltpu.CompilerParams(vmem_limit_bytes=EXPERT_VMEM),
        cost_estimate=pl.CostEstimate(
            flops=6 * rows * width * UNITS * 2, bytes_accessed=4 * rows * width, transcendentals=0
        ),
        name="expert",
    )(*pieces, *weights)


def join_kernel(gate_hbm, up_hbm, down_hbm, out_ref, sem):
    width = gate_hbm.shape[0]
    copies = [
        pltpu.make_async_copy(source, out_ref.at[pl.ds(0, width), pl.ds(i * UNITS, UNITS)], sem.at[i])
        for i, source in enumerate((gate_hbm, up_hbm))
    ]
    for i in range(width // DEPTH):
        part = out_ref.at[pl.ds(width + i * UNITS, UNITS)]
        copies.append(pltpu.make_async_copy(down_hbm.at[:, pl.ds(i * DEPTH, DEPTH)], part, sem.at[2 + i]))
    for copy in copies:
        copy.start()
    for copy in copies:
        copy.wait()


def joined(gate, up, down):
    width = gate.shape[0]
    blocks = width // DEPTH
    matrices = [pltpu.with_memory_space_constraint(matrix, pltpu.HBM) for matrix in (gate, up, down)]
    return pl.pallas_call(
        join_kernel,
        in_specs=[pl.BlockSpec(memory_space=pl.ANY)] * 3,
        out_specs=pl.BlockSpec(memory_space=pltpu.VMEM),
        out_shape=pltpu.VMEM((width + blocks * UNITS, DEPTH), jnp.bfloat16),
        scratch_shapes=[pltpu.SemaphoreType.DMA((2 + blocks,))],
        compiler_params=pltpu.CompilerParams(vmem_limit_bytes=KERNEL_VMEM),
        cost_estimate=pl.CostEstimate(flops=0, bytes_accessed=12 * width * UNITS, transcendentals=0),
        name="join",
    )(*matrices)


def pack_kernel(tokens_ref, routes_ref, scores_ref, out_ref):
    rows, width = tokens_ref.shape
    out_ref[:, :width] = tokens_ref[...]
    scores = scores_ref[...]
    weights = scores / jnp.sum(scores, axis=1, keepdims=True) * ROUTE_SCALE
    lane = lax.broadcasted_iota(jnp.int32, (rows, PACK), 1)
    dense = jnp.zeros((rows, PACK), jnp.float32)
    for choice in range(scores.shape[1]):
        named = routes_ref[:, choice : choice + 1] == lane % EXPERTS
        dense += jnp.where(named, weights[:, choice : choice + 1], 0.0)
    high = dense.astype(jnp.bfloat16).astype(jnp.float32)
    extra = jnp.where(lane < EXPERTS, high, jnp.where(lane < 2 * EXPERTS, dense - high, 0.0))
    out_ref[:, width:] = extra.astype(jnp.bfloat16)


def packed_rows(tokens, routes, gate_scores):
    rows, width = tokens.shape
    return pl.pallas_call(
        pack_kernel,
        out_shape=jax.ShapeDtypeStruct((rows, width + PACK), jnp.bfloat16),
        compiler_params=pltpu.CompilerParams(vmem_limit_bytes=KERNEL_VMEM),
        name="pack",
    )(*(pltpu.with_memory_space_constraint(value, pltpu.HBM) for value in (tokens, routes, gate_scores)))


def attention_kernel(
    sequence, length_ref, nope_ref, rope_ref, key_up_ref, value_up_ref, latent_ref, rope_key_ref,
    new_latent_ref, new_rope_ref, out_ref, query_ref, query_rope_ref, top_ref, sum_ref, total_ref,
):
    step = pl.program_id(0)
    length = length_ref[sequence]
    scale = (NOPE + ROPE) ** (-0.5) * LOG2E
    contract_last = (((1,), (1,)), ((), ()))

    def absorb(keys, rope_keys, values, bias):
        rows = HEAD_COUNT * NEW // PARTS
        parts = [slice(part * rows, (part + 1) * rows) for part in range(PARTS)]
        biases = [bias if bias.shape[0] == 1 else bias[part] for part in parts]
        scores = []
        for part, added_bias in zip(parts, biases):
            score = lax.dot_general(query_ref[part, :], keys, contract_last, preferred_element_type=jnp.float32)
            score += jnp.dot(query_rope_ref[part, :], rope_keys, preferred_element_type=jnp.float32)
            scores.append(score * scale + added_bias)
        for part, score in zip(parts, scores):
            old_top = top_ref[part, :]
            top = jnp.maximum(old_top, jnp.max(score, axis=1, keepdims=True))
            shrink = jnp.exp2(old_top - top)
            probs = jnp.exp2(score - top)
            top_ref[part, :] = top
            sum_ref[part, :] = sum_ref[part, :] * shrink + jnp.sum(probs, axis=1, keepdims=True)
            total_ref[part, :] = total_ref[part, :] * shrink + jnp.dot(
                probs.astype(jnp.bfloat16), values, preferred_element_type=jnp.float32
            )

    @pl.when(step == 0)
    def _():
        for head in range(HEAD_COUNT):
            query_ref[head * NEW : (head + 1) * NEW, :] = jnp.dot(
                nope_ref[:, head * NOPE : (head + 1) * NOPE], key_up_ref[head], preferred_element_type=jnp.float32
            ).astype(jnp.bfloat16)
            query_rope_ref[head * NEW : (head + 1) * NEW, :] = rope_ref[:, head * ROPE : (head + 1) * ROPE]
        top_ref[...] = jnp.full_like(top_ref, NEG_BIG)
        sum_ref[...] = jnp.zeros_like(sum_ref)
        total_ref[...] = jnp.zeros_like(total_ref)
        position = lax.broadcasted_iota(jnp.int32, (HEAD_COUNT * NEW, NEW), 0) % NEW
        fresh = lax.broadcasted_iota(jnp.int32, (HEAD_COUNT * NEW, NEW), 1)
        bias = jnp.where(fresh <= position, 0.0, NEG_BIG)
        absorb(new_latent_ref[...], new_rope_ref[:, sequence * NEW : (sequence + 1) * NEW], new_latent_ref[...], bias)

    @pl.when(step * KEY_BLOCK < length)
    def _():
        slot = step * KEY_BLOCK + lax.broadcasted_iota(jnp.int32, (1, KEY_BLOCK), 1)
        bias = jnp.where(slot < length, 0.0, NEG_BIG)
        absorb(latent_ref[...], rope_key_ref[...], latent_ref[...], bias)

    @pl.when(step == pl.num_programs(0) - 1)
    def _():
        latent_out = (total_ref[...] / sum_ref[...]).astype(jnp.bfloat16)
        for head in range(HEAD_COUNT):
            out_ref[:, head * NOPE : (head + 1) * NOPE] = jnp.dot(
                latent_out[head * NEW : (head + 1) * NEW], value_up_ref[head], preferred_element_type=jnp.float32
            ).astype(jnp.bfloat16)


def attend(weight, sequence, length, nope, rope, key_up, value_up, latent_cache, rope_cache, new_latent, new_rope):
    rows = HEAD_COUNT * NEW

    def whole(*shape):
        return pl.BlockSpec(shape, lambda step, length: (0,) * len(shape))

    def live(step, length):
        return (sequence, jnp.minimum(step, (length[sequence] + KEY_BLOCK - 1) // KEY_BLOCK - 1), 0)

    def live_last(step, length):
        sequence_place, block, column = live(step, length)
        return (sequence_place, column, block)

    def own(*shape):
        return pl.BlockSpec(shape, lambda step, length: (sequence,) + (0,) * (len(shape) - 1))

    return pl.pallas_call(
        functools.partial(attention_kernel, sequence),
        grid_spec=pltpu.PrefetchScalarGridSpec(
            num_scalar_prefetch=1,
            grid=(CACHE // KEY_BLOCK,),
            in_specs=[
                own(NEW, HEAD_COUNT * NOPE),
                own(NEW, HEAD_COUNT * ROPE),
                whole(HEAD_COUNT, NOPE, LATENT),
                whole(HEAD_COUNT, LATENT, NOPE),
                pl.BlockSpec((None, KEY_BLOCK, LATENT), live),
                pl.BlockSpec((None, ROPE, KEY_BLOCK), live_last),
                own(NEW, LATENT),
                pl.BlockSpec((ROPE, 2 * NEW), lambda step, length: (0, 0)),
            ],
            out_specs=whole(NEW, HEAD_COUNT * NOPE),
            scratch_shapes=[
                pltpu.VMEM((rows, LATENT), jnp.bfloat16),
                pltpu.VMEM((rows, ROPE), jnp.bfloat16),
                pltpu.VMEM((rows, 1), jnp.float32),
                pltpu.VMEM((rows, 1), jnp.float32),
                pltpu.VMEM((rows, LATENT), jnp.float32),
            ],
        ),
        out_shape=jax.ShapeDtypeStruct((NEW, HEAD_COUNT * NOPE), jnp.bfloat16),
        compiler_params=pltpu.CompilerParams(vmem_limit_bytes=KERNEL_VMEM),
        cost_estimate=pl.CostEstimate(flops=6_000_000_000 // weight, bytes_accessed=8_000_000 // weight, transcendentals=2_100_000 // weight),
        name="attend",
    )(length, nope, rope, key_up, value_up, latent_cache, rope_cache, new_latent, new_rope)


def body(
    tokens,
    routes,
    gate_scores,
    gate_weight,
    up_weight,
    down_weight,
    query_nope,
    query_rope,
    key_up,
    value_up,
    latent_cache,
    rope_cache,
    new_latent,
    new_rope,
    lengths,
):
    packed = packed_rows(tokens, routes, gate_scores)
    gathered = [packed] + [shift(packed, 0, -distance) for distance in (1, 2, 3)]
    packed, gate_weight, up_weight, down_weight = lax.optimization_barrier(
        (packed, gate_weight, up_weight, down_weight)
    )
    own_weights = joined(gate_weight[0], up_weight[0], down_weight[0])
    small = jnp.concatenate(gathered, axis=0)
    small, own_weights = lax.optimization_barrier((small, own_weights))
    weights = (own_weights, with_other_core(own_weights))
    rope_keys, new_rope_keys = jnp.swapaxes(rope_cache, 1, 2), new_rope.T
    latent_cache = pltpu.with_memory_space_constraint(latent_cache, pltpu.HBM)

    def attention(sequence, lengths, weight):
        return attend(
            weight, sequence, lengths, query_nope, query_rope, key_up, value_up, latent_cache, rope_keys, new_latent, new_rope_keys
        )

    above, below = shift(small, 1, -1), shift(small, 1, 1)
    half = small.shape[0] // 2
    own_low = jnp.concatenate([small, above], axis=0)
    below_low, above_low = shift(own_low, 2, 1), shift(own_low, 2, -1)
    far_low, far_high = lax.optimization_barrier((below[:half], above[half:]))
    far_low, far_high = shift(far_low, 1, 1), shift(far_high, 1, -1)
    own_high = jnp.concatenate([far_low, far_high, below], axis=0)
    below_high, above_high = shift(own_high, 2, 1), shift(own_high, 2, -1)
    own_low, own_high, below_low, above_low = lax.optimization_barrier((own_low, own_high, below_low, above_low))
    own_terms = expert_terms([own_low, own_high], weights)
    above_low, relayed, own_terms = lax.optimization_barrier((above_low, below_low, own_terms))
    above_low, below_low = expert_terms([above_low, relayed], weights)
    relayed, above_high, above_low, below_low = lax.optimization_barrier((relayed, above_high, above_low, below_low))
    far_low, far_high = shift(relayed, 2, 1), shift(above_high, 2, -1)
    above_high, below_high = expert_terms([above_high, below_high], weights)
    above_high, below_low = lax.optimization_barrier((above_high, below_low))
    near_high, near_low = shift(above_high, 2, 1), shift(below_low, 2, -1)
    far_low, far_high, above_high, below_low = lax.optimization_barrier((far_low, far_high, above_high, below_low))
    far_terms = expert_terms([far_low, far_high], weights)
    from_below, from_above = shift(far_terms[0], 2, 1), shift(far_terms[1], 2, -1)
    far_terms, lengths = lax.optimization_barrier((far_terms, lengths))
    first_attention = attention(0, lengths, SHORT)
    from_below, from_above, near_high, near_low, first_attention, lengths = lax.optimization_barrier(
        (from_below, from_above, near_high, near_low, first_attention, lengths)
    )
    from_below = shift(narrowed(added(above_low, from_below)), 2, 1)
    from_above = shift(narrowed(added(below_high, from_above)), 2, -1)
    second_attention = attention(1, lengths, LONG)
    from_below, from_above, second_attention = lax.optimization_barrier((from_below, from_above, second_attention))
    low = added(own_terms[0], near_low, from_below)
    high = added(own_terms[1], near_high, from_above)

    size = HALF // 2
    half = size // 2
    above, far, below = low[size:], high[:size], high[size:]
    up_first = narrowed(jnp.concatenate([far[:half], above[half:]], axis=0))
    down_first = narrowed(jnp.concatenate([far[half:], below[:half]], axis=0))
    from_below, from_above = shift(up_first, 1, 1), shift(down_first, 1, -1)
    up_second = narrowed(added(above[:half], from_below[:half]))
    down_second = narrowed(added(below[half:], from_above[:half]))
    up_second, down_second = lax.optimization_barrier((up_second, down_second))
    up_second, down_second = shift(up_second, 1, 1), shift(down_second, 1, -1)
    total = low[:size] + jnp.concatenate(
        [added(up_second, from_above[half:]), added(down_second, from_below[half:])], axis=0
    )

    total = narrowed(total)
    rows = tokens.shape[0]
    arrived = [shift(total[distance * rows : (distance + 1) * rows], 0, distance) for distance in (1, 2, 3)]
    routed_out = narrowed(added(total[:rows], *arrived))
    return (routed_out, jnp.concatenate([first_attention, second_attention], axis=0))


def solution(mesh):
    cube = Mesh(mesh.devices.reshape(4, 2, 4, 4), ("z", "core", "x", "y"))
    node, local = ("z", "core"), ("x", "y")
    every = node + local
    in_specs = (
        P(every, None),
        P(every, None),
        P(every, None),
        P(local, None, node),
        P(local, None, node),
        P(local, node, None),
        P(node, local),
        P(node, local),
        P(local, None, None),
        P(local, None, None),
        P(node, None, None),
        P(node, None, None),
        P(node, None),
        P(node, None),
        P(node),
    )
    out_specs = (P(every, None), P(node, local))
    return jax.shard_map(body, mesh=cube, in_specs=in_specs, out_specs=out_specs, check_vma=False)
```

```python
import functools

import jax
import jax.numpy as jnp
import numpy as np
from jax import lax
from jax.experimental import pallas as pl
from jax.experimental.pallas import tpu as pltpu
from jax.sharding import Mesh, PartitionSpec as P

NOPE = 128
ROPE = 64
NEW = 64
CACHE = 4096
EXPERTS = 16
ROUTE_SCALE = 2.5
NEG_BIG = -1e30
AXES = ("z", "core", "x", "y")
SIZES = (4, 2, 4, 4)
RING = 4
ORDERS = ((0, 3, 2), (2, 0, 3))
KERNEL_VMEM = 12 * 1024 * 1024
EXPERT_VMEM = 10 * 1024 * 1024
PACK = 128
DEPTH = 512
UNITS = 256
HALF = 64
KEY_BLOCK = 1024
HEAD_COUNT = 8
SHORT, LONG = 60, 1
PARTS = 2
LATENT = 512
LOG2E = 1.4426950408889634


def shift(value, phase, distance):
    pairs = []
    for place in np.ndindex(*SIZES):
        target = list(place)
        axis = ORDERS[place[1]][phase]
        target[axis] = (target[axis] + distance) % RING
        pairs.append((int(np.ravel_multi_index(place, SIZES)), int(np.ravel_multi_index(target, SIZES))))
    return lax.ppermute(value, AXES, pairs)


def widened(value):
    return value.astype(jnp.float32)


def narrowed(value):
    return value.astype(jnp.bfloat16)


def added(*values):
    return sum(widened(value) for value in values)


def with_other_core(value):
    return lax.ppermute(value, "core", [(0, 1), (1, 0)])


def expert_kernel(*refs, sources, outputs):
    row_hbm = refs[:sources]
    matrices = refs[sources : sources + 2]
    out_refs = refs[sources + 2 : sources + 2 + outputs]
    rows_ref, hidden_ref, row_sem = refs[sources + 2 + outputs :]
    width = out_refs[0].shape[1]
    span = rows_ref.shape[0] // sources
    row_copies = [
        pltpu.make_async_copy(source, rows_ref.at[pl.ds(i * span, span)], row_sem.at[i])
        for i, source in enumerate(row_hbm)
    ]
    for copy in row_copies:
        copy.start()
    for copy in row_copies:
        copy.wait()
    extra = rows_ref[:, width : width + PACK].astype(jnp.float32)
    lane = lax.broadcasted_iota(jnp.int32, extra.shape, 1)
    expert = lax.axis_index("x") * RING + lax.axis_index("y")
    pick = (lane % EXPERTS == expert) & (lane < 2 * EXPERTS)
    coefficient = jnp.sum(jnp.where(pick, extra, 0.0), axis=1, keepdims=True)
    for i, matrix in enumerate(matrices):
        sums = sum(
            jnp.dot(rows_ref[:, k : k + 2 * DEPTH], matrix[k : k + 2 * DEPTH, :], preferred_element_type=jnp.float32)
            for k in range(0, width, 2 * DEPTH)
        )
        gate, up = sums[:, :UNITS], sums[:, UNITS:]
        hidden = gate / (1.0 + jnp.exp(-gate)) * up * coefficient
        hidden_ref[i] = jnp.where(coefficient > 0, hidden, 0.0).astype(jnp.bfloat16)
    for block in range(width // DEPTH):
        part, place = slice(block * DEPTH, (block + 1) * DEPTH), slice(width + block * UNITS, width + (block + 1) * UNITS)
        result = jnp.dot(hidden_ref[0], matrices[0][place, :], preferred_element_type=jnp.float32)
        result += jnp.dot(hidden_ref[1], matrices[1][place, :], preferred_element_type=jnp.float32)
        result = result.astype(jnp.bfloat16)
        for i, out_ref in enumerate(out_refs):
            out_ref[:, part] = result[i * HALF : (i + 1) * HALF]


def expert_terms(pieces, weights):
    width = pieces[0].shape[1] - PACK
    rows = sum(piece.shape[0] for piece in pieces)
    outputs = rows // HALF
    weights = [pltpu.with_memory_space_constraint(matrix, pltpu.VMEM) for matrix in weights]
    return pl.pallas_call(
        functools.partial(expert_kernel, sources=len(pieces), outputs=outputs),
        in_specs=[pl.BlockSpec(memory_space=pl.ANY)] * len(pieces)
        + [pl.BlockSpec(memory_space=pltpu.VMEM)] * 2,
        out_specs=[pl.BlockSpec(memory_space=pltpu.VMEM)] * outputs,
        out_shape=[jax.ShapeDtypeStruct((HALF, width), jnp.bfloat16)] * outputs,
        scratch_shapes=[
            pltpu.VMEM((rows, width + PACK), jnp.bfloat16),
            pltpu.VMEM((2, rows, UNITS), jnp.bfloat16),
            pltpu.SemaphoreType.DMA((len(pieces),)),
        ],
        compiler_params=pltpu.CompilerParams(vmem_limit_bytes=EXPERT_VMEM),
        cost_estimate=pl.CostEstimate(
            flops=6 * rows * width * UNITS * 2, bytes_accessed=4 * rows * width, transcendentals=0
        ),
        name="expert",
    )(*pieces, *weights)


def join_kernel(gate_hbm, up_hbm, down_hbm, out_ref, sem):
    width = gate_hbm.shape[0]
    copies = [
        pltpu.make_async_copy(source, out_ref.at[pl.ds(0, width), pl.ds(i * UNITS, UNITS)], sem.at[i])
        for i, source in enumerate((gate_hbm, up_hbm))
    ]
    for i in range(width // DEPTH):
        part = out_ref.at[pl.ds(width + i * UNITS, UNITS)]
        copies.append(pltpu.make_async_copy(down_hbm.at[:, pl.ds(i * DEPTH, DEPTH)], part, sem.at[2 + i]))
    for copy in copies:
        copy.start()
    for copy in copies:
        copy.wait()


def joined(gate, up, down):
    width = gate.shape[0]
    blocks = width // DEPTH
    matrices = [pltpu.with_memory_space_constraint(matrix, pltpu.HBM) for matrix in (gate, up, down)]
    return pl.pallas_call(
        join_kernel,
        in_specs=[pl.BlockSpec(memory_space=pl.ANY)] * 3,
        out_specs=pl.BlockSpec(memory_space=pltpu.VMEM),
        out_shape=pltpu.VMEM((width + blocks * UNITS, DEPTH), jnp.bfloat16),
        scratch_shapes=[pltpu.SemaphoreType.DMA((2 + blocks,))],
        compiler_params=pltpu.CompilerParams(vmem_limit_bytes=KERNEL_VMEM),
        cost_estimate=pl.CostEstimate(flops=0, bytes_accessed=12 * width * UNITS, transcendentals=0),
        name="join",
    )(*matrices)


def pack_kernel(tokens_ref, routes_ref, scores_ref, out_ref):
    rows, width = tokens_ref.shape
    out_ref[:, :width] = tokens_ref[...]
    scores = scores_ref[...]
    weights = scores / jnp.sum(scores, axis=1, keepdims=True) * ROUTE_SCALE
    lane = lax.broadcasted_iota(jnp.int32, (rows, PACK), 1)
    dense = jnp.zeros((rows, PACK), jnp.float32)
    for choice in range(scores.shape[1]):
        named = routes_ref[:, choice : choice + 1] == lane % EXPERTS
        dense += jnp.where(named, weights[:, choice : choice + 1], 0.0)
    high = dense.astype(jnp.bfloat16).astype(jnp.float32)
    extra = jnp.where(lane < EXPERTS, high, jnp.where(lane < 2 * EXPERTS, dense - high, 0.0))
    out_ref[:, width:] = extra.astype(jnp.bfloat16)


def packed_rows(tokens, routes, gate_scores):
    rows, width = tokens.shape
    return pl.pallas_call(
        pack_kernel,
        out_shape=jax.ShapeDtypeStruct((rows, width + PACK), jnp.bfloat16),
        compiler_params=pltpu.CompilerParams(vmem_limit_bytes=KERNEL_VMEM),
        name="pack",
    )(*(pltpu.with_memory_space_constraint(value, pltpu.HBM) for value in (tokens, routes, gate_scores)))


def attention_kernel(
    sequence, length_ref, nope_ref, rope_ref, key_up_ref, value_up_ref, latent_ref, rope_key_ref,
    new_latent_ref, new_rope_ref, out_ref, query_ref, query_rope_ref, top_ref, sum_ref, total_ref,
):
    step = pl.program_id(0)
    length = length_ref[sequence]
    scale = (NOPE + ROPE) ** (-0.5) * LOG2E
    contract_last = (((1,), (1,)), ((), ()))

    def absorb(keys, rope_keys, values, bias):
        rows = HEAD_COUNT * NEW // PARTS
        parts = [slice(part * rows, (part + 1) * rows) for part in range(PARTS)]
        biases = [bias if bias.shape[0] == 1 else bias[part] for part in parts]
        scores = []
        for part, added_bias in zip(parts, biases):
            score = lax.dot_general(query_ref[part, :], keys, contract_last, preferred_element_type=jnp.float32)
            score += jnp.dot(query_rope_ref[part, :], rope_keys, preferred_element_type=jnp.float32)
            scores.append(score * scale + added_bias)
        for part, score in zip(parts, scores):
            old_top = top_ref[part, :]
            top = jnp.maximum(old_top, jnp.max(score, axis=1, keepdims=True))
            shrink = jnp.exp2(old_top - top)
            probs = jnp.exp2(score - top)
            top_ref[part, :] = top
            sum_ref[part, :] = sum_ref[part, :] * shrink + jnp.sum(probs, axis=1, keepdims=True)
            total_ref[part, :] = total_ref[part, :] * shrink + jnp.dot(
                probs.astype(jnp.bfloat16), values, preferred_element_type=jnp.float32
            )

    @pl.when(step == 0)
    def _():
        for head in range(HEAD_COUNT):
            query_ref[head * NEW : (head + 1) * NEW, :] = jnp.dot(
                nope_ref[:, head * NOPE : (head + 1) * NOPE], key_up_ref[head], preferred_element_type=jnp.float32
            ).astype(jnp.bfloat16)
            query_rope_ref[head * NEW : (head + 1) * NEW, :] = rope_ref[:, head * ROPE : (head + 1) * ROPE]
        top_ref[...] = jnp.full_like(top_ref, NEG_BIG)
        sum_ref[...] = jnp.zeros_like(sum_ref)
        total_ref[...] = jnp.zeros_like(total_ref)
        position = lax.broadcasted_iota(jnp.int32, (HEAD_COUNT * NEW, NEW), 0) % NEW
        fresh = lax.broadcasted_iota(jnp.int32, (HEAD_COUNT * NEW, NEW), 1)
        bias = jnp.where(fresh <= position, 0.0, NEG_BIG)
        absorb(new_latent_ref[...], new_rope_ref[:, sequence * NEW : (sequence + 1) * NEW], new_latent_ref[...], bias)

    @pl.when(step * KEY_BLOCK < length)
    def _():
        slot = step * KEY_BLOCK + lax.broadcasted_iota(jnp.int32, (1, KEY_BLOCK), 1)
        bias = jnp.where(slot < length, 0.0, NEG_BIG)
        absorb(latent_ref[...], rope_key_ref[...], latent_ref[...], bias)

    @pl.when(step == pl.num_programs(0) - 1)
    def _():
        latent_out = (total_ref[...] / sum_ref[...]).astype(jnp.bfloat16)
        for head in range(HEAD_COUNT):
            out_ref[:, head * NOPE : (head + 1) * NOPE] = jnp.dot(
                latent_out[head * NEW : (head + 1) * NEW], value_up_ref[head], preferred_element_type=jnp.float32
            ).astype(jnp.bfloat16)


def attend(weight, sequence, length, nope, rope, key_up, value_up, latent_cache, rope_cache, new_latent, new_rope):
    rows = HEAD_COUNT * NEW

    def whole(*shape):
        return pl.BlockSpec(shape, lambda step, length: (0,) * len(shape))

    def live(step, length):
        return (sequence, jnp.minimum(step, (length[sequence] + KEY_BLOCK - 1) // KEY_BLOCK - 1), 0)

    def live_last(step, length):
        sequence_place, block, column = live(step, length)
        return (sequence_place, column, block)

    def own(*shape):
        return pl.BlockSpec(shape, lambda step, length: (sequence,) + (0,) * (len(shape) - 1))

    return pl.pallas_call(
        functools.partial(attention_kernel, sequence),
        grid_spec=pltpu.PrefetchScalarGridSpec(
            num_scalar_prefetch=1,
            grid=(CACHE // KEY_BLOCK,),
            in_specs=[
                own(NEW, HEAD_COUNT * NOPE),
                own(NEW, HEAD_COUNT * ROPE),
                whole(HEAD_COUNT, NOPE, LATENT),
                whole(HEAD_COUNT, LATENT, NOPE),
                pl.BlockSpec((None, KEY_BLOCK, LATENT), live),
                pl.BlockSpec((None, ROPE, KEY_BLOCK), live_last),
                own(NEW, LATENT),
                pl.BlockSpec((ROPE, 2 * NEW), lambda step, length: (0, 0)),
            ],
            out_specs=whole(NEW, HEAD_COUNT * NOPE),
            scratch_shapes=[
                pltpu.VMEM((rows, LATENT), jnp.bfloat16),
                pltpu.VMEM((rows, ROPE), jnp.bfloat16),
                pltpu.VMEM((rows, 1), jnp.float32),
                pltpu.VMEM((rows, 1), jnp.float32),
                pltpu.VMEM((rows, LATENT), jnp.float32),
            ],
        ),
        out_shape=jax.ShapeDtypeStruct((NEW, HEAD_COUNT * NOPE), jnp.bfloat16),
        compiler_params=pltpu.CompilerParams(vmem_limit_bytes=KERNEL_VMEM),
        cost_estimate=pl.CostEstimate(flops=6_000_000_000 // weight, bytes_accessed=8_000_000 // weight, transcendentals=2_100_000 // weight),
        name="attend",
    )(length, nope, rope, key_up, value_up, latent_cache, rope_cache, new_latent, new_rope)


def body(
    tokens,
    routes,
    gate_scores,
    gate_weight,
    up_weight,
    down_weight,
    query_nope,
    query_rope,
    key_up,
    value_up,
    latent_cache,
    rope_cache,
    new_latent,
    new_rope,
    lengths,
):
    packed = packed_rows(tokens, routes, gate_scores)
    gathered = [packed] + [shift(packed, 0, -distance) for distance in (1, 2, 3)]
    packed, gate_weight, up_weight, down_weight = lax.optimization_barrier(
        (packed, gate_weight, up_weight, down_weight)
    )
    own_weights = joined(gate_weight[0], up_weight[0], down_weight[0])
    small = jnp.concatenate(gathered, axis=0)
    small, own_weights = lax.optimization_barrier((small, own_weights))
    weights = (own_weights, with_other_core(own_weights))
    rope_keys, new_rope_keys = jnp.swapaxes(rope_cache, 1, 2), new_rope.T
    latent_cache = pltpu.with_memory_space_constraint(latent_cache, pltpu.HBM)

    def attention(sequence, lengths, weight):
        return attend(
            weight, sequence, lengths, query_nope, query_rope, key_up, value_up, latent_cache, rope_keys, new_latent, new_rope_keys
        )

    above, below = shift(small, 1, -1), shift(small, 1, 1)
    half = small.shape[0] // 2
    own_low = jnp.concatenate([small, above], axis=0)
    far_low, far_high = lax.optimization_barrier((below[:half], above[half:]))
    far_low, far_high = shift(far_low, 1, 1), shift(far_high, 1, -1)
    own_low, far_low = lax.optimization_barrier((own_low, far_low))
    below_low, above_low = shift(own_low, 2, 1), shift(own_low, 2, -1)
    own_high = jnp.concatenate([far_low, far_high, below], axis=0)
    below_high, above_high = shift(own_high, 2, 1), shift(own_high, 2, -1)
    own_low, own_high, below_low, above_low = lax.optimization_barrier((own_low, own_high, below_low, above_low))
    own_terms = expert_terms([own_low, own_high], weights)
    above_low, relayed, own_terms = lax.optimization_barrier((above_low, below_low, own_terms))
    above_low, below_low = expert_terms([above_low, relayed], weights)
    relayed, above_high, above_low, below_low = lax.optimization_barrier((relayed, above_high, above_low, below_low))
    far_low, far_high = shift(relayed, 2, 1), shift(above_high, 2, -1)
    above_high, below_high = expert_terms([above_high, below_high], weights)
    above_high, below_low = lax.optimization_barrier((above_high, below_low))
    near_high, near_low = shift(above_high, 2, 1), shift(below_low, 2, -1)
    far_low, far_high, above_high, below_low = lax.optimization_barrier((far_low, far_high, above_high, below_low))
    far_terms = expert_terms([far_low, far_high], weights)
    from_below, from_above = shift(far_terms[0], 2, 1), shift(far_terms[1], 2, -1)
    far_terms, lengths = lax.optimization_barrier((far_terms, lengths))
    first_attention = attention(0, lengths, SHORT)
    from_below, from_above, near_high, near_low, first_attention, lengths = lax.optimization_barrier(
        (from_below, from_above, near_high, near_low, first_attention, lengths)
    )
    from_below = shift(narrowed(added(above_low, from_below)), 2, 1)
    from_above = shift(narrowed(added(below_high, from_above)), 2, -1)
    second_attention = attention(1, lengths, LONG)
    from_below, from_above, second_attention = lax.optimization_barrier((from_below, from_above, second_attention))
    low = added(own_terms[0], near_low, from_below)
    high = added(own_terms[1], near_high, from_above)

    size = HALF // 2
    half = size // 2
    above, far, below = low[size:], high[:size], high[size:]
    up_first = narrowed(jnp.concatenate([far[:half], above[half:]], axis=0))
    down_first = narrowed(jnp.concatenate([far[half:], below[:half]], axis=0))
    from_below, from_above = shift(up_first, 1, 1), shift(down_first, 1, -1)
    up_second = narrowed(added(above[:half], from_below[:half]))
    down_second = narrowed(added(below[half:], from_above[:half]))
    up_second, down_second = lax.optimization_barrier((up_second, down_second))
    up_second, down_second = shift(up_second, 1, 1), shift(down_second, 1, -1)
    total = low[:size] + jnp.concatenate(
        [added(up_second, from_above[half:]), added(down_second, from_below[half:])], axis=0
    )

    total = narrowed(total)
    rows = tokens.shape[0]
    arrived = [shift(total[distance * rows : (distance + 1) * rows], 0, distance) for distance in (1, 2, 3)]
    routed_out = narrowed(added(total[:rows], *arrived))
    return (routed_out, jnp.concatenate([first_attention, second_attention], axis=0))


def solution(mesh):
    cube = Mesh(mesh.devices.reshape(4, 2, 4, 4), ("z", "core", "x", "y"))
    node, local = ("z", "core"), ("x", "y")
    every = node + local
    in_specs = (
        P(every, None),
        P(every, None),
        P(every, None),
        P(local, None, node),
        P(local, None, node),
        P(local, node, None),
        P(node, local),
        P(node, local),
        P(local, None, None),
        P(local, None, None),
        P(node, None, None),
        P(node, None, None),
        P(node, None),
        P(node, None),
        P(node),
    )
    out_specs = (P(every, None), P(node, local))
    return jax.shard_map(body, mesh=cube, in_specs=in_specs, out_specs=out_specs, check_vma=False)
```

```python
import functools

import jax
import jax.numpy as jnp
import numpy as np
from jax import lax
from jax.experimental import pallas as pl
from jax.experimental.pallas import tpu as pltpu
from jax.sharding import Mesh, PartitionSpec as P

NOPE = 128
ROPE = 64
NEW = 64
CACHE = 4096
EXPERTS = 16
ROUTE_SCALE = 2.5
NEG_BIG = -1e30
AXES = ("z", "core", "x", "y")
SIZES = (4, 2, 4, 4)
RING = 4
ORDERS = ((0, 3, 2), (2, 0, 3))
KERNEL_VMEM = 12 * 1024 * 1024
EXPERT_VMEM = 10 * 1024 * 1024
PACK = 128
DEPTH = 512
UNITS = 256
HALF = 64
KEY_BLOCK = 1024
HEAD_COUNT = 8
SHORT, LONG = 60, 1
PARTS = 2
LATENT = 512
LOG2E = 1.4426950408889634


def shift(value, phase, distance):
    pairs = []
    for place in np.ndindex(*SIZES):
        target = list(place)
        axis = ORDERS[place[1]][phase]
        target[axis] = (target[axis] + distance) % RING
        pairs.append((int(np.ravel_multi_index(place, SIZES)), int(np.ravel_multi_index(target, SIZES))))
    return lax.ppermute(value, AXES, pairs)


def widened(value):
    return value.astype(jnp.float32)


def narrowed(value):
    return value.astype(jnp.bfloat16)


def added(*values):
    return sum(widened(value) for value in values)


def with_other_core(value):
    return lax.ppermute(value, "core", [(0, 1), (1, 0)])


def expert_kernel(*refs, sources, outputs):
    row_hbm = refs[:sources]
    matrices = refs[sources : sources + 2]
    out_refs = refs[sources + 2 : sources + 2 + outputs]
    rows_ref, hidden_ref, row_sem = refs[sources + 2 + outputs :]
    width = out_refs[0].shape[1]
    span = rows_ref.shape[0] // sources
    row_copies = [
        pltpu.make_async_copy(source, rows_ref.at[pl.ds(i * span, span)], row_sem.at[i])
        for i, source in enumerate(row_hbm)
    ]
    for copy in row_copies:
        copy.start()
    for copy in row_copies:
        copy.wait()
    extra = rows_ref[:, width : width + PACK].astype(jnp.float32)
    lane = lax.broadcasted_iota(jnp.int32, extra.shape, 1)
    expert = lax.axis_index("x") * RING + lax.axis_index("y")
    pick = (lane % EXPERTS == expert) & (lane < 2 * EXPERTS)
    coefficient = jnp.sum(jnp.where(pick, extra, 0.0), axis=1, keepdims=True)
    for i, matrix in enumerate(matrices):
        sums = sum(
            jnp.dot(rows_ref[:, k : k + 2 * DEPTH], matrix[k : k + 2 * DEPTH, :], preferred_element_type=jnp.float32)
            for k in range(0, width, 2 * DEPTH)
        )
        gate, up = sums[:, :UNITS], sums[:, UNITS:]
        hidden = gate / (1.0 + jnp.exp(-gate)) * up * coefficient
        hidden_ref[i] = jnp.where(coefficient > 0, hidden, 0.0).astype(jnp.bfloat16)
    for block in range(width // DEPTH):
        part, place = slice(block * DEPTH, (block + 1) * DEPTH), slice(width + block * UNITS, width + (block + 1) * UNITS)
        result = jnp.dot(hidden_ref[0], matrices[0][place, :], preferred_element_type=jnp.float32)
        result += jnp.dot(hidden_ref[1], matrices[1][place, :], preferred_element_type=jnp.float32)
        result = result.astype(jnp.bfloat16)
        for i, out_ref in enumerate(out_refs):
            out_ref[:, part] = result[i * HALF : (i + 1) * HALF]


def expert_terms(pieces, weights):
    width = pieces[0].shape[1] - PACK
    rows = sum(piece.shape[0] for piece in pieces)
    outputs = rows // HALF
    weights = [pltpu.with_memory_space_constraint(matrix, pltpu.VMEM) for matrix in weights]
    return pl.pallas_call(
        functools.partial(expert_kernel, sources=len(pieces), outputs=outputs),
        in_specs=[pl.BlockSpec(memory_space=pl.ANY)] * len(pieces)
        + [pl.BlockSpec(memory_space=pltpu.VMEM)] * 2,
        out_specs=[pl.BlockSpec(memory_space=pltpu.VMEM)] * outputs,
        out_shape=[jax.ShapeDtypeStruct((HALF, width), jnp.bfloat16)] * outputs,
        scratch_shapes=[
            pltpu.VMEM((rows, width + PACK), jnp.bfloat16),
            pltpu.VMEM((2, rows, UNITS), jnp.bfloat16),
            pltpu.SemaphoreType.DMA((len(pieces),)),
        ],
        compiler_params=pltpu.CompilerParams(vmem_limit_bytes=EXPERT_VMEM),
        cost_estimate=pl.CostEstimate(
            flops=6 * rows * width * UNITS * 2, bytes_accessed=4 * rows * width, transcendentals=0
        ),
        name="expert",
    )(*pieces, *weights)


def join_kernel(gate_hbm, up_hbm, down_hbm, out_ref, sem):
    width = gate_hbm.shape[0]
    copies = [
        pltpu.make_async_copy(source, out_ref.at[pl.ds(0, width), pl.ds(i * UNITS, UNITS)], sem.at[i])
        for i, source in enumerate((gate_hbm, up_hbm))
    ]
    for i in range(width // DEPTH):
        part = out_ref.at[pl.ds(width + i * UNITS, UNITS)]
        copies.append(pltpu.make_async_copy(down_hbm.at[:, pl.ds(i * DEPTH, DEPTH)], part, sem.at[2 + i]))
    for copy in copies:
        copy.start()
    for copy in copies:
        copy.wait()


def joined(gate, up, down):
    width = gate.shape[0]
    blocks = width // DEPTH
    matrices = [pltpu.with_memory_space_constraint(matrix, pltpu.HBM) for matrix in (gate, up, down)]
    return pl.pallas_call(
        join_kernel,
        in_specs=[pl.BlockSpec(memory_space=pl.ANY)] * 3,
        out_specs=pl.BlockSpec(memory_space=pltpu.VMEM),
        out_shape=pltpu.VMEM((width + blocks * UNITS, DEPTH), jnp.bfloat16),
        scratch_shapes=[pltpu.SemaphoreType.DMA((2 + blocks,))],
        compiler_params=pltpu.CompilerParams(vmem_limit_bytes=KERNEL_VMEM),
        cost_estimate=pl.CostEstimate(flops=0, bytes_accessed=12 * width * UNITS, transcendentals=0),
        name="join",
    )(*matrices)


def pack_kernel(tokens_ref, routes_ref, scores_ref, out_ref):
    rows, width = tokens_ref.shape
    out_ref[:, :width] = tokens_ref[...]
    scores = scores_ref[...]
    weights = scores / jnp.sum(scores, axis=1, keepdims=True) * ROUTE_SCALE
    lane = lax.broadcasted_iota(jnp.int32, (rows, PACK), 1)
    dense = jnp.zeros((rows, PACK), jnp.float32)
    for choice in range(scores.shape[1]):
        named = routes_ref[:, choice : choice + 1] == lane % EXPERTS
        dense += jnp.where(named, weights[:, choice : choice + 1], 0.0)
    high = dense.astype(jnp.bfloat16).astype(jnp.float32)
    extra = jnp.where(lane < EXPERTS, high, jnp.where(lane < 2 * EXPERTS, dense - high, 0.0))
    out_ref[:, width:] = extra.astype(jnp.bfloat16)


def packed_rows(tokens, routes, gate_scores):
    rows, width = tokens.shape
    return pl.pallas_call(
        pack_kernel,
        out_shape=jax.ShapeDtypeStruct((rows, width + PACK), jnp.bfloat16),
        compiler_params=pltpu.CompilerParams(vmem_limit_bytes=KERNEL_VMEM),
        name="pack",
    )(*(pltpu.with_memory_space_constraint(value, pltpu.HBM) for value in (tokens, routes, gate_scores)))


def attention_kernel(
    sequence, length_ref, nope_ref, rope_ref, key_up_ref, value_up_ref, latent_ref, rope_key_ref,
    new_latent_ref, new_rope_ref, out_ref, query_ref, query_rope_ref, top_ref, sum_ref, total_ref,
):
    step = pl.program_id(0)
    length = length_ref[sequence]
    scale = (NOPE + ROPE) ** (-0.5) * LOG2E
    contract_last = (((1,), (1,)), ((), ()))

    def absorb(keys, rope_keys, values, bias):
        rows = HEAD_COUNT * NEW // PARTS
        parts = [slice(part * rows, (part + 1) * rows) for part in range(PARTS)]
        biases = [bias if bias.shape[0] == 1 else bias[part] for part in parts]
        scores = []
        for part, added_bias in zip(parts, biases):
            score = lax.dot_general(query_ref[part, :], keys, contract_last, preferred_element_type=jnp.float32)
            score += jnp.dot(query_rope_ref[part, :], rope_keys, preferred_element_type=jnp.float32)
            scores.append(score * scale + added_bias)
        for part, score in zip(parts, scores):
            old_top = top_ref[part, :]
            top = jnp.maximum(old_top, jnp.max(score, axis=1, keepdims=True))
            shrink = jnp.exp2(old_top - top)
            probs = jnp.exp2(score - top)
            top_ref[part, :] = top
            sum_ref[part, :] = sum_ref[part, :] * shrink + jnp.sum(probs, axis=1, keepdims=True)
            total_ref[part, :] = total_ref[part, :] * shrink + jnp.dot(
                probs.astype(jnp.bfloat16), values, preferred_element_type=jnp.float32
            )

    @pl.when(step == 0)
    def _():
        for head in range(HEAD_COUNT):
            query_ref[head * NEW : (head + 1) * NEW, :] = jnp.dot(
                nope_ref[:, head * NOPE : (head + 1) * NOPE], key_up_ref[head], preferred_element_type=jnp.float32
            ).astype(jnp.bfloat16)
            query_rope_ref[head * NEW : (head + 1) * NEW, :] = rope_ref[:, head * ROPE : (head + 1) * ROPE]
        top_ref[...] = jnp.full_like(top_ref, NEG_BIG)
        sum_ref[...] = jnp.zeros_like(sum_ref)
        total_ref[...] = jnp.zeros_like(total_ref)
        position = lax.broadcasted_iota(jnp.int32, (HEAD_COUNT * NEW, NEW), 0) % NEW
        fresh = lax.broadcasted_iota(jnp.int32, (HEAD_COUNT * NEW, NEW), 1)
        bias = jnp.where(fresh <= position, 0.0, NEG_BIG)
        absorb(new_latent_ref[...], new_rope_ref[:, sequence * NEW : (sequence + 1) * NEW], new_latent_ref[...], bias)

    @pl.when(step * KEY_BLOCK < length)
    def _():
        slot = step * KEY_BLOCK + lax.broadcasted_iota(jnp.int32, (1, KEY_BLOCK), 1)
        bias = jnp.where(slot < length, 0.0, NEG_BIG)
        absorb(latent_ref[...], rope_key_ref[...], latent_ref[...], bias)

    @pl.when(step == pl.num_programs(0) - 1)
    def _():
        latent_out = (total_ref[...] / sum_ref[...]).astype(jnp.bfloat16)
        for head in range(HEAD_COUNT):
            out_ref[:, head * NOPE : (head + 1) * NOPE] = jnp.dot(
                latent_out[head * NEW : (head + 1) * NEW], value_up_ref[head], preferred_element_type=jnp.float32
            ).astype(jnp.bfloat16)


def attend(weight, sequence, length, nope, rope, key_up, value_up, latent_cache, rope_cache, new_latent, new_rope):
    rows = HEAD_COUNT * NEW

    def whole(*shape):
        return pl.BlockSpec(shape, lambda step, length: (0,) * len(shape))

    def live(step, length):
        return (sequence, jnp.minimum(step, (length[sequence] + KEY_BLOCK - 1) // KEY_BLOCK - 1), 0)

    def live_last(step, length):
        sequence_place, block, column = live(step, length)
        return (sequence_place, column, block)

    def own(*shape):
        return pl.BlockSpec(shape, lambda step, length: (sequence,) + (0,) * (len(shape) - 1))

    return pl.pallas_call(
        functools.partial(attention_kernel, sequence),
        grid_spec=pltpu.PrefetchScalarGridSpec(
            num_scalar_prefetch=1,
            grid=(CACHE // KEY_BLOCK,),
            in_specs=[
                own(NEW, HEAD_COUNT * NOPE),
                own(NEW, HEAD_COUNT * ROPE),
                whole(HEAD_COUNT, NOPE, LATENT),
                whole(HEAD_COUNT, LATENT, NOPE),
                pl.BlockSpec((None, KEY_BLOCK, LATENT), live),
                pl.BlockSpec((None, ROPE, KEY_BLOCK), live_last),
                own(NEW, LATENT),
                pl.BlockSpec((ROPE, 2 * NEW), lambda step, length: (0, 0)),
            ],
            out_specs=whole(NEW, HEAD_COUNT * NOPE),
            scratch_shapes=[
                pltpu.VMEM((rows, LATENT), jnp.bfloat16),
                pltpu.VMEM((rows, ROPE), jnp.bfloat16),
                pltpu.VMEM((rows, 1), jnp.float32),
                pltpu.VMEM((rows, 1), jnp.float32),
                pltpu.VMEM((rows, LATENT), jnp.float32),
            ],
        ),
        out_shape=jax.ShapeDtypeStruct((NEW, HEAD_COUNT * NOPE), jnp.bfloat16),
        compiler_params=pltpu.CompilerParams(vmem_limit_bytes=KERNEL_VMEM),
        cost_estimate=pl.CostEstimate(flops=6_000_000_000 // weight, bytes_accessed=8_000_000 // weight, transcendentals=2_100_000 // weight),
        name="attend",
    )(length, nope, rope, key_up, value_up, latent_cache, rope_cache, new_latent, new_rope)


def body(
    tokens,
    routes,
    gate_scores,
    gate_weight,
    up_weight,
    down_weight,
    query_nope,
    query_rope,
    key_up,
    value_up,
    latent_cache,
    rope_cache,
    new_latent,
    new_rope,
    lengths,
):
    packed = packed_rows(tokens, routes, gate_scores)
    gathered = [packed] + [shift(packed, 0, -distance) for distance in (1, 2, 3)]
    packed, gate_weight, up_weight, down_weight = lax.optimization_barrier(
        (packed, gate_weight, up_weight, down_weight)
    )
    own_weights = joined(gate_weight[0], up_weight[0], down_weight[0])
    small = jnp.concatenate(gathered, axis=0)
    small, own_weights = lax.optimization_barrier((small, own_weights))
    weights = (own_weights, with_other_core(own_weights))
    rope_keys, new_rope_keys = jnp.swapaxes(rope_cache, 1, 2), new_rope.T
    latent_cache = pltpu.with_memory_space_constraint(latent_cache, pltpu.HBM)

    def attention(sequence, lengths, weight):
        return attend(
            weight, sequence, lengths, query_nope, query_rope, key_up, value_up, latent_cache, rope_keys, new_latent, new_rope_keys
        )

    above, below = shift(small, 1, -1), shift(small, 1, 1)
    half = small.shape[0] // 2
    own_low = jnp.concatenate([small, above], axis=0)
    below_low, above_low = shift(own_low, 2, 1), shift(own_low, 2, -1)
    far_low, far_high = lax.optimization_barrier((below[:half], above[half:]))
    far_low, far_high = shift(far_low, 1, 1), shift(far_high, 1, -1)
    own_high = jnp.concatenate([far_low, far_high, below], axis=0)
    below_high, above_high = shift(own_high, 2, 1), shift(own_high, 2, -1)
    own_low, own_high, below_low, above_low = lax.optimization_barrier((own_low, own_high, below_low, above_low))
    own_terms = expert_terms([own_low, own_high], weights)
    above_low, relayed, own_terms = lax.optimization_barrier((above_low, below_low, own_terms))
    above_low, below_low = expert_terms([above_low, relayed], weights)
    relayed, above_high, above_low, below_low = lax.optimization_barrier((relayed, above_high, above_low, below_low))
    far_low, far_high = shift(relayed, 2, 1), shift(above_high, 2, -1)
    above_high, below_high = expert_terms([above_high, below_high], weights)
    above_high, below_low = lax.optimization_barrier((above_high, below_low))
    near_high, near_low = shift(above_high, 2, 1), shift(below_low, 2, -1)
    far_low, far_high, above_high, below_low = lax.optimization_barrier((far_low, far_high, above_high, below_low))
    far_terms = expert_terms([far_low, far_high], weights)
    from_below, from_above = shift(far_terms[0], 2, 1), shift(far_terms[1], 2, -1)
    far_terms, lengths = lax.optimization_barrier((far_terms, lengths))
    first_attention = attention(0, lengths, SHORT)
    from_below, from_above, near_high, near_low, first_attention, lengths = lax.optimization_barrier(
        (from_below, from_above, near_high, near_low, first_attention, lengths)
    )
    from_below = shift(narrowed(added(above_low, from_below)), 2, 1)
    from_above = shift(narrowed(added(below_high, from_above)), 2, -1)
    second_attention = attention(1, lengths, LONG)
    from_below, from_above, second_attention = lax.optimization_barrier((from_below, from_above, second_attention))
    low = added(own_terms[0], near_low, from_below)
    high = added(own_terms[1], near_high, from_above)

    size = HALF // 2
    half = size // 2
    above, far, below = low[size:], high[:size], high[size:]
    up_first = narrowed(jnp.concatenate([far[:half], above[half:]], axis=0))
    down_first = narrowed(jnp.concatenate([far[half:], below[:half]], axis=0))
    from_below, from_above = shift(up_first, 1, 1), shift(down_first, 1, -1)
    up_second = narrowed(added(above[:half], from_below[:half]))
    down_second = narrowed(added(below[half:], from_above[:half]))
    up_second, down_second = lax.optimization_barrier((up_second, down_second))
    up_second, down_second = shift(up_second, 1, 1), shift(down_second, 1, -1)
    total = low[:size] + jnp.concatenate(
        [added(up_second, from_above[half:]), added(down_second, from_below[half:])], axis=0
    )

    total = narrowed(total)
    rows = tokens.shape[0]
    arrived = [shift(total[distance * rows : (distance + 1) * rows], 0, distance) for distance in (1, 2, 3)]
    routed_out = narrowed(added(total[:rows], *arrived))
    return (routed_out, jnp.concatenate([first_attention, second_attention], axis=0))


def solution(mesh):
    cube = Mesh(mesh.devices.reshape(4, 2, 4, 4), ("z", "core", "x", "y"))
    node, local = ("z", "core"), ("x", "y")
    every = node + local
    in_specs = (
        P(every, None),
        P(every, None),
        P(every, None),
        P(local, None, node),
        P(local, None, node),
        P(local, node, None),
        P(node, local),
        P(node, local),
        P(local, None, None),
        P(local, None, None),
        P(node, None, None),
        P(node, None, None),
        P(node, None),
        P(node, None),
        P(node),
    )
    out_specs = (P(every, None), P(node, local))
    return jax.shard_map(body, mesh=cube, in_specs=in_specs, out_specs=out_specs, check_vma=False)
```

```python
import functools

import jax
import jax.numpy as jnp
import numpy as np
from jax import lax
from jax.experimental import pallas as pl
from jax.experimental.pallas import tpu as pltpu
from jax.sharding import Mesh, PartitionSpec as P

NOPE = 128
ROPE = 64
NEW = 64
CACHE = 4096
EXPERTS = 16
ROUTE_SCALE = 2.5
NEG_BIG = -1e30
AXES = ("z", "core", "x", "y")
SIZES = (4, 2, 4, 4)
RING = 4
ORDERS = ((0, 3, 2), (2, 0, 3))
KERNEL_VMEM = 12 * 1024 * 1024
EXPERT_VMEM = 10 * 1024 * 1024
PACK = 128
DEPTH = 512
UNITS = 256
HALF = 64
KEY_BLOCK = 1024
HEAD_COUNT = 8
SHORT, LONG = 60, 1
PARTS = 2
LATENT = 512
LOG2E = 1.4426950408889634


def shift(value, phase, distance):
    pairs = []
    for place in np.ndindex(*SIZES):
        target = list(place)
        axis = ORDERS[place[1]][phase]
        target[axis] = (target[axis] + distance) % RING
        pairs.append((int(np.ravel_multi_index(place, SIZES)), int(np.ravel_multi_index(target, SIZES))))
    return lax.ppermute(value, AXES, pairs)


def widened(value):
    return value.astype(jnp.float32)


def narrowed(value):
    return value.astype(jnp.bfloat16)


def added(*values):
    return sum(widened(value) for value in values)


def with_other_core(value):
    return lax.ppermute(value, "core", [(0, 1), (1, 0)])


def expert_kernel(*refs, sources, outputs):
    row_hbm = refs[:sources]
    matrices = refs[sources : sources + 2]
    out_refs = refs[sources + 2 : sources + 2 + outputs]
    rows_ref, hidden_ref, row_sem = refs[sources + 2 + outputs :]
    width = out_refs[0].shape[1]
    span = rows_ref.shape[0] // sources
    row_copies = [
        pltpu.make_async_copy(source, rows_ref.at[pl.ds(i * span, span)], row_sem.at[i])
        for i, source in enumerate(row_hbm)
    ]
    for copy in row_copies:
        copy.start()
    for copy in row_copies:
        copy.wait()
    extra = rows_ref[:, width : width + PACK].astype(jnp.float32)
    lane = lax.broadcasted_iota(jnp.int32, extra.shape, 1)
    expert = lax.axis_index("x") * RING + lax.axis_index("y")
    pick = (lane % EXPERTS == expert) & (lane < 2 * EXPERTS)
    coefficient = jnp.sum(jnp.where(pick, extra, 0.0), axis=1, keepdims=True)
    for i, matrix in enumerate(matrices):
        sums = sum(
            jnp.dot(rows_ref[:, k : k + 2 * DEPTH], matrix[k : k + 2 * DEPTH, :], preferred_element_type=jnp.float32)
            for k in range(0, width, 2 * DEPTH)
        )
        gate, up = sums[:, :UNITS], sums[:, UNITS:]
        hidden = gate / (1.0 + jnp.exp(-gate)) * up * coefficient
        hidden_ref[i] = jnp.where(coefficient > 0, hidden, 0.0).astype(jnp.bfloat16)
    for block in range(width // DEPTH):
        part, place = slice(block * DEPTH, (block + 1) * DEPTH), slice(width + block * UNITS, width + (block + 1) * UNITS)
        result = jnp.dot(hidden_ref[0], matrices[0][place, :], preferred_element_type=jnp.float32)
        result += jnp.dot(hidden_ref[1], matrices[1][place, :], preferred_element_type=jnp.float32)
        result = result.astype(jnp.bfloat16)
        for i, out_ref in enumerate(out_refs):
            out_ref[:, part] = result[i * HALF : (i + 1) * HALF]


def expert_terms(pieces, weights):
    width = pieces[0].shape[1] - PACK
    rows = sum(piece.shape[0] for piece in pieces)
    outputs = rows // HALF
    weights = [pltpu.with_memory_space_constraint(matrix, pltpu.VMEM) for matrix in weights]
    return pl.pallas_call(
        functools.partial(expert_kernel, sources=len(pieces), outputs=outputs),
        in_specs=[pl.BlockSpec(memory_space=pl.ANY)] * len(pieces)
        + [pl.BlockSpec(memory_space=pltpu.VMEM)] * 2,
        out_specs=[pl.BlockSpec(memory_space=pltpu.VMEM)] * outputs,
        out_shape=[jax.ShapeDtypeStruct((HALF, width), jnp.bfloat16)] * outputs,
        scratch_shapes=[
            pltpu.VMEM((rows, width + PACK), jnp.bfloat16),
            pltpu.VMEM((2, rows, UNITS), jnp.bfloat16),
            pltpu.SemaphoreType.DMA((len(pieces),)),
        ],
        compiler_params=pltpu.CompilerParams(vmem_limit_bytes=EXPERT_VMEM),
        cost_estimate=pl.CostEstimate(
            flops=6 * rows * width * UNITS * 2, bytes_accessed=4 * rows * width, transcendentals=0
        ),
        name="expert",
    )(*pieces, *weights)


def join_kernel(gate_hbm, up_hbm, down_hbm, out_ref, sem):
    width = gate_hbm.shape[0]
    copies = [
        pltpu.make_async_copy(source, out_ref.at[pl.ds(0, width), pl.ds(i * UNITS, UNITS)], sem.at[i])
        for i, source in enumerate((gate_hbm, up_hbm))
    ]
    for i in range(width // DEPTH):
        part = out_ref.at[pl.ds(width + i * UNITS, UNITS)]
        copies.append(pltpu.make_async_copy(down_hbm.at[:, pl.ds(i * DEPTH, DEPTH)], part, sem.at[2 + i]))
    for copy in copies:
        copy.start()
    for copy in copies:
        copy.wait()


def joined(gate, up, down):
    width = gate.shape[0]
    blocks = width // DEPTH
    matrices = [pltpu.with_memory_space_constraint(matrix, pltpu.HBM) for matrix in (gate, up, down)]
    return pl.pallas_call(
        join_kernel,
        in_specs=[pl.BlockSpec(memory_space=pl.ANY)] * 3,
        out_specs=pl.BlockSpec(memory_space=pltpu.VMEM),
        out_shape=pltpu.VMEM((width + blocks * UNITS, DEPTH), jnp.bfloat16),
        scratch_shapes=[pltpu.SemaphoreType.DMA((2 + blocks,))],
        compiler_params=pltpu.CompilerParams(vmem_limit_bytes=KERNEL_VMEM),
        cost_estimate=pl.CostEstimate(flops=0, bytes_accessed=12 * width * UNITS, transcendentals=0),
        name="join",
    )(*matrices)


def pack_kernel(tokens_ref, routes_ref, scores_ref, out_ref):
    rows, width = tokens_ref.shape
    out_ref[:, :width] = tokens_ref[...]
    scores = scores_ref[...]
    weights = scores / jnp.sum(scores, axis=1, keepdims=True) * ROUTE_SCALE
    lane = lax.broadcasted_iota(jnp.int32, (rows, PACK), 1)
    dense = jnp.zeros((rows, PACK), jnp.float32)
    for choice in range(scores.shape[1]):
        named = routes_ref[:, choice : choice + 1] == lane % EXPERTS
        dense += jnp.where(named, weights[:, choice : choice + 1], 0.0)
    high = dense.astype(jnp.bfloat16).astype(jnp.float32)
    extra = jnp.where(lane < EXPERTS, high, jnp.where(lane < 2 * EXPERTS, dense - high, 0.0))
    out_ref[:, width:] = extra.astype(jnp.bfloat16)


def packed_rows(tokens, routes, gate_scores):
    rows, width = tokens.shape
    return pl.pallas_call(
        pack_kernel,
        out_shape=jax.ShapeDtypeStruct((rows, width + PACK), jnp.bfloat16),
        compiler_params=pltpu.CompilerParams(vmem_limit_bytes=KERNEL_VMEM),
        name="pack",
    )(*(pltpu.with_memory_space_constraint(value, pltpu.HBM) for value in (tokens, routes, gate_scores)))


def attention_kernel(
    sequence, length_ref, nope_ref, rope_ref, key_up_ref, value_up_ref, latent_ref, rope_key_ref,
    new_latent_ref, new_rope_ref, out_ref, query_ref, query_rope_ref, top_ref, sum_ref, total_ref,
):
    step = pl.program_id(0)
    length = length_ref[sequence]
    scale = (NOPE + ROPE) ** (-0.5) * LOG2E
    contract_last = (((1,), (1,)), ((), ()))

    def absorb(keys, rope_keys, values, bias):
        rows = HEAD_COUNT * NEW // PARTS
        parts = [slice(part * rows, (part + 1) * rows) for part in range(PARTS)]
        biases = [bias if bias.shape[0] == 1 else bias[part] for part in parts]
        scores = []
        for part, added_bias in zip(parts, biases):
            score = lax.dot_general(query_ref[part, :], keys, contract_last, preferred_element_type=jnp.float32)
            score += jnp.dot(query_rope_ref[part, :], rope_keys, preferred_element_type=jnp.float32)
            scores.append(score * scale + added_bias)
        for part, score in zip(parts, scores):
            old_top = top_ref[part, :]
            top = jnp.maximum(old_top, jnp.max(score, axis=1, keepdims=True))
            shrink = jnp.exp2(old_top - top)
            probs = jnp.exp2(score - top)
            top_ref[part, :] = top
            sum_ref[part, :] = sum_ref[part, :] * shrink + jnp.sum(probs, axis=1, keepdims=True)
            total_ref[part, :] = total_ref[part, :] * shrink + jnp.dot(
                probs.astype(jnp.bfloat16), values, preferred_element_type=jnp.float32
            )

    @pl.when(step == 0)
    def _():
        for head in range(HEAD_COUNT):
            query_ref[head * NEW : (head + 1) * NEW, :] = jnp.dot(
                nope_ref[:, head * NOPE : (head + 1) * NOPE], key_up_ref[head], preferred_element_type=jnp.float32
            ).astype(jnp.bfloat16)
            query_rope_ref[head * NEW : (head + 1) * NEW, :] = rope_ref[:, head * ROPE : (head + 1) * ROPE]
        top_ref[...] = jnp.full_like(top_ref, NEG_BIG)
        sum_ref[...] = jnp.zeros_like(sum_ref)
        total_ref[...] = jnp.zeros_like(total_ref)
        position = lax.broadcasted_iota(jnp.int32, (HEAD_COUNT * NEW, NEW), 0) % NEW
        fresh = lax.broadcasted_iota(jnp.int32, (HEAD_COUNT * NEW, NEW), 1)
        bias = jnp.where(fresh <= position, 0.0, NEG_BIG)
        absorb(new_latent_ref[...], new_rope_ref[:, sequence * NEW : (sequence + 1) * NEW], new_latent_ref[...], bias)

    @pl.when(step * KEY_BLOCK < length)
    def _():
        slot = step * KEY_BLOCK + lax.broadcasted_iota(jnp.int32, (1, KEY_BLOCK), 1)
        bias = jnp.where(slot < length, 0.0, NEG_BIG)
        absorb(latent_ref[...], rope_key_ref[...], latent_ref[...], bias)

    @pl.when(step == pl.num_programs(0) - 1)
    def _():
        latent_out = (total_ref[...] / sum_ref[...]).astype(jnp.bfloat16)
        for head in range(HEAD_COUNT):
            out_ref[:, head * NOPE : (head + 1) * NOPE] = jnp.dot(
                latent_out[head * NEW : (head + 1) * NEW], value_up_ref[head], preferred_element_type=jnp.float32
            ).astype(jnp.bfloat16)


def attend(weight, sequence, length, nope, rope, key_up, value_up, latent_cache, rope_cache, new_latent, new_rope):
    rows = HEAD_COUNT * NEW

    def whole(*shape):
        return pl.BlockSpec(shape, lambda step, length: (0,) * len(shape))

    def live(step, length):
        return (sequence, jnp.minimum(step, (length[sequence] + KEY_BLOCK - 1) // KEY_BLOCK - 1), 0)

    def live_last(step, length):
        sequence_place, block, column = live(step, length)
        return (sequence_place, column, block)

    def own(*shape):
        return pl.BlockSpec(shape, lambda step, length: (sequence,) + (0,) * (len(shape) - 1))

    return pl.pallas_call(
        functools.partial(attention_kernel, sequence),
        grid_spec=pltpu.PrefetchScalarGridSpec(
            num_scalar_prefetch=1,
            grid=(CACHE // KEY_BLOCK,),
            in_specs=[
                own(NEW, HEAD_COUNT * NOPE),
                own(NEW, HEAD_COUNT * ROPE),
                whole(HEAD_COUNT, NOPE, LATENT),
                whole(HEAD_COUNT, LATENT, NOPE),
                pl.BlockSpec((None, KEY_BLOCK, LATENT), live),
                pl.BlockSpec((None, ROPE, KEY_BLOCK), live_last),
                own(NEW, LATENT),
                pl.BlockSpec((ROPE, 2 * NEW), lambda step, length: (0, 0)),
            ],
            out_specs=whole(NEW, HEAD_COUNT * NOPE),
            scratch_shapes=[
                pltpu.VMEM((rows, LATENT), jnp.bfloat16),
                pltpu.VMEM((rows, ROPE), jnp.bfloat16),
                pltpu.VMEM((rows, 1), jnp.float32),
                pltpu.VMEM((rows, 1), jnp.float32),
                pltpu.VMEM((rows, LATENT), jnp.float32),
            ],
        ),
        out_shape=jax.ShapeDtypeStruct((NEW, HEAD_COUNT * NOPE), jnp.bfloat16),
        compiler_params=pltpu.CompilerParams(vmem_limit_bytes=KERNEL_VMEM),
        cost_estimate=pl.CostEstimate(flops=6_000_000_000 // weight, bytes_accessed=8_000_000 // weight, transcendentals=2_100_000 // weight),
        name="attend",
    )(length, nope, rope, key_up, value_up, latent_cache, rope_cache, new_latent, new_rope)


def body(
    tokens,
    routes,
    gate_scores,
    gate_weight,
    up_weight,
    down_weight,
    query_nope,
    query_rope,
    key_up,
    value_up,
    latent_cache,
    rope_cache,
    new_latent,
    new_rope,
    lengths,
):
    packed = packed_rows(tokens, routes, gate_scores)
    gathered = [packed] + [shift(packed, 0, -distance) for distance in (1, 2, 3)]
    packed, gate_weight, up_weight, down_weight = lax.optimization_barrier(
        (packed, gate_weight, up_weight, down_weight)
    )
    own_weights = joined(gate_weight[0], up_weight[0], down_weight[0])
    small = jnp.concatenate(gathered, axis=0)
    small, own_weights = lax.optimization_barrier((small, own_weights))
    weights = (own_weights, with_other_core(own_weights))
    rope_keys, new_rope_keys = jnp.swapaxes(rope_cache, 1, 2), new_rope.T
    latent_cache = pltpu.with_memory_space_constraint(latent_cache, pltpu.HBM)

    def attention(sequence, lengths, weight):
        return attend(
            weight, sequence, lengths, query_nope, query_rope, key_up, value_up, latent_cache, rope_keys, new_latent, new_rope_keys
        )

    above, below = shift(small, 1, -1), shift(small, 1, 1)
    half = small.shape[0] // 2
    own_low = jnp.concatenate([small, above], axis=0)
    below_low, above_low = shift(own_low, 2, 1), shift(own_low, 2, -1)
    far_low, far_high = lax.optimization_barrier((below[:half], above[half:]))
    far_low, far_high = shift(far_low, 1, 1), shift(far_high, 1, -1)
    own_high = jnp.concatenate([far_low, far_high, below], axis=0)
    below_high, above_high = shift(own_high, 2, 1), shift(own_high, 2, -1)
    own_low, own_high, below_low, above_low = lax.optimization_barrier((own_low, own_high, below_low, above_low))
    own_terms = expert_terms([own_low, own_high], weights)
    above_low, relayed, own_terms = lax.optimization_barrier((above_low, below_low, own_terms))
    above_low, below_low = expert_terms([above_low, relayed], weights)
    far_low = shift(relayed, 2, 1)
    above_high, above_low, below_low = lax.optimization_barrier((above_high, above_low, below_low))
    far_high = shift(above_high, 2, -1)
    above_high, below_high = expert_terms([above_high, below_high], weights)
    above_high, below_low = lax.optimization_barrier((above_high, below_low))
    near_high, near_low = shift(above_high, 2, 1), shift(below_low, 2, -1)
    far_low, far_high, above_high, below_low = lax.optimization_barrier((far_low, far_high, above_high, below_low))
    far_terms = expert_terms([far_low, far_high], weights)
    from_below, from_above = shift(far_terms[0], 2, 1), shift(far_terms[1], 2, -1)
    far_terms, lengths = lax.optimization_barrier((far_terms, lengths))
    first_attention = attention(0, lengths, SHORT)
    from_below, from_above, near_high, near_low, first_attention, lengths = lax.optimization_barrier(
        (from_below, from_above, near_high, near_low, first_attention, lengths)
    )
    from_below = shift(narrowed(added(above_low, from_below)), 2, 1)
    from_above = shift(narrowed(added(below_high, from_above)), 2, -1)
    second_attention = attention(1, lengths, LONG)
    from_below, from_above, second_attention = lax.optimization_barrier((from_below, from_above, second_attention))
    low = added(own_terms[0], near_low, from_below)
    high = added(own_terms[1], near_high, from_above)

    size = HALF // 2
    half = size // 2
    above, far, below = low[size:], high[:size], high[size:]
    up_first = narrowed(jnp.concatenate([far[:half], above[half:]], axis=0))
    down_first = narrowed(jnp.concatenate([far[half:], below[:half]], axis=0))
    from_below, from_above = shift(up_first, 1, 1), shift(down_first, 1, -1)
    up_second = narrowed(added(above[:half], from_below[:half]))
    down_second = narrowed(added(below[half:], from_above[:half]))
    up_second, down_second = lax.optimization_barrier((up_second, down_second))
    up_second, down_second = shift(up_second, 1, 1), shift(down_second, 1, -1)
    total = low[:size] + jnp.concatenate(
        [added(up_second, from_above[half:]), added(down_second, from_below[half:])], axis=0
    )

    total = narrowed(total)
    rows = tokens.shape[0]
    arrived = [shift(total[distance * rows : (distance + 1) * rows], 0, distance) for distance in (1, 2, 3)]
    routed_out = narrowed(added(total[:rows], *arrived))
    return (routed_out, jnp.concatenate([first_attention, second_attention], axis=0))


def solution(mesh):
    cube = Mesh(mesh.devices.reshape(4, 2, 4, 4), ("z", "core", "x", "y"))
    node, local = ("z", "core"), ("x", "y")
    every = node + local
    in_specs = (
        P(every, None),
        P(every, None),
        P(every, None),
        P(local, None, node),
        P(local, None, node),
        P(local, node, None),
        P(node, local),
        P(node, local),
        P(local, None, None),
        P(local, None, None),
        P(node, None, None),
        P(node, None, None),
        P(node, None),
        P(node, None),
        P(node),
    )
    out_specs = (P(every, None), P(node, local))
    return jax.shard_map(body, mesh=cube, in_specs=in_specs, out_specs=out_specs, check_vma=False)
```

```python
import functools

import jax
import jax.numpy as jnp
import numpy as np
from jax import lax
from jax.experimental import pallas as pl
from jax.experimental.pallas import tpu as pltpu
from jax.sharding import Mesh, PartitionSpec as P

NOPE = 128
ROPE = 64
NEW = 64
CACHE = 4096
EXPERTS = 16
ROUTE_SCALE = 2.5
NEG_BIG = -1e30
AXES = ("z", "core", "x", "y")
SIZES = (4, 2, 4, 4)
RING = 4
ORDERS = ((3, 0, 2), (2, 0, 3))
KERNEL_VMEM = 12 * 1024 * 1024
EXPERT_VMEM = 10 * 1024 * 1024
PACK = 128
DEPTH = 512
UNITS = 256
HALF = 64
KEY_BLOCK = 1024
HEAD_COUNT = 8
SHORT, LONG = 60, 1
PARTS = 2
LATENT = 512
LOG2E = 1.4426950408889634


def shift(value, phase, distance):
    pairs = []
    for place in np.ndindex(*SIZES):
        target = list(place)
        axis = ORDERS[place[1]][phase]
        target[axis] = (target[axis] + distance) % RING
        pairs.append((int(np.ravel_multi_index(place, SIZES)), int(np.ravel_multi_index(target, SIZES))))
    return lax.ppermute(value, AXES, pairs)


def widened(value):
    return value.astype(jnp.float32)


def narrowed(value):
    return value.astype(jnp.bfloat16)


def added(*values):
    return sum(widened(value) for value in values)


def with_other_core(value):
    return lax.ppermute(value, "core", [(0, 1), (1, 0)])


def expert_kernel(*refs, sources, outputs):
    row_hbm = refs[:sources]
    matrices = refs[sources : sources + 2]
    out_refs = refs[sources + 2 : sources + 2 + outputs]
    rows_ref, hidden_ref, row_sem = refs[sources + 2 + outputs :]
    width = out_refs[0].shape[1]
    span = rows_ref.shape[0] // sources
    row_copies = [
        pltpu.make_async_copy(source, rows_ref.at[pl.ds(i * span, span)], row_sem.at[i])
        for i, source in enumerate(row_hbm)
    ]
    for copy in row_copies:
        copy.start()
    for copy in row_copies:
        copy.wait()
    extra = rows_ref[:, width : width + PACK].astype(jnp.float32)
    lane = lax.broadcasted_iota(jnp.int32, extra.shape, 1)
    expert = lax.axis_index("x") * RING + lax.axis_index("y")
    pick = (lane % EXPERTS == expert) & (lane < 2 * EXPERTS)
    coefficient = jnp.sum(jnp.where(pick, extra, 0.0), axis=1, keepdims=True)
    for i, matrix in enumerate(matrices):
        sums = sum(
            jnp.dot(rows_ref[:, k : k + 2 * DEPTH], matrix[k : k + 2 * DEPTH, :], preferred_element_type=jnp.float32)
            for k in range(0, width, 2 * DEPTH)
        )
        gate, up = sums[:, :UNITS], sums[:, UNITS:]
        hidden = gate / (1.0 + jnp.exp(-gate)) * up * coefficient
        hidden_ref[i] = jnp.where(coefficient > 0, hidden, 0.0).astype(jnp.bfloat16)
    for block in range(width // DEPTH):
        part, place = slice(block * DEPTH, (block + 1) * DEPTH), slice(width + block * UNITS, width + (block + 1) * UNITS)
        result = jnp.dot(hidden_ref[0], matrices[0][place, :], preferred_element_type=jnp.float32)
        result += jnp.dot(hidden_ref[1], matrices[1][place, :], preferred_element_type=jnp.float32)
        result = result.astype(jnp.bfloat16)
        for i, out_ref in enumerate(out_refs):
            out_ref[:, part] = result[i * HALF : (i + 1) * HALF]


def expert_terms(pieces, weights):
    width = pieces[0].shape[1] - PACK
    rows = sum(piece.shape[0] for piece in pieces)
    outputs = rows // HALF
    weights = [pltpu.with_memory_space_constraint(matrix, pltpu.VMEM) for matrix in weights]
    return pl.pallas_call(
        functools.partial(expert_kernel, sources=len(pieces), outputs=outputs),
        in_specs=[pl.BlockSpec(memory_space=pl.ANY)] * len(pieces)
        + [pl.BlockSpec(memory_space=pltpu.VMEM)] * 2,
        out_specs=[pl.BlockSpec(memory_space=pltpu.VMEM)] * outputs,
        out_shape=[jax.ShapeDtypeStruct((HALF, width), jnp.bfloat16)] * outputs,
        scratch_shapes=[
            pltpu.VMEM((rows, width + PACK), jnp.bfloat16),
            pltpu.VMEM((2, rows, UNITS), jnp.bfloat16),
            pltpu.SemaphoreType.DMA((len(pieces),)),
        ],
        compiler_params=pltpu.CompilerParams(vmem_limit_bytes=EXPERT_VMEM),
        cost_estimate=pl.CostEstimate(
            flops=6 * rows * width * UNITS * 2, bytes_accessed=4 * rows * width, transcendentals=0
        ),
        name="expert",
    )(*pieces, *weights)


def join_kernel(gate_hbm, up_hbm, down_hbm, out_ref, sem):
    width = gate_hbm.shape[0]
    copies = [
        pltpu.make_async_copy(source, out_ref.at[pl.ds(0, width), pl.ds(i * UNITS, UNITS)], sem.at[i])
        for i, source in enumerate((gate_hbm, up_hbm))
    ]
    for i in range(width // DEPTH):
        part = out_ref.at[pl.ds(width + i * UNITS, UNITS)]
        copies.append(pltpu.make_async_copy(down_hbm.at[:, pl.ds(i * DEPTH, DEPTH)], part, sem.at[2 + i]))
    for copy in copies:
        copy.start()
    for copy in copies:
        copy.wait()


def joined(gate, up, down):
    width = gate.shape[0]
    blocks = width // DEPTH
    matrices = [pltpu.with_memory_space_constraint(matrix, pltpu.HBM) for matrix in (gate, up, down)]
    return pl.pallas_call(
        join_kernel,
        in_specs=[pl.BlockSpec(memory_space=pl.ANY)] * 3,
        out_specs=pl.BlockSpec(memory_space=pltpu.VMEM),
        out_shape=pltpu.VMEM((width + blocks * UNITS, DEPTH), jnp.bfloat16),
        scratch_shapes=[pltpu.SemaphoreType.DMA((2 + blocks,))],
        compiler_params=pltpu.CompilerParams(vmem_limit_bytes=KERNEL_VMEM),
        cost_estimate=pl.CostEstimate(flops=0, bytes_accessed=12 * width * UNITS, transcendentals=0),
        name="join",
    )(*matrices)


def pack_kernel(tokens_ref, routes_ref, scores_ref, out_ref):
    rows, width = tokens_ref.shape
    out_ref[:, :width] = tokens_ref[...]
    scores = scores_ref[...]
    weights = scores / jnp.sum(scores, axis=1, keepdims=True) * ROUTE_SCALE
    lane = lax.broadcasted_iota(jnp.int32, (rows, PACK), 1)
    dense = jnp.zeros((rows, PACK), jnp.float32)
    for choice in range(scores.shape[1]):
        named = routes_ref[:, choice : choice + 1] == lane % EXPERTS
        dense += jnp.where(named, weights[:, choice : choice + 1], 0.0)
    high = dense.astype(jnp.bfloat16).astype(jnp.float32)
    extra = jnp.where(lane < EXPERTS, high, jnp.where(lane < 2 * EXPERTS, dense - high, 0.0))
    out_ref[:, width:] = extra.astype(jnp.bfloat16)


def packed_rows(tokens, routes, gate_scores):
    rows, width = tokens.shape
    return pl.pallas_call(
        pack_kernel,
        out_shape=jax.ShapeDtypeStruct((rows, width + PACK), jnp.bfloat16),
        compiler_params=pltpu.CompilerParams(vmem_limit_bytes=KERNEL_VMEM),
        name="pack",
    )(*(pltpu.with_memory_space_constraint(value, pltpu.HBM) for value in (tokens, routes, gate_scores)))


def attention_kernel(
    sequence, length_ref, nope_ref, rope_ref, key_up_ref, value_up_ref, latent_ref, rope_key_ref,
    new_latent_ref, new_rope_ref, out_ref, query_ref, query_rope_ref, top_ref, sum_ref, total_ref,
):
    step = pl.program_id(0)
    length = length_ref[sequence]
    scale = (NOPE + ROPE) ** (-0.5) * LOG2E
    contract_last = (((1,), (1,)), ((), ()))

    def absorb(keys, rope_keys, values, bias):
        rows = HEAD_COUNT * NEW // PARTS
        parts = [slice(part * rows, (part + 1) * rows) for part in range(PARTS)]
        biases = [bias if bias.shape[0] == 1 else bias[part] for part in parts]
        scores = []
        for part, added_bias in zip(parts, biases):
            score = lax.dot_general(query_ref[part, :], keys, contract_last, preferred_element_type=jnp.float32)
            score += jnp.dot(query_rope_ref[part, :], rope_keys, preferred_element_type=jnp.float32)
            scores.append(score * scale + added_bias)
        for part, score in zip(parts, scores):
            old_top = top_ref[part, :]
            top = jnp.maximum(old_top, jnp.max(score, axis=1, keepdims=True))
            shrink = jnp.exp2(old_top - top)
            probs = jnp.exp2(score - top)
            top_ref[part, :] = top
            sum_ref[part, :] = sum_ref[part, :] * shrink + jnp.sum(probs, axis=1, keepdims=True)
            total_ref[part, :] = total_ref[part, :] * shrink + jnp.dot(
                probs.astype(jnp.bfloat16), values, preferred_element_type=jnp.float32
            )

    @pl.when(step == 0)
    def _():
        for head in range(HEAD_COUNT):
            query_ref[head * NEW : (head + 1) * NEW, :] = jnp.dot(
                nope_ref[:, head * NOPE : (head + 1) * NOPE], key_up_ref[head], preferred_element_type=jnp.float32
            ).astype(jnp.bfloat16)
            query_rope_ref[head * NEW : (head + 1) * NEW, :] = rope_ref[:, head * ROPE : (head + 1) * ROPE]
        top_ref[...] = jnp.full_like(top_ref, NEG_BIG)
        sum_ref[...] = jnp.zeros_like(sum_ref)
        total_ref[...] = jnp.zeros_like(total_ref)
        position = lax.broadcasted_iota(jnp.int32, (HEAD_COUNT * NEW, NEW), 0) % NEW
        fresh = lax.broadcasted_iota(jnp.int32, (HEAD_COUNT * NEW, NEW), 1)
        bias = jnp.where(fresh <= position, 0.0, NEG_BIG)
        absorb(new_latent_ref[...], new_rope_ref[:, sequence * NEW : (sequence + 1) * NEW], new_latent_ref[...], bias)

    @pl.when(step * KEY_BLOCK < length)
    def _():
        slot = step * KEY_BLOCK + lax.broadcasted_iota(jnp.int32, (1, KEY_BLOCK), 1)
        bias = jnp.where(slot < length, 0.0, NEG_BIG)
        absorb(latent_ref[...], rope_key_ref[...], latent_ref[...], bias)

    @pl.when(step == pl.num_programs(0) - 1)
    def _():
        latent_out = (total_ref[...] / sum_ref[...]).astype(jnp.bfloat16)
        for head in range(HEAD_COUNT):
            out_ref[:, head * NOPE : (head + 1) * NOPE] = jnp.dot(
                latent_out[head * NEW : (head + 1) * NEW], value_up_ref[head], preferred_element_type=jnp.float32
            ).astype(jnp.bfloat16)


def attend(weight, sequence, length, nope, rope, key_up, value_up, latent_cache, rope_cache, new_latent, new_rope):
    rows = HEAD_COUNT * NEW

    def whole(*shape):
        return pl.BlockSpec(shape, lambda step, length: (0,) * len(shape))

    def live(step, length):
        return (sequence, jnp.minimum(step, (length[sequence] + KEY_BLOCK - 1) // KEY_BLOCK - 1), 0)

    def live_last(step, length):
        sequence_place, block, column = live(step, length)
        return (sequence_place, column, block)

    def own(*shape):
        return pl.BlockSpec(shape, lambda step, length: (sequence,) + (0,) * (len(shape) - 1))

    return pl.pallas_call(
        functools.partial(attention_kernel, sequence),
        grid_spec=pltpu.PrefetchScalarGridSpec(
            num_scalar_prefetch=1,
            grid=(CACHE // KEY_BLOCK,),
            in_specs=[
                own(NEW, HEAD_COUNT * NOPE),
                own(NEW, HEAD_COUNT * ROPE),
                whole(HEAD_COUNT, NOPE, LATENT),
                whole(HEAD_COUNT, LATENT, NOPE),
                pl.BlockSpec((None, KEY_BLOCK, LATENT), live),
                pl.BlockSpec((None, ROPE, KEY_BLOCK), live_last),
                own(NEW, LATENT),
                pl.BlockSpec((ROPE, 2 * NEW), lambda step, length: (0, 0)),
            ],
            out_specs=whole(NEW, HEAD_COUNT * NOPE),
            scratch_shapes=[
                pltpu.VMEM((rows, LATENT), jnp.bfloat16),
                pltpu.VMEM((rows, ROPE), jnp.bfloat16),
                pltpu.VMEM((rows, 1), jnp.float32),
                pltpu.VMEM((rows, 1), jnp.float32),
                pltpu.VMEM((rows, LATENT), jnp.float32),
            ],
        ),
        out_shape=jax.ShapeDtypeStruct((NEW, HEAD_COUNT * NOPE), jnp.bfloat16),
        compiler_params=pltpu.CompilerParams(vmem_limit_bytes=KERNEL_VMEM),
        cost_estimate=pl.CostEstimate(flops=6_000_000_000 // weight, bytes_accessed=8_000_000 // weight, transcendentals=2_100_000 // weight),
        name="attend",
    )(length, nope, rope, key_up, value_up, latent_cache, rope_cache, new_latent, new_rope)


def body(
    tokens,
    routes,
    gate_scores,
    gate_weight,
    up_weight,
    down_weight,
    query_nope,
    query_rope,
    key_up,
    value_up,
    latent_cache,
    rope_cache,
    new_latent,
    new_rope,
    lengths,
):
    packed = packed_rows(tokens, routes, gate_scores)
    gathered = [packed] + [shift(packed, 0, -distance) for distance in (1, 2, 3)]
    packed, gate_weight, up_weight, down_weight = lax.optimization_barrier(
        (packed, gate_weight, up_weight, down_weight)
    )
    own_weights = joined(gate_weight[0], up_weight[0], down_weight[0])
    small = jnp.concatenate(gathered, axis=0)
    small, own_weights = lax.optimization_barrier((small, own_weights))
    weights = (own_weights, with_other_core(own_weights))
    rope_keys, new_rope_keys = jnp.swapaxes(rope_cache, 1, 2), new_rope.T
    latent_cache = pltpu.with_memory_space_constraint(latent_cache, pltpu.HBM)

    def attention(sequence, lengths, weight):
        return attend(
            weight, sequence, lengths, query_nope, query_rope, key_up, value_up, latent_cache, rope_keys, new_latent, new_rope_keys
        )

    above, below = shift(small, 1, -1), shift(small, 1, 1)
    half = small.shape[0] // 2
    own_low = jnp.concatenate([small, above], axis=0)
    below_low, above_low = shift(own_low, 2, 1), shift(own_low, 2, -1)
    far_low, far_high = lax.optimization_barrier((below[:half], above[half:]))
    far_low, far_high = shift(far_low, 1, 1), shift(far_high, 1, -1)
    own_high = jnp.concatenate([far_low, far_high, below], axis=0)
    below_high, above_high = shift(own_high, 2, 1), shift(own_high, 2, -1)
    own_low, own_high, below_low, above_low = lax.optimization_barrier((own_low, own_high, below_low, above_low))
    own_terms = expert_terms([own_low, own_high], weights)
    above_low, relayed, own_terms = lax.optimization_barrier((above_low, below_low, own_terms))
    above_low, below_low = expert_terms([above_low, relayed], weights)
    relayed, above_high, above_low, below_low = lax.optimization_barrier((relayed, above_high, above_low, below_low))
    far_low, far_high = shift(relayed, 2, 1), shift(above_high, 2, -1)
    above_high, below_high = expert_terms([above_high, below_high], weights)
    above_high, below_low = lax.optimization_barrier((above_high, below_low))
    near_high, near_low = shift(above_high, 2, 1), shift(below_low, 2, -1)
    far_low, far_high, above_high, below_low = lax.optimization_barrier((far_low, far_high, above_high, below_low))
    far_terms = expert_terms([far_low, far_high], weights)
    from_below, from_above = shift(far_terms[0], 2, 1), shift(far_terms[1], 2, -1)
    far_terms, lengths = lax.optimization_barrier((far_terms, lengths))
    first_attention = attention(0, lengths, SHORT)
    from_below, from_above, near_high, near_low, first_attention, lengths = lax.optimization_barrier(
        (from_below, from_above, near_high, near_low, first_attention, lengths)
    )
    from_below = shift(narrowed(added(above_low, from_below)), 2, 1)
    from_above = shift(narrowed(added(below_high, from_above)), 2, -1)
    second_attention = attention(1, lengths, LONG)
    from_below, from_above, second_attention = lax.optimization_barrier((from_below, from_above, second_attention))
    low = added(own_terms[0], near_low, from_below)
    high = added(own_terms[1], near_high, from_above)

    size = HALF // 2
    half = size // 2
    above, far, below = low[size:], high[:size], high[size:]
    up_first = narrowed(jnp.concatenate([far[:half], above[half:]], axis=0))
    down_first = narrowed(jnp.concatenate([far[half:], below[:half]], axis=0))
    from_below, from_above = shift(up_first, 1, 1), shift(down_first, 1, -1)
    up_second = narrowed(added(above[:half], from_below[:half]))
    down_second = narrowed(added(below[half:], from_above[:half]))
    up_second, down_second = lax.optimization_barrier((up_second, down_second))
    up_second, down_second = shift(up_second, 1, 1), shift(down_second, 1, -1)
    total = low[:size] + jnp.concatenate(
        [added(up_second, from_above[half:]), added(down_second, from_below[half:])], axis=0
    )

    total = narrowed(total)
    rows = tokens.shape[0]
    arrived = [shift(total[distance * rows : (distance + 1) * rows], 0, distance) for distance in (1, 2, 3)]
    routed_out = narrowed(added(total[:rows], *arrived))
    return (routed_out, jnp.concatenate([first_attention, second_attention], axis=0))


def solution(mesh):
    cube = Mesh(mesh.devices.reshape(4, 2, 4, 4), ("z", "core", "x", "y"))
    node, local = ("z", "core"), ("x", "y")
    every = node + local
    in_specs = (
        P(every, None),
        P(every, None),
        P(every, None),
        P(local, None, node),
        P(local, None, node),
        P(local, node, None),
        P(node, local),
        P(node, local),
        P(local, None, None),
        P(local, None, None),
        P(node, None, None),
        P(node, None, None),
        P(node, None),
        P(node, None),
        P(node),
    )
    out_specs = (P(every, None), P(node, local))
    return jax.shard_map(body, mesh=cube, in_specs=in_specs, out_specs=out_specs, check_vma=False)
```
